128 devices in a mesh: enc: 32 (over y_lo, z, x), bb: 4 (over y_hi, core).
Axes of the slice: x: 4, y: 4 (y_hi: 2, y_lo: 2; y = y_hi * 2 + y_lo), z: 4, core: 2. Of those that a mesh axis runs over, the one named last changes fastest.
Arguments:
- image_tiles: bfloat16 [256, 16, 32, 384], P(('enc', 'bb')), may hold values from -6 to 6
- depth_kernel: float32 [7, 7, 384], replicated, may hold values from -0.875 to 0.875
- norm_gain: float32 [384], replicated, may hold values from 0.5 to 1.5
- weight_in: bfloat16 [384, 1536], replicated, may hold values from -0.3125 to 0.3125
- bias_in: float32 [1536], replicated, may hold values from -3 to 3
- weight_out: bfloat16 [1536, 384], replicated, may hold values from -0.15625 to 0.15625
- layer_scale: float32 [384], replicated, may hold values from 0.3 to 3
- weight_proj: bfloat16 [384, 4096], replicated, may hold values from -0.3125 to 0.3125
- image_counts: int32 [128], P(('enc', 'bb')), may hold values from 1 to 2, as said below
- destination: int32 [128, 32], P(('enc', 'bb')), may hold values from 0 to 31, as said below
- row_offset: int32 [128, 32], P(('enc', 'bb')), may hold values from 0 to 1, as said below
- connector: bfloat16 [4096, 3584], P(None, 'bb'), may hold values from -0.09375 to 0.09375
- cotangent: bfloat16 [16384, 3584], P('enc', 'bb'), may hold values from -6 to 6
Outputs:
- grad_kernel: float32 [7, 7, 384], replicated
- grad_gain: float32 [384], replicated
- grad_weight_in: bfloat16 [384, 1536], replicated
- grad_bias_in: float32 [1536], replicated
- grad_weight_out: bfloat16 [1536, 384], replicated
- grad_layer_scale: float32 [384], replicated
- grad_weight_proj: bfloat16 [384, 4096], replicated
- token_grads: bfloat16 [8192, 4096], P(('enc', 'bb'))
The draws below stay inside these ranges and needn't reach their ends.
Inputs may be any that keep to these rules, and one draw needn't show every extreme that they name: `image_counts`: every source has at least one live image. `destination`: no group is named by more than 2 blocks of one source, and in every source some group is named by exactly 2 blocks of its first image. `row_offset`: the number of earlier blocks of the same source naming the same group, so a source's (destination, row_offset) pairs are distinct.
All inputs are finite; a program needn't handle non-finite values.
Results may differ from the reference program's by a relative error of at most 0.023.
Values may be sent and summed in bfloat16 or wider, within the bound.
No kernel may reach another device: no remote copies, remote signals or barrier semaphores. Data moves between devices by JAX's collectives and lax.ppermute only.
A program may use at most 128 MiB of HBM per device.

```python
import math
import jax
import jax.numpy as jnp
from jax import lax

C = 384
HID = 1536
D = 4096
FCONN = 3584
TH = 16
TW = 32
IMG_DEV = 2
BT = 2
TOK_DEV = 64
NBLK = 32
BLK_TILE = 16
CAP = 2
ROWS_BB = 512
N_ENC = 32
N_BB = 4
DEVICES = 128


def route_table(key):
    device_keys = jax.random.split(key, DEVICES)

    def one_device(device_key):
        key_first, key_pool, key_mix = jax.random.split(device_key, 3)
        leading = jax.random.randint(key_first, (), 0, N_ENC)
        others = jnp.arange((N_ENC - 1) * CAP, dtype=jnp.int32) // CAP
        others = others + (others >= leading).astype(jnp.int32)
        others = jax.random.permutation(key_pool, others)[:NBLK - CAP]
        head_tile = jnp.concatenate([jnp.full((CAP,), leading, jnp.int32), others[:BLK_TILE - CAP]])
        head_tile = jax.random.permutation(key_mix, head_tile)
        return jnp.concatenate([head_tile, others[BLK_TILE - CAP:]]).astype(jnp.int32)
    targets = jax.vmap(one_device)(device_keys)
    matches = targets[:, :, None] == targets[:, None, :]
    earlier = jnp.arange(NBLK)[None, :] < jnp.arange(NBLK)[:, None]
    ranks = jnp.sum(jnp.logical_and(matches, earlier[None]), axis=2).astype(jnp.int32)
    return (targets, ranks)


def draw_destination(key, part):
    return route_table(key)[0]


def draw_row_offset(key, part):
    return route_table(key)[1]


def draw_image_counts(key, part):
    key = jax.random.fold_in(key, 11)
    key_mode, key_low, key_pick, key_other = jax.random.split(key, 4)
    lower = jax.random.randint(key_low, (DEVICES,), 1, IMG_DEV + 1)
    reduced = jax.random.randint(key_mode, (DEVICES,), 0, 4) == 0
    counts = jnp.where(reduced, lower, IMG_DEV)
    chosen = jax.random.randint(key_pick, (), 0, DEVICES)
    second = (chosen + 1 + jax.random.randint(key_other, (), 0, DEVICES - 1)) % DEVICES
    spots = jnp.arange(DEVICES)
    counts = jnp.where(spots == chosen, IMG_DEV, counts)
    counts = jnp.where(spots == second, 1, counts)
    return counts.astype(jnp.int32)


def steps_of(rng, extent, pieces, least, largest):
    loudness = 1.0
    for position, blocks in pieces:
        steps = jax.random.uniform(jax.random.fold_in(jax.random.fold_in(rng, 6), position), (blocks,), jnp.float32, least / len(pieces), largest / len(pieces))
        loudness = loudness * jnp.repeat(jnp.exp(steps), extent[position] // blocks).reshape((-1,) + (1,) * (len(extent) - 1 - position))
    return loudness


def gaussian(key, dims, scale, limit, shards=(), held_as=jnp.bfloat16):
    gain = steps_of(key, dims, shards, -0.22, 0.18) if shards else 1.0
    array = jax.random.normal(key, dims, jnp.float32) * scale * gain
    return jnp.minimum(jnp.maximum(array, -limit), limit).astype(held_as)


def setup_inputs(seed: int = 0) -> dict:
    arg_keys = jax.random.split(jax.random.key(seed), 14)
    return {
        "image_tiles": gaussian(arg_keys[0], (DEVICES * IMG_DEV, TH, TW, C), 1.0, 6.0, ((0, 128),)),
        "depth_kernel": gaussian(arg_keys[1], (7, 7, C), 49 ** -0.5, 0.875, (), jnp.float32),
        "norm_gain": jnp.clip(jax.random.uniform(arg_keys[2], (C,), jnp.float32, 0.5, 1.5), 0.5, 1.5),
        "weight_in": gaussian(arg_keys[3], (C, HID), C ** -0.5, 0.3125),
        "bias_in": gaussian(arg_keys[4], (HID,), 0.5, 3.0, (), jnp.float32),
        "weight_out": gaussian(arg_keys[5], (HID, C), HID ** -0.5, 0.15625),
        "layer_scale": jnp.clip(jnp.exp(jax.random.uniform(arg_keys[6], (C,), jnp.float32, math.log(0.3), math.log(3.0))), 0.3, 3.0),
        "weight_proj": gaussian(arg_keys[7], (C, D), C ** -0.5, 0.3125),
        "image_counts": draw_image_counts(jax.random.fold_in(arg_keys[13], 71), 0),
        "destination": draw_destination(jax.random.fold_in(arg_keys[13], 71), 0),
        "row_offset": draw_row_offset(jax.random.fold_in(arg_keys[13], 71), 0),
        "connector": gaussian(arg_keys[11], (D, FCONN), D ** -0.5, 0.09375, ((1, 4),)),
        "cotangent": gaussian(arg_keys[12], (N_ENC * ROWS_BB, FCONN), 1.0, 6.0, ((0, 32), (1, 4))),
    }


EPS = 1e-06

def contract_first(first_operand, second_operand):
    return lax.dot_general(first_operand, second_operand, (((0,), (0,)), ((), ())), preferred_element_type=jnp.float32)

def contract_last(first_operand, second_operand):
    return lax.dot_general(first_operand, second_operand, (((1,), (1,)), ((), ())), preferred_element_type=jnp.float32)

def front(image_tiles, depth_kernel, norm_gain):
    tile_height = image_tiles.shape[1]
    tile_width = image_tiles.shape[2]
    source = image_tiles.astype(jnp.float32)
    padded = jnp.pad(source, ((0, 0), (3, 3), (3, 3), (0, 0)))
    conv_sum = jnp.zeros_like(source)
    for row_shift in range(7):
        for col_shift in range(7):
            conv_sum = conv_sum + padded[:, row_shift:row_shift + tile_height, col_shift:col_shift + tile_width, :] * depth_kernel[row_shift, col_shift]
    centered = conv_sum - lax.optimization_barrier(jnp.mean(conv_sum, axis=-1, keepdims=True))
    variance = lax.optimization_barrier(jnp.mean(centered * centered, axis=-1, keepdims=True))
    return centered * lax.rsqrt(variance + EPS) * norm_gain

def encode(image_tiles, params):
    depth_kernel, norm_gain, weight_in, bias_in, weight_out, layer_scale, weight_proj = params
    tile_count, tile_height, tile_width, channels = image_tiles.shape
    normed = front(image_tiles, depth_kernel, norm_gain).astype(jnp.bfloat16).reshape(-1, channels)
    hidden_pre = jnp.dot(normed, weight_in, preferred_element_type=jnp.float32) + bias_in
    hidden = jax.nn.gelu(hidden_pre).astype(jnp.bfloat16)
    branch = jnp.dot(hidden, weight_out, preferred_element_type=jnp.float32)
    block_out = image_tiles.astype(jnp.float32).reshape(-1, channels) + layer_scale * branch
    pooled = block_out.reshape(tile_count, tile_height // 4, 4, tile_width // 4, 4, channels).mean(axis=(2, 4))
    pooled = pooled.reshape(-1, channels).astype(jnp.bfloat16)
    visual = jnp.dot(pooled, weight_proj, preferred_element_type=jnp.float32).astype(jnp.bfloat16)
    return (visual, (normed, hidden_pre, hidden, branch, pooled))

def encode_grads(image_tiles, params, residuals, token_grads, settle_proj, settle_mlp, settle_front):
    depth_kernel, norm_gain, weight_in, bias_in, weight_out, layer_scale, weight_proj = params
    normed, hidden_pre, hidden, branch, pooled = residuals
    tile_count, tile_height, tile_width, channels = image_tiles.shape
    grad_proj = settle_proj(contract_first(pooled, token_grads))
    grad_pooled = contract_last(token_grads, weight_proj) / 16.0
    spread_cells = jnp.broadcast_to(grad_pooled.reshape(tile_count, tile_height // 4, 1, tile_width // 4, 1, channels), (tile_count, tile_height // 4, 4, tile_width // 4, 4, channels)).reshape(-1, channels)
    grad_scale = lax.optimization_barrier(jnp.sum(spread_cells * branch, axis=0))
    grad_branch = (spread_cells * layer_scale).astype(jnp.bfloat16)
    grad_out = contract_first(hidden, grad_branch)
    grad_hidden = contract_last(grad_branch, weight_out)
    gelu_back = jax.vjp(jax.nn.gelu, hidden_pre)[1]
    grad_pre = gelu_back(grad_hidden)[0].astype(jnp.bfloat16)
    grad_in = contract_first(normed, grad_pre)
    grad_bias = lax.optimization_barrier(jnp.sum(grad_pre.astype(jnp.float32), axis=0))
    grad_scale, grad_out, grad_in, grad_bias = settle_mlp((grad_scale, grad_out, grad_in, grad_bias))
    grad_normed = contract_last(grad_pre, weight_in).reshape(image_tiles.shape)

    def front_of(kernel_value, gain_value):
        return front(image_tiles, kernel_value, gain_value)
    front_back = jax.vjp(front_of, depth_kernel, norm_gain)[1]
    grad_kernel, grad_gain = settle_front(front_back(grad_normed))
    return (grad_kernel, grad_gain, grad_in, grad_bias, grad_out, grad_scale, grad_proj)

def unchanged(value_in):
    return value_in

def reference(image_tiles, depth_kernel, norm_gain, weight_in, bias_in, weight_out, layer_scale, weight_proj, image_counts, destination, row_offset, connector, cotangent):
    params = (depth_kernel, norm_gain, weight_in, bias_in, weight_out, layer_scale, weight_proj)
    stacks = image_tiles.reshape(DEVICES, IMG_DEV, TH, TW, C)

    def tokens_of(device_tiles):
        return encode(device_tiles, params)[0]
    visual = lax.map(tokens_of, stacks)
    blocks = visual.reshape(DEVICES, NBLK, BT, D)
    in_use = (jnp.arange(NBLK, dtype=jnp.int32) // BLK_TILE)[None, :] < image_counts[:, None]
    blocks = jnp.where(in_use[:, :, None, None], blocks, jnp.zeros((), jnp.bfloat16))
    sources = jnp.broadcast_to(jnp.arange(DEVICES, dtype=jnp.int32)[:, None], (DEVICES, NBLK))
    buffer = jnp.zeros((N_ENC, DEVICES, CAP, BT, D), jnp.bfloat16).at[destination, sources, row_offset].set(blocks)

    def group_grads(inputs):
        group_in, group_cot = inputs
        group_rows = group_in.reshape(N_ENC, N_BB, CAP * BT, D).transpose(1, 0, 2, 3).reshape(ROWS_BB, D)
        pre_act = jnp.dot(group_rows, connector, preferred_element_type=jnp.float32)
        gelu_back = jax.vjp(jax.nn.gelu, pre_act)[1]
        grad_pre = gelu_back(group_cot.astype(jnp.float32))[0].astype(jnp.bfloat16)
        row_grads = contract_last(grad_pre, connector).astype(jnp.bfloat16)
        return row_grads.reshape(N_BB, N_ENC, CAP, BT, D).transpose(1, 0, 2, 3, 4).reshape(DEVICES, CAP, BT, D)
    returned = lax.map(group_grads, (buffer, cotangent.reshape(N_ENC, ROWS_BB, FCONN)))
    picked = returned[destination, sources, row_offset]
    token_grads = jnp.where(in_use[:, :, None, None], picked, jnp.zeros((), jnp.bfloat16)).reshape(DEVICES, TOK_DEV, D)

    def accumulate(running, inputs):
        device_tiles, device_grads = inputs
        residuals = encode(device_tiles, params)[1]
        grads = encode_grads(device_tiles, params, residuals, device_grads, unchanged, unchanged, unchanged)
        return (jax.tree.map(jnp.add, running, grads), None)
    initial = tuple((jnp.zeros(value.shape, jnp.float32) for value in params))
    summed = lax.scan(accumulate, initial, (stacks, token_grads))[0]
    factor = 1.0 / DEVICES
    return (summed[0] * factor, summed[1] * factor, (summed[2] * factor).astype(jnp.bfloat16), summed[3] * factor, (summed[4] * factor).astype(jnp.bfloat16), summed[5] * factor, (summed[6] * factor).astype(jnp.bfloat16), token_grads.reshape(DEVICES * TOK_DEV, D))
```

```python
import functools

import jax
import jax.numpy as jnp
import numpy as np
from jax import lax
from jax.experimental import pallas as pl
from jax.experimental.pallas import tpu as pltpu
from jax.sharding import Mesh, PartitionSpec as P

EPS = 1e-06
GELU_A = float(np.sqrt(2.0 / np.pi))
GELU_B = 0.044715
BF = jnp.bfloat16
F32 = jnp.float32
ALL = ("yl", "z", "x", "yh", "co")
ENC = ("yl", "z", "x")
BB = ("yh", "co")
SAME_CORE = ("yl", "z", "x", "yh")
PLANE = ("z", "x")
COLS = ("yl", "yh", "co")
VMEM_LIMIT = 56 * 1024 * 1024


def nn(a, b):
    return lax.dot_general(a, b, (((1,), (0,)), ((), ())), preferred_element_type=F32)


def nt(a, b):
    return lax.dot_general(a, b, (((1,), (1,)), ((), ())), preferred_element_type=F32)


def gelu_parts(u):
    u2 = u * u
    t = jnp.tanh(u * (GELU_A + (GELU_A * GELU_B) * u2))
    half = 0.5 * (1.0 + t)
    value = u * half
    slope = half + 0.5 * u * (1.0 - t * t) * (GELU_A + (3.0 * GELU_A * GELU_B) * u2)
    return value, slope


def vmem():
    return pl.BlockSpec(memory_space=pltpu.VMEM)


def smem():
    return pl.BlockSpec(memory_space=pltpu.SMEM)


def call(kernel, out_shape, scratch, in_specs, flops=0, nbytes=0):
    multi = isinstance(out_shape, (list, tuple))
    return pl.pallas_call(
        kernel,
        out_shape=out_shape,
        in_specs=in_specs,
        out_specs=[vmem()] * len(out_shape) if multi else vmem(),
        scratch_shapes=scratch,
        compiler_params=pltpu.CompilerParams(vmem_limit_bytes=VMEM_LIMIT),
        cost_estimate=pl.CostEstimate(flops=flops, bytes_accessed=nbytes, transcendentals=0),
    )


def arrange_kernel(cot_ref, out_ref):
    r = lax.broadcasted_iota(jnp.int32, (512, 512), 0)
    s = lax.broadcasted_iota(jnp.int32, (512, 512), 1)
    want = ((r // 4) % 4) * 128 + (r // 16) * 4 + r % 4
    pick = jnp.where(s == want, 1.0, 0.0).astype(BF)
    out_ref[...] = nn(pick, cot_ref[...]).astype(BF)


def forward_kernel(
    x_ref, k_ref, gain_ref, win_ref, bias_ref, wout_ref, scale_ref, code_ref,
    pay_ref, normt_ref, xhat_ref, rstd_ref, slope_ref, hsum_ref, gsum_ref, bsum_ref, xs_ref,
    xf_ref, kb_ref, conv_ref, norm_ref, hs_ref,
):
    for lt in range(3):
        lanes = slice(lt * 128, lt * 128 + 128)
        kb_ref[lt] = k_ref[:, lanes]
        for t in range(2):
            xf_ref[lt, t] = x_ref[t, :, :, lanes].astype(F32)

    row = lax.broadcasted_iota(jnp.int32, (8, 128), 0)
    first = row == 0
    last = row == 7

    def split(n, carry):
        lt = n // 2
        t = n % 2
        for jj in range(4):
            for i in range(16):
                v = xf_ref[lt, t, i, pl.ds(jj, 8, stride=4), :]
                xs_ref[1, lt, t, jj, i] = v
                xs_ref[0, lt, t, jj, i] = jnp.where(first, 0.0, pltpu.roll(v, 1, 0))
                xs_ref[2, lt, t, jj, i] = jnp.where(last, 0.0, pltpu.roll(v, 7, 0))
        return carry

    lax.fori_loop(0, 6, split, 0)

    def conv(n, carry):
        lt = n // 8
        t = (n // 4) % 2
        jj = n % 4
        acc = [None] * 16
        for b in range(7):
            q = jj + (b + 1)
            s = q // 4
            jin = q % 4
            w = [
                jnp.broadcast_to(kb_ref[lt, pl.ds(a * 7 + b, 1), :], (8, 128)) for a in range(7)
            ]
            for r in range(16):
                v = xs_ref[s, lt, t, jin, r]
                for a in range(7):
                    i = r - a + 3
                    if 0 <= i < 16:
                        term = v * w[a]
                        acc[i] = term if acc[i] is None else acc[i] + term
        for i in range(16):
            conv_ref[lt, t, i // 4, jj, i % 4] = acc[i]
        return carry

    lax.fori_loop(0, 24, conv, 0)

    def block(n, carry):
        t = n // 4
        q = n % 4
        rows = pl.ds(pl.multiple_of(n * 128, 128), 128)
        c = [conv_ref[lt, t, q].reshape(128, 128) for lt in range(3)]
        mean = jnp.sum(c[0] + c[1] + c[2], axis=1, keepdims=True) * (1.0 / 384.0)
        c = [v - mean for v in c]
        var = jnp.sum(c[0] * c[0] + c[1] * c[1] + c[2] * c[2], axis=1, keepdims=True) * (
            1.0 / 384.0
        )
        rstd = lax.rsqrt(var + EPS)
        rstd_ref[rows, :] = jnp.broadcast_to(rstd, (128, 128))
        for lt in range(3):
            lanes = slice(lt * 128, lt * 128 + 128)
            xhat = c[lt] * rstd
            xhat_ref[lt, rows, :] = xhat
            normed = xhat * gain_ref[:, lanes]
            norm_ref[:, lanes] = normed.astype(BF)
            normt_ref[n, lanes, :] = normed.T.astype(BF)
        toks = pl.ds(pl.multiple_of(n * 8, 8), 8)
        for h in range(6):
            hid = slice(h * 256, h * 256 + 256)
            u = nn(norm_ref[...], win_ref[:, hid]) + bias_ref[:, hid]
            value, slope = gelu_parts(u)
            value = value.astype(BF).astype(F32)
            hs_ref[toks, hid] = jnp.sum(value.reshape(16, 8, 256), axis=0)
            gsum_ref[toks, hid] = jnp.sum(slope.reshape(16, 8, 256), axis=0)
            slope_ref[rows, hid] = slope.astype(BF)
        return carry

    lax.fori_loop(0, 8, block, 0)

    hs = hs_ref[...]
    hi = hs.astype(BF)
    hsum_ref[...] = hi
    lo = (hs - hi.astype(F32)).astype(BF)
    bsum = nn(hi, wout_ref[...]) + nn(lo, wout_ref[...])
    bsum_ref[...] = bsum
    for lt in range(3):
        lanes = slice(lt * 128, lt * 128 + 128)
        for t in range(2):
            for q in range(4):
                total = xs_ref[1, lt, t, 0, 4 * q]
                for jj in range(4):
                    for im in range(4):
                        if jj + im > 0:
                            total = total + xs_ref[1, lt, t, jj, 4 * q + im]
                tok = slice(t * 32 + q * 8, t * 32 + q * 8 + 8)
                hs_ref[tok, lanes] = total
    pooled = (hs_ref[:, 0:384] + scale_ref[...] * bsum) * (1.0 / 16.0)
    pay_ref[:, 0:384] = pooled.astype(BF)
    pay_ref[:, 384:512] = code_ref[...]


def forward(x, k, gain, win, bias, wout, scale, code):
    shape = jax.ShapeDtypeStruct
    return call(
        forward_kernel,
        [
            shape((64, 512), BF),
            shape((8, 384, 128), BF),
            shape((3, 1024, 128), F32),
            shape((1024, 128), F32),
            shape((1024, 1536), BF),
            shape((64, 1536), BF),
            shape((64, 1536), F32),
            shape((64, 384), F32),
            shape((3, 3, 2, 4, 16, 8, 128), F32),
        ],
        [
            pltpu.VMEM((3, 2, 16, 32, 128), F32),
            pltpu.VMEM((3, 49, 128), F32),
            pltpu.VMEM((3, 2, 4, 4, 4, 8, 128), F32),
            pltpu.VMEM((128, 384), BF),
            pltpu.VMEM((64, 1536), F32),
        ],
        [vmem()] * 8,
        flops=20_000_000_000,
        nbytes=10_000_000,
    )(x, k, gain, win, bias, wout, scale, code)


def connector_kernel(
    bb_ref, p0_ref, p1_ref, p2_ref, p3_ref, cot_ref, wc_ref, gp_ref, t_ref, s_ref,
    pick_ref, pool_ref,
):
    row = lax.broadcasted_iota(jnp.int32, (64, 128), 0)
    lane = lax.broadcasted_iota(jnp.int32, (64, 128), 1)
    for d, p_ref in enumerate((p0_ref, p1_ref, p2_ref, p3_ref)):
        tok = slice(d * 64, d * 64 + 64)
        pool_ref[tok, :] = p_ref[:, 0:384]
        code = p_ref[:, 384:512].astype(F32).astype(jnp.int32)
        src = bb_ref[0] ^ d
        want = (code >> 1) * 16 + src * 4 + (code & 1) * 2 + (row & 1)
        want = jnp.where(code < 0, -1, want)
        for q in range(4):
            pick_ref[tok, q * 128 : q * 128 + 128] = jnp.where(
                lane + q * 128 == want, 1.0, 0.0
            ).astype(BF)
    for h in range(7):
        cols = slice(h * 128, h * 128 + 128)
        cot = nn(pick_ref[...], cot_ref[:, cols])
        pre = nn(pool_ref[...], wc_ref[:, cols])
        gp_ref[:, cols] = (cot * gelu_parts(pre)[1]).astype(BF)
    t_ref[...] = nt(gp_ref[...], wc_ref[...])
    pool_t = pool_ref[...].astype(F32).T.astype(BF)
    s_ref[...] = nn(pool_t, gp_ref[...]).astype(BF)


def connector_part(bb, pays, cot, wc):
    shape = jax.ShapeDtypeStruct
    return call(
        connector_kernel,
        [shape((256, 896), BF), shape((256, 384), F32), shape((384, 896), BF)],
        [pltpu.VMEM((256, 512), BF), pltpu.VMEM((256, 384), BF)],
        [smem()] + [vmem()] * 6,
        flops=1_000_000_000,
        nbytes=2_000_000,
    )(bb, *pays, cot, wc)


def mlp_back_kernel(
    co_ref, dtok_ref, normt_ref, slope_ref, hsum_ref, gsum_ref, bsum_ref, wout_ref, scale_ref,
    keep_ref, send_ref, dpre_ref, small_ref, dh_ref,
):
    dtok = dtok_ref[...] * (1.0 / 16.0)
    small_ref[0:1, :] = jnp.sum(dtok * bsum_ref[...], axis=0, keepdims=True)
    dbr = (dtok * scale_ref[...]).astype(BF)
    dh_ref[...] = nt(dbr, wout_ref[...])
    db = jnp.sum(dh_ref[...] * gsum_ref[...], axis=0, keepdims=True)
    for q in range(4):
        small_ref[1 + q : 2 + q, :] = db[:, q * 384 : q * 384 + 384]
    small_ref[5:8, :] = jnp.zeros((3, 384), F32)

    def block(n, carry):
        rows = pl.ds(pl.multiple_of(n * 128, 128), 128)
        toks = pl.ds(pl.multiple_of(n * 8, 8), 8)
        for h in range(4):
            hid = slice(h * 384, h * 384 + 384)
            g = slope_ref[rows, hid].astype(F32).reshape(16, 8, 384)
            d = g * dh_ref[toks, hid][None]
            dpre_ref[h, rows, :] = d.reshape(128, 384).astype(BF)
        return carry

    lax.fori_loop(0, 8, block, 0)
    hsum_t = hsum_ref[...].astype(F32).T.astype(BF)
    normt = jnp.concatenate([normt_ref[n] for n in range(8)], axis=1)
    mine = co_ref[0] == 0
    for h in range(2):
        def put(out_ref):
            for q in range(2):
                rows = slice(q * 384, q * 384 + 384)
                out_ref[rows, :] = nn(normt, dpre_ref[2 * h + q]).astype(out_ref.dtype)
            out_ref[768:1536, :] = nn(hsum_t[h * 768 : h * 768 + 768], dbr).astype(out_ref.dtype)

        here = mine if h == 0 else jnp.logical_not(mine)

        @pl.when(here)
        def _():
            put(keep_ref)

        @pl.when(jnp.logical_not(here))
        def _():
            put(send_ref)


def mlp_back(co, dtok, normt, slope, hsum, gsum, bsum, wout, scale):
    shape = jax.ShapeDtypeStruct
    return call(
        mlp_back_kernel,
        [
            shape((1536, 384), BF),
            shape((1536, 384), BF),
            shape((4, 1024, 384), BF),
            shape((8, 384), F32),
        ],
        [pltpu.VMEM((64, 1536), F32)],
        [smem()] + [vmem()] * 8,
        flops=4_000_000_000,
        nbytes=10_000_000,
    )(co, dtok, normt, slope, hsum, gsum, bsum, wout, scale)


def front_back_kernel(
    dpre_ref, win_ref, xhat_ref, rstd_ref, gain_ref, xs_ref, out_ref, dc_ref, dk_ref
):
    def block(n, carry):
        t = n // 4
        q = n % 4
        rows = pl.ds(pl.multiple_of(n * 128, 128), 128)
        dn = nt(dpre_ref[0, rows, :], win_ref[:, 0:384])
        for h in range(1, 4):
            dn = dn + nt(dpre_ref[h, rows, :], win_ref[:, h * 384 : h * 384 + 384])
        rstd = rstd_ref[rows, :]
        dx = []
        xh = []
        gains = []
        for lt in range(3):
            lanes = slice(lt * 128, lt * 128 + 128)
            xhat = xhat_ref[lt, rows, :]
            part = dn[:, lanes]
            gains.append(jnp.sum((part * xhat).reshape(16, 8, 128), axis=0))
            dx.append(part * gain_ref[:, lanes])
            xh.append(xhat)
        m1 = jnp.sum(dx[0] + dx[1] + dx[2], axis=1, keepdims=True) * (1.0 / 384.0)
        m2 = jnp.sum(dx[0] * xh[0] + dx[1] * xh[1] + dx[2] * xh[2], axis=1, keepdims=True) * (
            1.0 / 384.0
        )
        for lt in range(3):
            dc = rstd * (dx[lt] - m1 - xh[lt] * m2)
            dc_ref[lt, t, q] = dc.reshape(4, 4, 8, 128)
        return tuple(c + g for c, g in zip(carry, gains))

    zero = jnp.zeros((8, 128), F32)
    gains = lax.fori_loop(0, 8, block, (zero, zero, zero))
    for lt in range(3):
        lanes = slice(lt * 128, lt * 128 + 128)
        out_ref[49:50, lanes] = jnp.sum(gains[lt], axis=0, keepdims=True)

    dk_ref[...] = jnp.zeros_like(dk_ref)

    def conv(n, carry):
        lt = n // 8
        t = (n // 4) % 2
        jj = n % 4
        d = [dc_ref[lt, t, i // 4, jj, i % 4] for i in range(16)]
        for b in range(7):
            q = jj + (b + 1)
            s = q // 4
            jin = q % 4
            acc = [None] * 7
            for r in range(16):
                v = xs_ref[s, lt, t, jin, r]
                for a in range(7):
                    i = r - a + 3
                    if 0 <= i < 16:
                        term = v * d[i]
                        acc[a] = term if acc[a] is None else acc[a] + term
            for a in range(7):
                dk_ref[lt, a * 7 + b] += acc[a]
        return carry

    lax.fori_loop(0, 24, conv, 0)
    for lt in range(3):
        lanes = slice(lt * 128, lt * 128 + 128)
        out_ref[0:49, lanes] = jnp.sum(dk_ref[lt], axis=1)
    out_ref[50:56, :] = jnp.zeros((6, 384), F32)


def front_back(dpre, win, xhat, rstd, gain, xs):
    return call(
        front_back_kernel,
        jax.ShapeDtypeStruct((56, 384), F32),
        [pltpu.VMEM((3, 2, 4, 4, 4, 8, 128), F32), pltpu.VMEM((3, 49, 8, 128), F32)],
        [vmem()] * 6,
        flops=10_000_000_000,
        nbytes=10_000_000,
    )(dpre, win, xhat, rstd, gain, xs)


def swap(v, axes, size, d):
    return lax.ppermute(v, axes, [(i, i ^ d) for i in range(size)])


def ring_sum(v, axes, size):
    others = [lax.ppermute(v, axes, [(i, (i + d) % size) for i in range(size)]) for d in range(1, size)]
    for other in others:
        v = v + other
    return v


def exchange(v, axes):
    return lax.all_to_all(v, axes, split_axis=0, concat_axis=0, tiled=True)


def spread(v, axes, size):
    return exchange(jnp.broadcast_to(v[None], (size,) + v.shape), axes)


def on_device(
    image_tiles,
    depth_kernel,
    norm_gain,
    weight_in,
    bias_in,
    weight_out,
    layer_scale,
    weight_proj,
    image_counts,
    destination,
    row_offset,
    connector,
    cotangent,
):
    bb = lax.axis_index(BB).astype(jnp.int32)
    co = lax.axis_index("co").astype(jnp.int32)
    factor = 1.0 / 128.0

    sent = call(
        arrange_kernel, jax.ShapeDtypeStruct((512, 896), BF), [], [vmem()], 500_000_000, 2_000_000
    )(cotangent)
    cot = exchange(sent.reshape(32, 16, 896), ENC).reshape(512, 896)

    live = jnp.arange(32, dtype=jnp.int32) // 16 < image_counts[0]
    code = jnp.where(live, destination[0] * 2 + row_offset[0], -1).astype(BF)
    code = jnp.broadcast_to(jnp.repeat(code, 2)[:, None], (64, 128))
    gain = norm_gain.reshape(1, 384)
    scale = layer_scale.reshape(1, 384)
    pay, normt, xhat, rstd, slope, hsum, gsum, bsum, xs = forward(
        image_tiles,
        depth_kernel.reshape(49, 384),
        gain,
        weight_in,
        bias_in.reshape(1, 1536),
        weight_out,
        scale,
        code,
    )
    wc = nn(weight_proj, connector).astype(BF)
    pays = [pay] + [swap(pay, BB, 4, d) for d in (1, 2, 3)]
    grad_pre, tok, outer = connector_part(bb.reshape(1), pays, cot, wc)

    tok = tok.reshape(4, 64, 384)
    near = swap(jnp.concatenate([tok[1], tok[3]], axis=0), "co", 2, 1)
    far = swap(tok[2] + near[64:], "yh", 2, 1)
    dtok = tok[0] + near[:64] + far

    keep, send, dpre, small_a = mlp_back(
        co.reshape(1), dtok, normt, slope, hsum, gsum, bsum, weight_out, scale
    )
    pair = keep.astype(F32) + swap(send, "co", 2, 1).astype(F32)
    parts = exchange(pair.astype(BF).reshape(64, 24, 384), SAME_CORE)
    mine = (jnp.sum(parts.astype(F32), axis=0) * factor).astype(BF)

    small_b = front_back(dpre, weight_in, xhat, rstd, gain, xs)
    small = jnp.concatenate([small_a, small_b], axis=0)
    small = small + swap(small, "co", 2, 1)
    small = ring_sum(small, "x", 4)
    small = ring_sum(small, "z", 4)
    small = ring_sum(small, ("yl", "yh"), 4) * factor

    rows = nt(grad_pre, connector).astype(BF).reshape(4, 64, 4096)
    near = swap(jnp.concatenate([rows[1], rows[3]], axis=0), "co", 2, 1).astype(F32)
    far = swap((rows[2].astype(F32) + near[64:]).astype(BF), "yh", 2, 1)
    token_grads = (rows[0].astype(F32) + near[:64] + far.astype(F32)).astype(BF)

    outer = jnp.sum(exchange(outer.reshape(16, 24, 896), PLANE).astype(F32), axis=0).astype(BF)
    proj = lax.dot_general(
        connector.reshape(8, 512, 896), outer, (((2,), (1,)), ((), ())), preferred_element_type=F32
    )
    proj = proj.transpose(0, 2, 1).astype(BF)
    proj = jnp.sum(exchange(proj, COLS).astype(F32), axis=0) * factor
    proj = spread(proj.astype(BF), SAME_CORE, 64)
    other = swap(proj, "co", 2, 1)
    both = jnp.stack([jnp.where(co == 0, proj, other), jnp.where(co == 0, other, proj)])
    both = both.reshape(2, 2, 16, 2, 24, 512).transpose(2, 4, 1, 3, 0, 5)
    grad_proj = both.reshape(384, 4096)

    full = spread(mine, SAME_CORE, 64).reshape(1536, 384)
    other = swap(full, "co", 2, 1)
    low = jnp.where(co == 0, full, other)
    high = jnp.where(co == 0, other, full)
    grad_in = jnp.concatenate([low[:384], low[384:768], high[:384], high[384:768]], axis=1)
    grad_out = jnp.concatenate([low[768:], high[768:]], axis=0)

    return (
        small[8:57].reshape(7, 7, 384),
        small[57],
        grad_in,
        small[1:5].reshape(1536),
        grad_out,
        small[0],
        grad_proj,
        token_grads,
    )


def solution(mesh):
    fine = Mesh(mesh.devices.reshape(2, 4, 4, 2, 2), ALL)
    in_specs = (
        P(ALL, None, None, None),
        P(),
        P(),
        P(),
        P(),
        P(),
        P(),
        P(),
        P(ALL),
        P(ALL, None),
        P(ALL, None),
        P(None, BB),
        P(ENC, BB),
    )
    out_specs = (P(), P(), P(), P(), P(), P(), P(), P(ALL, None))
    return jax.shard_map(
        on_device, mesh=fine, in_specs=in_specs, out_specs=out_specs, check_vma=False
    )
```

```python
import jax
import jax.numpy as jnp
import numpy as np
from jax import lax
from jax.experimental import pallas as pl
from jax.experimental.pallas import tpu as pltpu
from jax.sharding import Mesh, PartitionSpec as P

EPS = 1e-06
GELU_A = float(np.sqrt(2.0 / np.pi))
GELU_B = 0.044715
BF = jnp.bfloat16
F32 = jnp.float32
ALL = ("yl", "z", "x", "yh", "co")
ENC = ("yl", "z", "x")
BB = ("yh", "co")
SAME_CORE = ("yl", "z", "x", "yh")
PLANE = ("z", "x")
MIB = 1024 * 1024


def cost(us):
    return pl.CostEstimate(flops=int(us * 1.1e9) + 1, bytes_accessed=1, transcendentals=0)


def nn(a, b):
    return lax.dot_general(a, b, (((1,), (0,)), ((), ())), preferred_element_type=F32)


def nt(a, b):
    return lax.dot_general(a, b, (((1,), (1,)), ((), ())), preferred_element_type=F32)


def gelu_parts(u):
    u2 = u * u
    t = jnp.tanh(u * (GELU_A + (GELU_A * GELU_B) * u2))
    half = 0.5 * (1.0 + t)
    value = u * half
    slope = half + 0.5 * u * (1.0 - t * t) * (GELU_A + (3.0 * GELU_A * GELU_B) * u2)
    return value, slope


def vmem():
    return pl.BlockSpec(memory_space=pltpu.VMEM)


def smem():
    return pl.BlockSpec(memory_space=pltpu.SMEM)


def call(kernel, out_shape, scratch, in_specs, limit, us):
    multi = isinstance(out_shape, (list, tuple))
    return pl.pallas_call(
        kernel,
        out_shape=out_shape,
        in_specs=in_specs,
        out_specs=[vmem()] * len(out_shape) if multi else vmem(),
        scratch_shapes=scratch,
        compiler_params=pltpu.CompilerParams(vmem_limit_bytes=limit * MIB),
        cost_estimate=cost(us),
    )


def arrange_kernel(cot_ref, out_ref):
    r = lax.broadcasted_iota(jnp.int32, (512, 512), 0)
    s = lax.broadcasted_iota(jnp.int32, (512, 512), 1)
    want = ((r // 4) % 4) * 128 + (r // 16) * 4 + r % 4
    pick = jnp.where(s == want, 1.0, 0.0).astype(BF)
    out_ref[...] = nn(pick, cot_ref[...]).astype(BF)


def shifted(v):
    row = lax.broadcasted_iota(jnp.int32, (8, 128), 0)
    down = jnp.where(row == 0, 0.0, pltpu.roll(v, 1, 0))
    up = jnp.where(row == 7, 0.0, pltpu.roll(v, 7, 0))
    return down, v, up


def forward_kernel(
    x_ref, k_ref, gain_ref, win_ref, bias_ref, wout_ref, scale_ref, code_ref,
    pay_ref, normt_ref, xhat_ref, rstd_ref, slope_ref, hsum_ref, gsum_ref, bsum_ref, xp_ref,
    xf_ref, xs_ref, kb_ref, conv_ref, norm_ref, hs_ref,
):
    for lt in range(3):
        lanes = slice(lt * 128, lt * 128 + 128)
        for a in range(7):
            kb_ref[lt, a] = k_ref[a, :, lanes]
        for t in range(2):
            xf_ref[lt, t] = x_ref[t, :, :, lanes].astype(F32)

    def split(n, carry):
        lt = n // 2
        t = n % 2
        for jj in range(4):
            plain = []
            for i in range(16):
                v = xf_ref[lt, t, i, pl.ds(jj, 8, stride=4), :]
                plain.append(v)
                for s, w in enumerate(shifted(v)):
                    xs_ref[s, lt, t, jj, i] = w
            xp_ref[lt, t, jj] = jnp.concatenate(plain, axis=0).astype(BF)
        return carry

    lax.fori_loop(0, 6, split, 0)

    def conv(n, carry):
        lt = n // 8
        t = (n // 4) % 2
        jj = n % 4
        acc = [None] * 16
        for b in range(7):
            q = jj + (b + 1)
            s = q // 4
            jin = q % 4
            w = [
                jnp.broadcast_to(kb_ref[lt, a, pl.ds(b, 1), :], (8, 128)) for a in range(7)
            ]
            for r in range(16):
                v = xs_ref[s, lt, t, jin, r]
                for a in range(7):
                    i = r - a + 3
                    if 0 <= i < 16:
                        term = v * w[a]
                        acc[i] = term if acc[i] is None else acc[i] + term
        for i in range(16):
            conv_ref[lt, t, i // 4, jj, i % 4] = acc[i]
        return carry

    lax.fori_loop(0, 24, conv, 0)

    def block(n, carry):
        t = n // 4
        q = n % 4
        rows = pl.ds(pl.multiple_of(n * 128, 128), 128)
        c = [conv_ref[lt, t, q].reshape(128, 128) for lt in range(3)]
        mean = jnp.sum(c[0] + c[1] + c[2], axis=1, keepdims=True) * (1.0 / 384.0)
        c = [v - mean for v in c]
        var = jnp.sum(c[0] * c[0] + c[1] * c[1] + c[2] * c[2], axis=1, keepdims=True) * (
            1.0 / 384.0
        )
        rstd = lax.rsqrt(var + EPS)
        rstd_ref[rows, :] = jnp.broadcast_to(rstd, (128, 128))
        for lt in range(3):
            lanes = slice(lt * 128, lt * 128 + 128)
            xhat = c[lt] * rstd
            xhat_ref[lt, rows, :] = xhat
            normed = xhat * gain_ref[lanes].reshape(1, 128)
            norm_ref[:, lanes] = normed.astype(BF)
            normt_ref[n, lanes, :] = normed.T.astype(BF)
        toks = pl.ds(pl.multiple_of(n * 8, 8), 8)
        for h in range(6):
            hid = slice(h * 256, h * 256 + 256)
            u = nn(norm_ref[...], win_ref[:, hid]) + bias_ref[hid].reshape(1, 256)
            value, slope = gelu_parts(u)
            value = value.astype(BF).astype(F32)
            hs_ref[toks, hid] = jnp.sum(value.reshape(16, 8, 256), axis=0)
            gsum_ref[toks, hid] = jnp.sum(slope.reshape(16, 8, 256), axis=0)
            slope_ref[rows, hid] = slope.astype(BF)
        return carry

    lax.fori_loop(0, 8, block, 0)

    hs = hs_ref[...]
    hi = hs.astype(BF)
    hsum_ref[...] = hi
    lo = (hs - hi.astype(F32)).astype(BF)
    bsum = nn(hi, wout_ref[...]) + nn(lo, wout_ref[...])
    bsum_ref[...] = bsum
    for lt in range(3):
        lanes = slice(lt * 128, lt * 128 + 128)
        for t in range(2):
            for q in range(4):
                total = xs_ref[1, lt, t, 0, 4 * q]
                for jj in range(4):
                    for im in range(4):
                        if jj + im > 0:
                            total = total + xs_ref[1, lt, t, jj, 4 * q + im]
                tok = slice(t * 32 + q * 8, t * 32 + q * 8 + 8)
                hs_ref[tok, lanes] = total
        pooled = hs_ref[:, lanes] + scale_ref[lanes].reshape(1, 128) * bsum[:, lanes]
        pay_ref[:, lanes] = (pooled * (1.0 / 16.0)).astype(BF)
    pay_ref[:, 384:512] = code_ref[...]


def forward(x, k, gain, win, bias, wout, scale, code):
    shape = jax.ShapeDtypeStruct
    return call(
        forward_kernel,
        [
            shape((64, 512), BF),
            shape((8, 384, 128), BF),
            shape((3, 1024, 128), F32),
            shape((1024, 128), F32),
            shape((1024, 1536), BF),
            shape((64, 1536), BF),
            shape((64, 1536), F32),
            shape((64, 384), F32),
            shape((3, 2, 4, 128, 128), BF),
        ],
        [
            pltpu.VMEM((3, 2, 16, 32, 128), F32),
            pltpu.VMEM((3, 3, 2, 4, 16, 8, 128), F32),
            pltpu.VMEM((3, 7, 7, 128), F32),
            pltpu.VMEM((3, 2, 4, 4, 4, 8, 128), F32),
            pltpu.VMEM((128, 384), BF),
            pltpu.VMEM((64, 1536), F32),
        ],
        [vmem()] * 8,
        26,
        14,
    )(x, k, gain, win, bias, wout, scale, code)


def fold_kernel(proj_ref, conn_ref, out_ref, acc_ref):
    n = pl.program_id(0)

    @pl.when(n == 0)
    def _():
        acc_ref[...] = jnp.zeros_like(acc_ref)

    acc_ref[...] += nn(proj_ref[...], conn_ref[...])

    @pl.when(n == pl.num_programs(0) - 1)
    def _():
        out_ref[...] = acc_ref[...].astype(BF)


def fold(weight_proj, connector):
    return pl.pallas_call(
        fold_kernel,
        out_shape=jax.ShapeDtypeStruct((384, 896), BF),
        grid=(8,),
        in_specs=[
            pl.BlockSpec((384, 512), lambda n: (0, n)),
            pl.BlockSpec((512, 896), lambda n: (n, 0)),
        ],
        out_specs=pl.BlockSpec((384, 896), lambda n: (0, 0)),
        scratch_shapes=[pltpu.VMEM((384, 896), F32)],
        compiler_params=pltpu.CompilerParams(vmem_limit_bytes=12 * MIB),
        cost_estimate=cost(0),
    )(weight_proj, connector)


def rows_kernel(gp_ref, conn_ref, keep_ref, send_ref):
    out = nt(gp_ref[...], conn_ref[...]).astype(BF)
    keep_ref[...] = out[:128]
    send_ref[...] = out[128:]


def token_rows(grad_pre, connector):
    shape = jax.ShapeDtypeStruct((128, 4096), BF)
    return pl.pallas_call(
        rows_kernel,
        out_shape=[shape, shape],
        grid=(8,),
        in_specs=[
            pl.BlockSpec((256, 896), lambda n: (0, 0)),
            pl.BlockSpec((512, 896), lambda n: (n, 0)),
        ],
        out_specs=[pl.BlockSpec((128, 512), lambda n: (0, n))] * 2,
        compiler_params=pltpu.CompilerParams(vmem_limit_bytes=12 * MIB),
        cost_estimate=cost(5),
    )(grad_pre, connector)


def proj_kernel(at_ref, parts_ref, conn_ref, send_ref, keep_ref, sum_ref):
    n = pl.program_id(0)

    @pl.when(n == 0)
    def _():
        total = parts_ref[0].astype(F32)
        for m in range(1, 16):
            total = total + parts_ref[m].astype(F32)
        sum_ref[...] = total.astype(BF)

    out = nt(sum_ref[...], conn_ref[...])

    @pl.when(n < 4)
    def _():
        send_ref[0] = out.astype(BF)

    @pl.when(n >= 4)
    def _():
        keep_ref[0] = out


def proj_rows(at, parts, connector):
    def chunk(n, at):
        return (
            (at[0] ^ (1 - n // 4)) * 4 + (at[1] ^ (1 - (n % 4) // 2)) * 2 + (at[2] ^ (1 - n % 2)),
            0,
        )

    return pl.pallas_call(
        proj_kernel,
        out_shape=[
            jax.ShapeDtypeStruct((4, 24, 512), BF),
            jax.ShapeDtypeStruct((4, 24, 512), F32),
        ],
        grid_spec=pltpu.PrefetchScalarGridSpec(
            num_scalar_prefetch=1,
            grid=(8,),
            in_specs=[
                pl.BlockSpec((16, 24, 896), lambda n, at: (0, 0, 0)),
                pl.BlockSpec((512, 896), chunk),
            ],
            out_specs=[
                pl.BlockSpec((1, 24, 512), lambda n, at: (jnp.minimum(n, 3), 0, 0)),
                pl.BlockSpec((1, 24, 512), lambda n, at: (jnp.maximum(n - 4, 0), 0, 0)),
            ],
            scratch_shapes=[pltpu.VMEM((24, 896), BF)],
        ),
        compiler_params=pltpu.CompilerParams(vmem_limit_bytes=12 * MIB),
        cost_estimate=cost(4),
    )(at, parts, connector)


def connector_kernel(
    bb_ref, p0_ref, p1_ref, p2_ref, p3_ref, cot_ref, wc_ref,
    gp_ref, keep_ref, send_ref, s_ref, pick_ref, pool_ref,
):
    row = lax.broadcasted_iota(jnp.int32, (64, 128), 0)
    lane = lax.broadcasted_iota(jnp.int32, (64, 128), 1)
    for n, (d, p_ref) in enumerate(((0, p0_ref), (2, p1_ref), (1, p2_ref), (3, p3_ref))):
        tok = slice(n * 64, n * 64 + 64)
        pool_ref[tok, :] = p_ref[:, 0:384]
        code = p_ref[:, 384:512].astype(F32).astype(jnp.int32)
        src = bb_ref[0] ^ d
        want = (code >> 1) * 16 + src * 4 + (code & 1) * 2 + (row & 1)
        want = jnp.where(code < 0, -1, want)
        for q in range(4):
            pick_ref[tok, q * 128 : q * 128 + 128] = jnp.where(
                lane + q * 128 == want, 1.0, 0.0
            ).astype(BF)
    for h in range(7):
        cols = slice(h * 128, h * 128 + 128)
        cot = nn(pick_ref[...], cot_ref[:, cols])
        pre = nn(pool_ref[...], wc_ref[:, cols])
        gp_ref[:, cols] = (cot * gelu_parts(pre)[1]).astype(BF)
    tok = nt(gp_ref[...], wc_ref[...])
    keep_ref[...] = tok[:128]
    send_ref[...] = tok[128:]
    pool_t = pool_ref[...].astype(F32).T.astype(BF)
    s_ref[...] = nn(pool_t, gp_ref[...]).astype(BF)


def connector_part(bb, pays, cot, wc):
    shape = jax.ShapeDtypeStruct
    return call(
        connector_kernel,
        [
            shape((256, 896), BF),
            shape((128, 384), F32),
            shape((128, 384), F32),
            shape((384, 896), BF),
        ],
        [pltpu.VMEM((256, 512), BF), pltpu.VMEM((256, 384), BF)],
        [smem()] + [vmem()] * 6,
        12,
        3,
    )(bb, *pays, cot, wc)


def mlp_back_kernel(
    co_ref, near_ref, part_ref, far_ref, normt_ref, slope_ref, hsum_ref, gsum_ref, bsum_ref, wout_ref, scale_ref,
    keep_ref, send_ref, dpre_ref, small_ref, dh_ref,
):
    dtok = (part_ref[0:64, :] + near_ref[0:64, :] + far_ref[...]) * (1.0 / 16.0)
    small_ref[0:1, :] = jnp.sum(dtok * bsum_ref[...], axis=0, keepdims=True)
    dbr = (dtok * scale_ref[...].reshape(1, 384)).astype(BF)
    dh_ref[...] = nt(dbr, wout_ref[...])
    db = jnp.sum(dh_ref[...] * gsum_ref[...], axis=0, keepdims=True)
    for q in range(4):
        small_ref[1 + q : 2 + q, :] = db[:, q * 384 : q * 384 + 384]
    small_ref[5:8, :] = jnp.zeros((3, 384), F32)

    def block(n, carry):
        rows = pl.ds(pl.multiple_of(n * 128, 128), 128)
        toks = pl.ds(pl.multiple_of(n * 8, 8), 8)
        for h in range(4):
            hid = slice(h * 384, h * 384 + 384)
            g = slope_ref[rows, hid].astype(F32).reshape(16, 8, 384)
            d = g * dh_ref[toks, hid][None]
            dpre_ref[h, rows, :] = d.reshape(128, 384).astype(BF)
        return carry

    lax.fori_loop(0, 8, block, 0)
    hsum_t = hsum_ref[...].astype(F32).T.astype(BF)
    normt = jnp.concatenate([normt_ref[n] for n in range(8)], axis=1)
    mine = co_ref[0] == 0
    for h in range(2):
        def put(out_ref):
            for q in range(2):
                rows = slice(q * 384, q * 384 + 384)
                out_ref[rows, :] = nn(normt, dpre_ref[2 * h + q]).astype(out_ref.dtype)
            out_ref[768:1536, :] = nn(hsum_t[h * 768 : h * 768 + 768], dbr).astype(out_ref.dtype)

        here = mine if h == 0 else jnp.logical_not(mine)

        @pl.when(here)
        def _():
            put(keep_ref)

        @pl.when(jnp.logical_not(here))
        def _():
            put(send_ref)


def mlp_back(co, near, part, far, normt, slope, hsum, gsum, bsum, wout, scale):
    shape = jax.ShapeDtypeStruct
    return call(
        mlp_back_kernel,
        [
            shape((1536, 384), BF),
            shape((1536, 384), BF),
            shape((4, 1024, 384), BF),
            shape((8, 384), F32),
        ],
        [pltpu.VMEM((64, 1536), F32)],
        [smem()] + [vmem()] * 10,
        20,
        5,
    )(co, near, part, far, normt, slope, hsum, gsum, bsum, wout, scale)


def front_back_kernel(
    dpre_ref, win_ref, xhat_ref, rstd_ref, gain_ref, xp_ref, out_ref, dc_ref, dk_ref
):
    def block(n, carry):
        t = n // 4
        q = n % 4
        rows = pl.ds(pl.multiple_of(n * 128, 128), 128)
        dn = nt(dpre_ref[0, rows, :], win_ref[:, 0:384])
        for h in range(1, 4):
            dn = dn + nt(dpre_ref[h, rows, :], win_ref[:, h * 384 : h * 384 + 384])
        rstd = rstd_ref[rows, :]
        dx = []
        xh = []
        gains = []
        for lt in range(3):
            lanes = slice(lt * 128, lt * 128 + 128)
            xhat = xhat_ref[lt, rows, :]
            part = dn[:, lanes]
            gains.append(jnp.sum((part * xhat).reshape(16, 8, 128), axis=0))
            dx.append(part * gain_ref[lanes].reshape(1, 128))
            xh.append(xhat)
        m1 = jnp.sum(dx[0] + dx[1] + dx[2], axis=1, keepdims=True) * (1.0 / 384.0)
        m2 = jnp.sum(dx[0] * xh[0] + dx[1] * xh[1] + dx[2] * xh[2], axis=1, keepdims=True) * (
            1.0 / 384.0
        )
        for lt in range(3):
            dc = rstd * (dx[lt] - m1 - xh[lt] * m2)
            for jj in range(4):
                for im in range(4):
                    at = (jj * 4 + im) * 8
                    for s, w in enumerate(shifted(dc[at : at + 8])):
                        dc_ref[s, lt, t, jj, q * 4 + im] = w
        return tuple(c + g for c, g in zip(carry, gains))

    zero = jnp.zeros((8, 128), F32)
    gains = lax.fori_loop(0, 8, block, (zero, zero, zero))
    for lt in range(3):
        lanes = slice(lt * 128, lt * 128 + 128)
        out_ref[49:50, lanes] = jnp.sum(gains[lt], axis=0, keepdims=True)

    dk_ref[...] = jnp.zeros_like(dk_ref)

    def conv(n, carry):
        lt = n // 8
        t = (n // 4) % 2
        jj = n % 4
        x = xp_ref[lt, t, jj].astype(F32)
        x = [x[i * 8 : i * 8 + 8] for i in range(16)]
        for b in range(7):
            q = jj + (7 - b)
            s = q // 4
            jin = q % 4
            acc = [None] * 7
            for i in range(16):
                v = dc_ref[s, lt, t, jin, i]
                for a in range(7):
                    r = i + a - 3
                    if 0 <= r < 16:
                        term = v * x[r]
                        acc[a] = term if acc[a] is None else acc[a] + term
            for a in range(7):
                dk_ref[lt, a * 7 + b] += acc[a]
        return carry

    lax.fori_loop(0, 24, conv, 0)
    for lt in range(3):
        lanes = slice(lt * 128, lt * 128 + 128)
        out_ref[0:49, lanes] = jnp.sum(dk_ref[lt], axis=1)
    out_ref[50:56, :] = jnp.zeros((6, 384), F32)


def front_back(dpre, win, xhat, rstd, gain, xp):
    return call(
        front_back_kernel,
        jax.ShapeDtypeStruct((56, 384), F32),
        [pltpu.VMEM((3, 3, 2, 4, 16, 8, 128), F32), pltpu.VMEM((3, 49, 8, 128), F32)],
        [vmem()] * 6,
        20,
        10,
    )(dpre, win, xhat, rstd, gain, xp)


def three(v):
    return [v[:, q * 128 : q * 128 + 128] for q in range(3)]


def two_parts(v):
    high = v.astype(BF).astype(F32)
    return three(high) + three(v - high)


def pack_kernel(keep_ref, recv_ref, a_ref, b_ref, out_ref):
    pad = jnp.zeros((2, 128), F32)

    def one(n, small):
        rows = slice(n * 24, n * 24 + 24)
        pair = keep_ref[rows, :].astype(F32) + recv_ref[rows, :].astype(F32)
        out_ref[n] = jnp.concatenate(three(pair) + two_parts(small) + [pad], axis=0).astype(BF)

    for n in range(64):
        one(n, a_ref[n : n + 1, :] if n < 8 else b_ref[n - 8 : n - 7, :])


def pack(keep, recv, small_a, small_b):
    return call(
        pack_kernel, jax.ShapeDtypeStruct((64, 80, 128), BF), [], [vmem()] * 4, 12, 2
    )(keep, recv, small_a, small_b)


def settle_kernel(parts_ref, proj_ref, more_ref, out_ref):
    total = parts_ref[0].astype(F32)
    for n in range(1, 64):
        total = total + parts_ref[n].astype(F32)
    total = total * (1.0 / 128.0)
    small = total[72:75] + total[75:78]
    high = small.astype(BF).astype(F32)
    proj = (proj_ref[...] + more_ref[...].astype(F32)) * (1.0 / 128.0)
    shard = jnp.concatenate(
        [total[:72], high, small - high, total[78:80]]
        + [proj[:, q * 128 : q * 128 + 128] for q in range(4)],
        axis=0,
    ).astype(BF)
    for n in range(64):
        out_ref[n] = shard


def settle(parts, proj, more):
    return call(
        settle_kernel, jax.ShapeDtypeStruct((64, 176, 128), BF), [], [vmem()] * 3, 12, 2
    )(parts, proj, more)


def place_kernel(co_ref, mine_ref, other_ref, in_ref, out_ref, proj_ref, small_ref):
    def put(src_ref, half):
        def pair(low, high, at):
            return jnp.concatenate(
                [
                    src_ref[low, at : at + 24, :].astype(F32),
                    src_ref[high, at : at + 24, :].astype(F32),
                ],
                axis=0,
            ).astype(BF)

        for p in range(3):
            for m in range(8):
                rows = slice(m * 48, m * 48 + 48)
                for q in range(2):
                    n = q * 16 + 2 * m
                    col = half * 768 + q * 384 + p * 128
                    in_ref[rows, col : col + 128] = pair(n, n + 1, p * 24)
            for m in range(16):
                at = half * 768 + m * 48
                out_ref[at : at + 48, p * 128 : p * 128 + 128] = pair(
                    32 + 2 * m, 33 + 2 * m, p * 24
                )
        for yl in range(2):
            for yh in range(2):
                for p in range(4):
                    col = (half * 4 + yh * 2 + yl) * 512 + p * 128
                    for m in range(8):
                        n = yl * 32 + 4 * m + yh
                        proj_ref[m * 48 : m * 48 + 48, col : col + 128] = pair(
                            n, n + 2, 80 + p * 24
                        )

    low = co_ref[0] == 0

    @pl.when(low)
    def _():
        put(mine_ref, 0)
        put(other_ref, 1)

    @pl.when(jnp.logical_not(low))
    def _():
        put(other_ref, 0)
        put(mine_ref, 1)

    for n in range(64):
        small = mine_ref[n, 64:80, :].astype(F32) + other_ref[n, 64:80, :].astype(F32)
        small = small[8:11] + small[11:14]
        for p in range(3):
            small_ref[n : n + 1, p * 128 : p * 128 + 128] = small[p : p + 1]


def place(co, mine, other):
    shape = jax.ShapeDtypeStruct
    return call(
        place_kernel,
        [
            shape((384, 1536), BF),
            shape((1536, 384), BF),
            shape((384, 4096), BF),
            shape((64, 384), F32),
        ],
        [],
        [smem()] + [vmem()] * 2,
        26,
        5,
    )(co, mine, other)


def swap(v, axes, size, d):
    return lax.ppermute(v, axes, [(i, i ^ d) for i in range(size)])


def exchange(v, axes):
    return lax.all_to_all(v, axes, split_axis=0, concat_axis=0, tiled=True)


def on_device(
    image_tiles,
    depth_kernel,
    norm_gain,
    weight_in,
    bias_in,
    weight_out,
    layer_scale,
    weight_proj,
    image_counts,
    destination,
    row_offset,
    connector,
    cotangent,
):
    bb = lax.axis_index(BB).astype(jnp.int32)
    co = lax.axis_index("co").astype(jnp.int32)

    sent = call(arrange_kernel, jax.ShapeDtypeStruct((512, 896), BF), [], [vmem()], 8, 2)(cotangent)
    cot = exchange(sent.reshape(32, 16, 896), ENC).reshape(512, 896)
    image_tiles, sent = lax.optimization_barrier((image_tiles, sent))

    live = jnp.arange(32, dtype=jnp.int32) // 16 < image_counts[0]
    code = jnp.where(live, destination[0] * 2 + row_offset[0], -1).astype(BF)
    code = jnp.broadcast_to(jnp.repeat(code, 2)[:, None], (64, 128))
    pay, normt, xhat, rstd, slope, hsum, gsum, bsum, xp = forward(
        image_tiles,
        depth_kernel,
        norm_gain,
        weight_in,
        bias_in,
        weight_out,
        layer_scale,
        code,
    )
    pays = [pay] + [swap(pay, BB, 4, d) for d in (2, 1, 3)]
    wc = fold(lax.optimization_barrier((weight_proj, pay))[0], connector)
    grad_pre, part, give, outer = connector_part(bb.reshape(1), pays, cot, wc)

    near = swap(give, "co", 2, 1)
    tail, outer = lax.optimization_barrier((part[64:] + near[64:], outer))
    far = swap(tail, "yh", 2, 1)
    outer = exchange(outer.reshape(16, 24, 896), PLANE)

    keep, send, dpre, small_a = mlp_back(
        co.reshape(1), near, part, far, normt, slope, hsum, gsum, bsum, weight_out, layer_scale
    )
    keep, send, outer = lax.optimization_barrier((keep, send, outer))
    recv = swap(send, "co", 2, 1)
    at = jnp.stack([lax.axis_index(axis) for axis in ("co", "yh", "yl")]).astype(jnp.int32)
    give, own = proj_rows(at, outer, connector)
    own = own + swap(give, "co", 2, 1).astype(F32)
    own = own[2:] + swap(own[:2].astype(BF), "yh", 2, 1).astype(F32)
    own, more = own[1], swap(own[0].astype(BF), "yl", 2, 1)

    small_b = front_back(dpre, weight_in, xhat, rstd, norm_gain, xp)
    packed = pack(keep, recv, small_a, small_b)
    packed, own, more, grad_pre = lax.optimization_barrier((packed, own, more, grad_pre))
    shards = settle(exchange(packed, SAME_CORE), own, more)
    whole = exchange(shards, SAME_CORE)

    part, give = token_rows(grad_pre, connector)
    near = swap(give, "co", 2, 1).astype(F32)
    far = swap((part[64:].astype(F32) + near[64:]).astype(BF), "yh", 2, 1)
    token_grads = (part[:64].astype(F32) + near[:64] + far.astype(F32)).astype(BF)

    whole, token_grads = lax.optimization_barrier((whole, token_grads))
    grad_in, grad_out, grad_proj, small = place(co.reshape(1), whole, swap(whole, "co", 2, 1))

    return (
        small[8:57].reshape(7, 7, 384),
        small[57],
        grad_in,
        small[1:5].reshape(1536),
        grad_out,
        small[0],
        grad_proj,
        token_grads,
    )


def solution(mesh):
    fine = Mesh(mesh.devices.reshape(2, 4, 4, 2, 2), ALL)
    in_specs = (
        P(ALL, None, None, None),
        P(),
        P(),
        P(),
        P(),
        P(),
        P(),
        P(),
        P(ALL),
        P(ALL, None),
        P(ALL, None),
        P(None, BB),
        P(ENC, BB),
    )
    out_specs = (P(), P(), P(), P(), P(), P(), P(), P(ALL, None))
    return jax.shard_map(
        on_device, mesh=fine, in_specs=in_specs, out_specs=out_specs, check_vma=False
    )
```

```python
import jax
import jax.numpy as jnp
import numpy as np
from jax import lax
from jax.experimental import pallas as pl
from jax.experimental.pallas import tpu as pltpu
from jax.sharding import Mesh, PartitionSpec as P

EPS = 1e-06
GELU_A = float(np.sqrt(2.0 / np.pi))
GELU_B = 0.044715
BF = jnp.bfloat16
F32 = jnp.float32
ALL = ("yl", "z", "x", "yh", "co")
ENC = ("yl", "z", "x")
BB = ("yh", "co")
SAME_CORE = ("yl", "z", "x", "yh")
PLANE = ("z", "x")
COLS = ("yl", "yh", "co")
MIB = 1024 * 1024


def cost(us):
    return pl.CostEstimate(flops=int(us * 1.1e9) + 1, bytes_accessed=1, transcendentals=0)


def nn(a, b):
    return lax.dot_general(a, b, (((1,), (0,)), ((), ())), preferred_element_type=F32)


def nt(a, b):
    return lax.dot_general(a, b, (((1,), (1,)), ((), ())), preferred_element_type=F32)


def gelu_parts(u):
    u2 = u * u
    t = jnp.tanh(u * (GELU_A + (GELU_A * GELU_B) * u2))
    half = 0.5 * (1.0 + t)
    value = u * half
    slope = half + 0.5 * u * (1.0 - t * t) * (GELU_A + (3.0 * GELU_A * GELU_B) * u2)
    return value, slope


def vmem():
    return pl.BlockSpec(memory_space=pltpu.VMEM)


def smem():
    return pl.BlockSpec(memory_space=pltpu.SMEM)


def call(kernel, out_shape, scratch, in_specs, limit, us):
    multi = isinstance(out_shape, (list, tuple))
    return pl.pallas_call(
        kernel,
        out_shape=out_shape,
        in_specs=in_specs,
        out_specs=[vmem()] * len(out_shape) if multi else vmem(),
        scratch_shapes=scratch,
        compiler_params=pltpu.CompilerParams(vmem_limit_bytes=limit * MIB),
        cost_estimate=cost(us),
    )


def arrange_kernel(cot_ref, out_ref):
    r = lax.broadcasted_iota(jnp.int32, (512, 512), 0)
    s = lax.broadcasted_iota(jnp.int32, (512, 512), 1)
    want = ((r // 4) % 4) * 128 + (r // 16) * 4 + r % 4
    pick = jnp.where(s == want, 1.0, 0.0).astype(BF)
    out_ref[...] = nn(pick, cot_ref[...]).astype(BF)


def shifted(v):
    row = lax.broadcasted_iota(jnp.int32, (8, 128), 0)
    down = jnp.where(row == 0, 0.0, pltpu.roll(v, 1, 0))
    up = jnp.where(row == 7, 0.0, pltpu.roll(v, 7, 0))
    return down, v, up


def forward_kernel(
    x_ref, k_ref, gain_ref, win_ref, bias_ref, wout_ref, scale_ref, code_ref,
    pay_ref, normt_ref, xhat_ref, rstd_ref, slope_ref, hsum_ref, gsum_ref, bsum_ref, xp_ref,
    xf_ref, xs_ref, kb_ref, conv_ref, norm_ref, hs_ref,
):
    for lt in range(3):
        lanes = slice(lt * 128, lt * 128 + 128)
        for a in range(7):
            kb_ref[lt, a] = k_ref[a, :, lanes]
        for t in range(2):
            xf_ref[lt, t] = x_ref[t, :, :, lanes].astype(F32)

    def split(n, carry):
        lt = n // 2
        t = n % 2
        for jj in range(4):
            plain = []
            for i in range(16):
                v = xf_ref[lt, t, i, pl.ds(jj, 8, stride=4), :]
                plain.append(v)
                for s, w in enumerate(shifted(v)):
                    xs_ref[s, lt, t, jj, i] = w
            xp_ref[lt, t, jj] = jnp.concatenate(plain, axis=0).astype(BF)
        return carry

    lax.fori_loop(0, 6, split, 0)

    def conv(n, carry):
        lt = n // 8
        t = (n // 4) % 2
        jj = n % 4
        acc = [None] * 16
        for b in range(7):
            q = jj + (b + 1)
            s = q // 4
            jin = q % 4
            w = [
                jnp.broadcast_to(kb_ref[lt, a, pl.ds(b, 1), :], (8, 128)) for a in range(7)
            ]
            for r in range(16):
                v = xs_ref[s, lt, t, jin, r]
                for a in range(7):
                    i = r - a + 3
                    if 0 <= i < 16:
                        term = v * w[a]
                        acc[i] = term if acc[i] is None else acc[i] + term
        for i in range(16):
            conv_ref[lt, t, i // 4, jj, i % 4] = acc[i]
        return carry

    lax.fori_loop(0, 24, conv, 0)

    def block(n, carry):
        t = n // 4
        q = n % 4
        rows = pl.ds(pl.multiple_of(n * 128, 128), 128)
        c = [conv_ref[lt, t, q].reshape(128, 128) for lt in range(3)]
        mean = jnp.sum(c[0] + c[1] + c[2], axis=1, keepdims=True) * (1.0 / 384.0)
        c = [v - mean for v in c]
        var = jnp.sum(c[0] * c[0] + c[1] * c[1] + c[2] * c[2], axis=1, keepdims=True) * (
            1.0 / 384.0
        )
        rstd = lax.rsqrt(var + EPS)
        rstd_ref[rows, :] = jnp.broadcast_to(rstd, (128, 128))
        for lt in range(3):
            lanes = slice(lt * 128, lt * 128 + 128)
            xhat = c[lt] * rstd
            xhat_ref[lt, rows, :] = xhat
            normed = xhat * gain_ref[lanes].reshape(1, 128)
            norm_ref[:, lanes] = normed.astype(BF)
            normt_ref[n, lanes, :] = normed.T.astype(BF)
        toks = pl.ds(pl.multiple_of(n * 8, 8), 8)
        for h in range(6):
            hid = slice(h * 256, h * 256 + 256)
            u = nn(norm_ref[...], win_ref[:, hid]) + bias_ref[hid].reshape(1, 256)
            value, slope = gelu_parts(u)
            value = value.astype(BF).astype(F32)
            hs_ref[toks, hid] = jnp.sum(value.reshape(16, 8, 256), axis=0)
            gsum_ref[toks, hid] = jnp.sum(slope.reshape(16, 8, 256), axis=0)
            slope_ref[rows, hid] = slope.astype(BF)
        return carry

    lax.fori_loop(0, 8, block, 0)

    hs = hs_ref[...]
    hi = hs.astype(BF)
    hsum_ref[...] = hi
    lo = (hs - hi.astype(F32)).astype(BF)
    bsum = nn(hi, wout_ref[...]) + nn(lo, wout_ref[...])
    bsum_ref[...] = bsum
    for lt in range(3):
        lanes = slice(lt * 128, lt * 128 + 128)
        for t in range(2):
            for q in range(4):
                total = xs_ref[1, lt, t, 0, 4 * q]
                for jj in range(4):
                    for im in range(4):
                        if jj + im > 0:
                            total = total + xs_ref[1, lt, t, jj, 4 * q + im]
                tok = slice(t * 32 + q * 8, t * 32 + q * 8 + 8)
                hs_ref[tok, lanes] = total
        pooled = hs_ref[:, lanes] + scale_ref[lanes].reshape(1, 128) * bsum[:, lanes]
        pay_ref[:, lanes] = (pooled * (1.0 / 16.0)).astype(BF)
    pay_ref[:, 384:512] = code_ref[...]


def forward(x, k, gain, win, bias, wout, scale, code):
    shape = jax.ShapeDtypeStruct
    return call(
        forward_kernel,
        [
            shape((64, 512), BF),
            shape((8, 384, 128), BF),
            shape((3, 1024, 128), F32),
            shape((1024, 128), F32),
            shape((1024, 1536), BF),
            shape((64, 1536), BF),
            shape((64, 1536), F32),
            shape((64, 384), F32),
            shape((3, 2, 4, 128, 128), BF),
        ],
        [
            pltpu.VMEM((3, 2, 16, 32, 128), F32),
            pltpu.VMEM((3, 3, 2, 4, 16, 8, 128), F32),
            pltpu.VMEM((3, 7, 7, 128), F32),
            pltpu.VMEM((3, 2, 4, 4, 4, 8, 128), F32),
            pltpu.VMEM((128, 384), BF),
            pltpu.VMEM((64, 1536), F32),
        ],
        [vmem()] * 8,
        22,
        14,
    )(x, k, gain, win, bias, wout, scale, code)


def fold_kernel(proj_ref, conn_ref, out_ref, acc_ref):
    n = pl.program_id(0)

    @pl.when(n == 0)
    def _():
        acc_ref[...] = jnp.zeros_like(acc_ref)

    acc_ref[...] += nn(proj_ref[...], conn_ref[...])

    @pl.when(n == pl.num_programs(0) - 1)
    def _():
        out_ref[...] = acc_ref[...].astype(BF)


def fold(weight_proj, connector):
    return pl.pallas_call(
        fold_kernel,
        out_shape=jax.ShapeDtypeStruct((384, 896), BF),
        grid=(8,),
        in_specs=[
            pl.BlockSpec((384, 512), lambda n: (0, n)),
            pl.BlockSpec((512, 896), lambda n: (n, 0)),
        ],
        out_specs=pl.BlockSpec((384, 896), lambda n: (0, 0)),
        scratch_shapes=[pltpu.VMEM((384, 896), F32)],
        compiler_params=pltpu.CompilerParams(vmem_limit_bytes=8 * MIB),
        cost_estimate=cost(0),
    )(weight_proj, connector)


def rows_kernel(gp_ref, conn_ref, keep_ref, send_ref):
    out = nt(gp_ref[...], conn_ref[...]).astype(BF)
    keep_ref[...] = out[:128]
    send_ref[...] = out[128:]


def token_rows(grad_pre, connector):
    shape = jax.ShapeDtypeStruct((128, 4096), BF)
    return pl.pallas_call(
        rows_kernel,
        out_shape=[shape, shape],
        grid=(8,),
        in_specs=[
            pl.BlockSpec((256, 896), lambda n: (0, 0)),
            pl.BlockSpec((512, 896), lambda n: (n, 0)),
        ],
        out_specs=[pl.BlockSpec((128, 512), lambda n: (0, n))] * 2,
        compiler_params=pltpu.CompilerParams(vmem_limit_bytes=8 * MIB),
        cost_estimate=cost(0),
    )(grad_pre, connector)


def proj_kernel(at_ref, parts_ref, conn_ref, out_ref, sum_ref):
    @pl.when(pl.program_id(0) == 0)
    def _():
        total = parts_ref[0].astype(F32)
        for m in range(1, 16):
            total = total + parts_ref[m].astype(F32)
        sum_ref[...] = total.astype(BF)

    out_ref[0] = nt(sum_ref[...], conn_ref[...]).astype(BF)


def proj_rows(at, parts, connector):
    def chunk(n, at):
        return (
            (at[0] ^ (1 - n // 4)) * 4 + (at[1] ^ (1 - (n % 4) // 2)) * 2 + (at[2] ^ (1 - n % 2)),
            0,
        )

    return pl.pallas_call(
        proj_kernel,
        out_shape=jax.ShapeDtypeStruct((8, 24, 512), BF),
        grid_spec=pltpu.PrefetchScalarGridSpec(
            num_scalar_prefetch=1,
            grid=(8,),
            in_specs=[
                pl.BlockSpec((16, 24, 896), lambda n, at: (0, 0, 0)),
                pl.BlockSpec((512, 896), chunk),
            ],
            out_specs=pl.BlockSpec((1, 24, 512), lambda n, at: (n, 0, 0)),
            scratch_shapes=[pltpu.VMEM((24, 896), BF)],
        ),
        compiler_params=pltpu.CompilerParams(vmem_limit_bytes=8 * MIB),
        cost_estimate=cost(0),
    )(at, parts, connector)


def connector_kernel(
    bb_ref, p0_ref, p1_ref, p2_ref, p3_ref, cot_ref, wc_ref,
    gp_ref, keep_ref, send_ref, s_ref, pick_ref, pool_ref,
):
    row = lax.broadcasted_iota(jnp.int32, (64, 128), 0)
    lane = lax.broadcasted_iota(jnp.int32, (64, 128), 1)
    for n, (d, p_ref) in enumerate(((0, p0_ref), (2, p1_ref), (1, p2_ref), (3, p3_ref))):
        tok = slice(n * 64, n * 64 + 64)
        pool_ref[tok, :] = p_ref[:, 0:384]
        code = p_ref[:, 384:512].astype(F32).astype(jnp.int32)
        src = bb_ref[0] ^ d
        want = (code >> 1) * 16 + src * 4 + (code & 1) * 2 + (row & 1)
        want = jnp.where(code < 0, -1, want)
        for q in range(4):
            pick_ref[tok, q * 128 : q * 128 + 128] = jnp.where(
                lane + q * 128 == want, 1.0, 0.0
            ).astype(BF)
    for h in range(7):
        cols = slice(h * 128, h * 128 + 128)
        cot = nn(pick_ref[...], cot_ref[:, cols])
        pre = nn(pool_ref[...], wc_ref[:, cols])
        gp_ref[:, cols] = (cot * gelu_parts(pre)[1]).astype(BF)
    tok = nt(gp_ref[...], wc_ref[...])
    keep_ref[...] = tok[:128]
    send_ref[...] = tok[128:]
    pool_t = pool_ref[...].astype(F32).T.astype(BF)
    s_ref[...] = nn(pool_t, gp_ref[...]).astype(BF)


def connector_part(bb, pays, cot, wc):
    shape = jax.ShapeDtypeStruct
    return call(
        connector_kernel,
        [
            shape((256, 896), BF),
            shape((128, 384), F32),
            shape((128, 384), F32),
            shape((384, 896), BF),
        ],
        [pltpu.VMEM((256, 512), BF), pltpu.VMEM((256, 384), BF)],
        [smem()] + [vmem()] * 6,
        6,
        3,
    )(bb, *pays, cot, wc)


def mlp_back_kernel(
    co_ref, near_ref, part_ref, far_ref, normt_ref, slope_ref, hsum_ref, gsum_ref, bsum_ref, wout_ref, scale_ref,
    keep_ref, send_ref, dpre_ref, small_ref, dh_ref,
):
    dtok = (part_ref[0:64, :] + near_ref[0:64, :] + far_ref[...]) * (1.0 / 16.0)
    small_ref[0:1, :] = jnp.sum(dtok * bsum_ref[...], axis=0, keepdims=True)
    dbr = (dtok * scale_ref[...].reshape(1, 384)).astype(BF)
    dh_ref[...] = nt(dbr, wout_ref[...])
    db = jnp.sum(dh_ref[...] * gsum_ref[...], axis=0, keepdims=True)
    for q in range(4):
        small_ref[1 + q : 2 + q, :] = db[:, q * 384 : q * 384 + 384]
    small_ref[5:8, :] = jnp.zeros((3, 384), F32)

    def block(n, carry):
        rows = pl.ds(pl.multiple_of(n * 128, 128), 128)
        toks = pl.ds(pl.multiple_of(n * 8, 8), 8)
        for h in range(4):
            hid = slice(h * 384, h * 384 + 384)
            g = slope_ref[rows, hid].astype(F32).reshape(16, 8, 384)
            d = g * dh_ref[toks, hid][None]
            dpre_ref[h, rows, :] = d.reshape(128, 384).astype(BF)
        return carry

    lax.fori_loop(0, 8, block, 0)
    hsum_t = hsum_ref[...].astype(F32).T.astype(BF)
    normt = jnp.concatenate([normt_ref[n] for n in range(8)], axis=1)
    mine = co_ref[0] == 0
    for h in range(2):
        def put(out_ref):
            for q in range(2):
                rows = slice(q * 384, q * 384 + 384)
                out_ref[rows, :] = nn(normt, dpre_ref[2 * h + q]).astype(out_ref.dtype)
            out_ref[768:1536, :] = nn(hsum_t[h * 768 : h * 768 + 768], dbr).astype(out_ref.dtype)

        here = mine if h == 0 else jnp.logical_not(mine)

        @pl.when(here)
        def _():
            put(keep_ref)

        @pl.when(jnp.logical_not(here))
        def _():
            put(send_ref)


def mlp_back(co, near, part, far, normt, slope, hsum, gsum, bsum, wout, scale):
    shape = jax.ShapeDtypeStruct
    return call(
        mlp_back_kernel,
        [
            shape((1536, 384), BF),
            shape((1536, 384), BF),
            shape((4, 1024, 384), BF),
            shape((8, 384), F32),
        ],
        [pltpu.VMEM((64, 1536), F32)],
        [smem()] + [vmem()] * 10,
        14,
        5,
    )(co, near, part, far, normt, slope, hsum, gsum, bsum, wout, scale)


def front_back_kernel(
    dpre_ref, win_ref, xhat_ref, rstd_ref, gain_ref, xp_ref, out_ref, dc_ref, dk_ref
):
    def block(n, carry):
        t = n // 4
        q = n % 4
        rows = pl.ds(pl.multiple_of(n * 128, 128), 128)
        dn = nt(dpre_ref[0, rows, :], win_ref[:, 0:384])
        for h in range(1, 4):
            dn = dn + nt(dpre_ref[h, rows, :], win_ref[:, h * 384 : h * 384 + 384])
        rstd = rstd_ref[rows, :]
        dx = []
        xh = []
        gains = []
        for lt in range(3):
            lanes = slice(lt * 128, lt * 128 + 128)
            xhat = xhat_ref[lt, rows, :]
            part = dn[:, lanes]
            gains.append(jnp.sum((part * xhat).reshape(16, 8, 128), axis=0))
            dx.append(part * gain_ref[lanes].reshape(1, 128))
            xh.append(xhat)
        m1 = jnp.sum(dx[0] + dx[1] + dx[2], axis=1, keepdims=True) * (1.0 / 384.0)
        m2 = jnp.sum(dx[0] * xh[0] + dx[1] * xh[1] + dx[2] * xh[2], axis=1, keepdims=True) * (
            1.0 / 384.0
        )
        for lt in range(3):
            dc = rstd * (dx[lt] - m1 - xh[lt] * m2)
            for jj in range(4):
                for im in range(4):
                    at = (jj * 4 + im) * 8
                    for s, w in enumerate(shifted(dc[at : at + 8])):
                        dc_ref[s, lt, t, jj, q * 4 + im] = w
        return tuple(c + g for c, g in zip(carry, gains))

    zero = jnp.zeros((8, 128), F32)
    gains = lax.fori_loop(0, 8, block, (zero, zero, zero))
    for lt in range(3):
        lanes = slice(lt * 128, lt * 128 + 128)
        out_ref[49:50, lanes] = jnp.sum(gains[lt], axis=0, keepdims=True)

    dk_ref[...] = jnp.zeros_like(dk_ref)

    def conv(n, carry):
        lt = n // 8
        t = (n // 4) % 2
        jj = n % 4
        x = xp_ref[lt, t, jj].astype(F32)
        x = [x[i * 8 : i * 8 + 8] for i in range(16)]
        for b in range(7):
            q = jj + (7 - b)
            s = q // 4
            jin = q % 4
            acc = [None] * 7
            for i in range(16):
                v = dc_ref[s, lt, t, jin, i]
                for a in range(7):
                    r = i + a - 3
                    if 0 <= r < 16:
                        term = v * x[r]
                        acc[a] = term if acc[a] is None else acc[a] + term
            for a in range(7):
                dk_ref[lt, a * 7 + b] += acc[a]
        return carry

    lax.fori_loop(0, 24, conv, 0)
    for lt in range(3):
        lanes = slice(lt * 128, lt * 128 + 128)
        out_ref[0:49, lanes] = jnp.sum(dk_ref[lt], axis=1)
    out_ref[50:56, :] = jnp.zeros((6, 384), F32)


def front_back(dpre, win, xhat, rstd, gain, xp):
    return call(
        front_back_kernel,
        jax.ShapeDtypeStruct((56, 384), F32),
        [pltpu.VMEM((3, 3, 2, 4, 16, 8, 128), F32), pltpu.VMEM((3, 49, 8, 128), F32)],
        [vmem()] * 6,
        15,
        10,
    )(dpre, win, xhat, rstd, gain, xp)


def three(v):
    return [v[:, q * 128 : q * 128 + 128] for q in range(3)]


def two_parts(v):
    high = v.astype(BF).astype(F32)
    return three(high) + three(v - high)


def pack_kernel(keep_ref, recv_ref, a_ref, b_ref, out_ref):
    pad = jnp.zeros((2, 128), F32)

    def one(n, small):
        rows = slice(n * 24, n * 24 + 24)
        pair = keep_ref[rows, :].astype(F32) + recv_ref[rows, :].astype(F32)
        out_ref[n] = jnp.concatenate(three(pair) + two_parts(small) + [pad], axis=0).astype(BF)

    for n in range(64):
        one(n, a_ref[n : n + 1, :] if n < 8 else b_ref[n - 8 : n - 7, :])


def pack(keep, recv, small_a, small_b):
    return call(
        pack_kernel, jax.ShapeDtypeStruct((64, 80, 128), BF), [], [vmem()] * 4, 6, 2
    )(keep, recv, small_a, small_b)


def settle_kernel(parts_ref, *refs):
    proj_refs, out_ref = refs[:8], refs[8]
    total = parts_ref[0].astype(F32)
    for n in range(1, 64):
        total = total + parts_ref[n].astype(F32)
    total = total * (1.0 / 128.0)
    small = total[72:75] + total[75:78]
    high = small.astype(BF).astype(F32)
    proj = proj_refs[0][...].astype(F32)
    for ref in proj_refs[1:]:
        proj = proj + ref[...].astype(F32)
    proj = proj * (1.0 / 128.0)
    shard = jnp.concatenate(
        [total[:72], high, small - high, total[78:80]]
        + [proj[:, q * 128 : q * 128 + 128] for q in range(4)],
        axis=0,
    ).astype(BF)
    for n in range(64):
        out_ref[n] = shard


def settle(parts, proj):
    return call(
        settle_kernel, jax.ShapeDtypeStruct((64, 176, 128), BF), [], [vmem()] * 9, 6, 2
    )(parts, *proj)


def place_kernel(
    co_ref, mine_ref, other_ref,
    in_ref, out_ref, proj_ref, kernel_ref, gain_ref, bias_ref, scale_ref,
):
    def put(src_ref, half):
        def pair(low, high, at):
            return jnp.concatenate(
                [
                    src_ref[low, at : at + 24, :].astype(F32),
                    src_ref[high, at : at + 24, :].astype(F32),
                ],
                axis=0,
            ).astype(BF)

        for p in range(3):
            for m in range(8):
                rows = slice(m * 48, m * 48 + 48)
                for q in range(2):
                    n = q * 16 + 2 * m
                    col = half * 768 + q * 384 + p * 128
                    in_ref[rows, col : col + 128] = pair(n, n + 1, p * 24)
            for m in range(16):
                at = half * 768 + m * 48
                out_ref[at : at + 48, p * 128 : p * 128 + 128] = pair(
                    32 + 2 * m, 33 + 2 * m, p * 24
                )
        for yl in range(2):
            for yh in range(2):
                for p in range(4):
                    col = (half * 4 + yh * 2 + yl) * 512 + p * 128
                    for m in range(8):
                        n = yl * 32 + 4 * m + yh
                        proj_ref[m * 48 : m * 48 + 48, col : col + 128] = pair(
                            n, n + 2, 80 + p * 24
                        )

    low = co_ref[0] == 0

    @pl.when(low)
    def _():
        put(mine_ref, 0)
        put(other_ref, 1)

    @pl.when(jnp.logical_not(low))
    def _():
        put(other_ref, 0)
        put(mine_ref, 1)

    for n in range(58):
        small = mine_ref[n, 64:80, :].astype(F32) + other_ref[n, 64:80, :].astype(F32)
        small = small[8:11] + small[11:14]
        for p in range(3):
            lanes = slice(p * 128, p * 128 + 128)
            row = small[p : p + 1]
            if n == 0:
                scale_ref[lanes] = row.reshape(128)
            elif n < 5:
                bias_ref[(n - 1) * 384 + p * 128 : (n - 1) * 384 + p * 128 + 128] = row.reshape(128)
            elif n == 57:
                gain_ref[lanes] = row.reshape(128)
            elif n >= 8:
                a, b = (n - 8) // 7, (n - 8) % 7
                kernel_ref[a, b : b + 1, lanes] = row


def place(co, mine, other):
    shape = jax.ShapeDtypeStruct
    return call(
        place_kernel,
        [
            shape((384, 1536), BF),
            shape((1536, 384), BF),
            shape((384, 4096), BF),
            shape((7, 7, 384), F32),
            shape((384,), F32),
            shape((1536,), F32),
            shape((384,), F32),
        ],
        [],
        [smem()] + [vmem()] * 2,
        14,
        5,
    )(co, mine, other)


def swap(v, axes, size, d):
    return lax.ppermute(v, axes, [(i, i ^ d) for i in range(size)])


def exchange(v, axes):
    return lax.all_to_all(v, axes, split_axis=0, concat_axis=0, tiled=True)


def on_device(
    image_tiles,
    depth_kernel,
    norm_gain,
    weight_in,
    bias_in,
    weight_out,
    layer_scale,
    weight_proj,
    image_counts,
    destination,
    row_offset,
    connector,
    cotangent,
):
    at = jnp.stack([lax.axis_index(axis) for axis in ("co", "yh", "yl")]).astype(jnp.int32)
    bb = lax.axis_index(BB).astype(jnp.int32).reshape(1)
    sent = call(
        arrange_kernel, jax.ShapeDtypeStruct((512, 896), BF), [], [vmem()], 4, 2
    )(cotangent)
    cot = exchange(sent.reshape(32, 16, 896), ENC).reshape(512, 896)
    image_tiles, sent, at, bb = lax.optimization_barrier((image_tiles, sent, at, bb))

    live = jnp.arange(32, dtype=jnp.int32) // 16 < image_counts[0]
    code = jnp.where(live, destination[0] * 2 + row_offset[0], -1).astype(BF)
    code = jnp.broadcast_to(jnp.repeat(code, 2)[:, None], (64, 128))
    pay, normt, xhat, rstd, slope, hsum, gsum, bsum, xp = forward(
        image_tiles,
        depth_kernel,
        norm_gain,
        weight_in,
        bias_in,
        weight_out,
        layer_scale,
        code,
    )
    pays = [pay] + [swap(pay, BB, 4, d) for d in (2, 1, 3)]
    wc = fold(lax.optimization_barrier((weight_proj, pay))[0], connector)
    grad_pre, part, give, outer = connector_part(bb, pays, cot, wc)

    near = swap(give, "co", 2, 1)
    far = swap(part[64:] + near[64:], "yh", 2, 1)
    outer = exchange(outer.reshape(16, 24, 896), PLANE)
    row_part, row_give = token_rows(grad_pre, connector)
    near, far, outer, row_part, row_give = lax.optimization_barrier(
        (near, far, outer, row_part, row_give)
    )

    row_near = swap(row_give, "co", 2, 1).astype(F32)
    row_far = swap((row_part[64:].astype(F32) + row_near[64:]).astype(BF), "yh", 2, 1)
    keep, send, dpre, small_a = mlp_back(
        at, near, part, far, normt, slope, hsum, gsum, bsum, weight_out, layer_scale
    )
    recv = swap(send, "co", 2, 1)
    small_b = front_back(dpre, weight_in, xhat, rstd, norm_gain, xp)
    small_b, row_far = lax.optimization_barrier((small_b, row_far))
    packed = pack(keep, recv, small_a, small_b)
    parts = exchange(packed, SAME_CORE)
    packed, outer = lax.optimization_barrier((packed, outer))

    proj = proj_rows(at, outer, connector)
    proj = [proj[7]] + [
        swap(proj[n], COLS, 8, (1 - n % 2) * 4 + (1 - (n % 4) // 2) * 2 + (1 - n // 4))
        for n in range(7)
    ]
    shards = settle(parts, proj)
    whole = exchange(shards, SAME_CORE)

    token_grads = (row_part[:64].astype(F32) + row_near[:64] + row_far.astype(F32)).astype(BF)
    whole, token_grads = lax.optimization_barrier((whole, token_grads))
    grad_in, grad_out, grad_proj, grad_kernel, grad_gain, grad_bias, grad_scale = place(
        at, whole, swap(whole, "co", 2, 1)
    )

    return (
        grad_kernel,
        grad_gain,
        grad_in,
        grad_bias,
        grad_out,
        grad_scale,
        grad_proj,
        token_grads,
    )


def solution(mesh):
    fine = Mesh(mesh.devices.reshape(2, 4, 4, 2, 2), ALL)
    in_specs = (
        P(ALL, None, None, None),
        P(),
        P(),
        P(),
        P(),
        P(),
        P(),
        P(),
        P(ALL),
        P(ALL, None),
        P(ALL, None),
        P(None, BB),
        P(ENC, BB),
    )
    out_specs = (P(), P(), P(), P(), P(), P(), P(), P(ALL, None))
    return jax.shard_map(
        on_device, mesh=fine, in_specs=in_specs, out_specs=out_specs, check_vma=False
    )
```

```python
import jax
import jax.numpy as jnp
import numpy as np
from jax import lax
from jax.experimental import pallas as pl
from jax.experimental.pallas import tpu as pltpu
from jax.sharding import Mesh, PartitionSpec as P

EPS = 1e-06
GELU_A = float(np.sqrt(2.0 / np.pi))
GELU_B = 0.044715
BF = jnp.bfloat16
F32 = jnp.float32
ALL = ("yl", "z", "x", "yh", "co")
ENC = ("yl", "z", "x")
BB = ("yh", "co")
SAME_CORE = ("yl", "z", "x", "yh")
COLS = ("yl", "yh", "co")
MIB = 1024 * 1024


def cost(us):
    return pl.CostEstimate(flops=int(us * 1.1e9) + 1, bytes_accessed=1, transcendentals=0)


def nn(a, b):
    return lax.dot_general(a, b, (((1,), (0,)), ((), ())), preferred_element_type=F32)


def nt(a, b):
    return lax.dot_general(a, b, (((1,), (1,)), ((), ())), preferred_element_type=F32)


def gelu_parts(u):
    u2 = u * u
    t = jnp.tanh(u * (GELU_A + (GELU_A * GELU_B) * u2))
    half = 0.5 * (1.0 + t)
    value = u * half
    slope = half + 0.5 * u * (1.0 - t * t) * (GELU_A + (3.0 * GELU_A * GELU_B) * u2)
    return value, slope


def vmem():
    return pl.BlockSpec(memory_space=pltpu.VMEM)


def hbm():
    return pl.BlockSpec(memory_space=pltpu.HBM)


def smem():
    return pl.BlockSpec(memory_space=pltpu.SMEM)


def call(kernel, out_shape, scratch, in_specs, limit, us):
    multi = isinstance(out_shape, (list, tuple))
    return pl.pallas_call(
        kernel,
        out_shape=out_shape,
        in_specs=in_specs,
        out_specs=[vmem()] * len(out_shape) if multi else vmem(),
        scratch_shapes=scratch,
        compiler_params=pltpu.CompilerParams(vmem_limit_bytes=limit * MIB),
        cost_estimate=cost(us),
    )


def arrange_kernel(cot_ref, out_ref):
    r = lax.broadcasted_iota(jnp.int32, (512, 512), 0)
    s = lax.broadcasted_iota(jnp.int32, (512, 512), 1)
    want = ((r // 4) % 4) * 128 + (r // 16) * 4 + r % 4
    pick = jnp.where(s == want, 1.0, 0.0).astype(BF)
    out_ref[...] = nn(pick, cot_ref[...]).astype(BF)


def shifted(v):
    row = lax.broadcasted_iota(jnp.int32, (8, 128), 0)
    down = jnp.where(row == 0, 0.0, pltpu.roll(v, 1, 0))
    up = jnp.where(row == 7, 0.0, pltpu.roll(v, 7, 0))
    return down, v, up


def forward_kernel(
    x_hbm, k_ref, gain_ref, win_hbm, bias_ref, wout_hbm, scale_ref, code_ref,
    pay_ref, normt_ref, xhat_ref, rstd_ref, slope_ref, hsum_ref, gsum_ref, bsum_ref, xp_ref,
    xf_ref, xs_ref, kb_ref, conv_ref, norm_ref, hs_ref, x_ref, win_ref, wout_ref, sem,
):
    load_x = [pltpu.make_async_copy(x_hbm.at[t], x_ref.at[t], sem.at[t]) for t in range(2)]
    load_win = pltpu.make_async_copy(win_hbm, win_ref, sem.at[2])
    load_wout = pltpu.make_async_copy(wout_hbm, wout_ref, sem.at[3])
    for load in load_x + [load_win, load_wout]:
        load.start()
    for lt in range(3):
        lanes = slice(lt * 128, lt * 128 + 128)
        for a in range(7):
            kb_ref[lt, a] = k_ref[a, :, lanes]
    for t in range(2):
        load_x[t].wait()
        for lt in range(3):
            xf_ref[lt, t] = x_ref[t, :, :, lt * 128 : lt * 128 + 128].astype(F32)

    def split(n, carry):
        lt = n // 2
        t = n % 2
        for jj in range(4):
            plain = []
            for i in range(16):
                v = xf_ref[lt, t, i, pl.ds(jj, 8, stride=4), :]
                plain.append(v)
                for s, w in enumerate(shifted(v)):
                    xs_ref[s, lt, t, jj, i] = w
            xp_ref[lt, t, jj] = jnp.concatenate(plain, axis=0).astype(BF)
        return carry

    lax.fori_loop(0, 6, split, 0)

    def conv(n, carry):
        lt = n // 8
        t = (n // 4) % 2
        jj = n % 4
        acc = [None] * 16
        for b in range(7):
            q = jj + (b + 1)
            s = q // 4
            jin = q % 4
            w = [
                jnp.broadcast_to(kb_ref[lt, a, pl.ds(b, 1), :], (8, 128)) for a in range(7)
            ]
            for r in range(16):
                v = xs_ref[s, lt, t, jin, r]
                for a in range(7):
                    i = r - a + 3
                    if 0 <= i < 16:
                        term = v * w[a]
                        acc[i] = term if acc[i] is None else acc[i] + term
        for i in range(16):
            conv_ref[lt, t, i // 4, jj, i % 4] = acc[i]
        return carry

    lax.fori_loop(0, 24, conv, 0)

    def block(n, carry):
        t = n // 4
        q = n % 4
        rows = pl.ds(pl.multiple_of(n * 128, 128), 128)
        c = [conv_ref[lt, t, q].reshape(128, 128) for lt in range(3)]
        mean = jnp.sum(c[0] + c[1] + c[2], axis=1, keepdims=True) * (1.0 / 384.0)
        c = [v - mean for v in c]
        var = jnp.sum(c[0] * c[0] + c[1] * c[1] + c[2] * c[2], axis=1, keepdims=True) * (
            1.0 / 384.0
        )
        rstd = lax.rsqrt(var + EPS)
        rstd_ref[rows, :] = jnp.broadcast_to(rstd, (128, 128))
        for lt in range(3):
            lanes = slice(lt * 128, lt * 128 + 128)
            xhat = c[lt] * rstd
            xhat_ref[lt, rows, :] = xhat
            normed = xhat * gain_ref[lanes].reshape(1, 128)
            norm_ref[n, :, lanes] = normed.astype(BF)
            normt_ref[n, lanes, :] = normed.T.astype(BF)
        toks = pl.ds(pl.multiple_of(n * 8, 8), 8)
        for h in range(6):
            hid = slice(h * 256, h * 256 + 256)
            u = nn(norm_ref[n], win_ref[:, hid]) + bias_ref[hid].reshape(1, 256)
            value, slope = gelu_parts(u)
            value = value.astype(BF).astype(F32)
            hs_ref[toks, hid] = jnp.sum(value.reshape(16, 8, 256), axis=0)
            gsum_ref[toks, hid] = jnp.sum(slope.reshape(16, 8, 256), axis=0)
            slope_ref[rows, hid] = slope.astype(BF)
        return carry

    load_win.wait()
    lax.fori_loop(0, 8, block, 0, unroll=8)
    load_wout.wait()

    hs = hs_ref[...]
    hi = hs.astype(BF)
    hsum_ref[...] = hi
    lo = (hs - hi.astype(F32)).astype(BF)
    bsum = nn(hi, wout_ref[...]) + nn(lo, wout_ref[...])
    bsum_ref[...] = bsum
    for lt in range(3):
        lanes = slice(lt * 128, lt * 128 + 128)
        for t in range(2):
            for q in range(4):
                total = xs_ref[1, lt, t, 0, 4 * q]
                for jj in range(4):
                    for im in range(4):
                        if jj + im > 0:
                            total = total + xs_ref[1, lt, t, jj, 4 * q + im]
                tok = slice(t * 32 + q * 8, t * 32 + q * 8 + 8)
                hs_ref[tok, lanes] = total
        pooled = hs_ref[:, lanes] + scale_ref[lanes].reshape(1, 128) * bsum[:, lanes]
        pay_ref[:, lanes] = (pooled * (1.0 / 16.0)).astype(BF)
    pay_ref[:, 384:512] = code_ref[...]


def forward(x, k, gain, win, bias, wout, scale, code):
    shape = jax.ShapeDtypeStruct
    return call(
        forward_kernel,
        [
            shape((64, 512), BF),
            shape((8, 384, 128), BF),
            shape((3, 1024, 128), F32),
            shape((1024, 128), F32),
            shape((1024, 1536), BF),
            shape((64, 1536), BF),
            shape((64, 1536), F32),
            shape((64, 384), F32),
            shape((3, 2, 4, 128, 128), BF),
        ],
        [
            pltpu.VMEM((3, 2, 16, 32, 128), F32),
            pltpu.VMEM((3, 3, 2, 4, 16, 8, 128), F32),
            pltpu.VMEM((3, 7, 7, 128), F32),
            pltpu.VMEM((3, 2, 4, 4, 4, 8, 128), F32),
            pltpu.VMEM((8, 128, 384), BF),
            pltpu.VMEM((64, 1536), F32),
            pltpu.VMEM((2, 16, 32, 384), BF),
            pltpu.VMEM((384, 1536), BF),
            pltpu.VMEM((1536, 384), BF),
            pltpu.SemaphoreType.DMA((4,)),
        ],
        [hbm(), vmem(), vmem(), hbm(), vmem(), hbm(), vmem(), vmem()],
        26,
        14,
    )(x, k, gain, win, bias, wout, scale, code)


def fold_kernel(proj_ref, conn_ref, out_ref):
    for at, size in ((0, 512), (512, 384)):
        out_ref[:, at : at + size] = nn(proj_ref[...], conn_ref[:, at : at + size]).astype(BF)


def fold(weight_proj, connector):
    return call(
        fold_kernel, jax.ShapeDtypeStruct((384, 896), BF), [], [vmem()] * 2, 16, 0
    )(weight_proj, connector)


def rows_kernel(gp_ref, conn_ref, keep_ref, send_ref):
    for n in range(8):
        cols = slice(n * 512, n * 512 + 512)
        out = nt(gp_ref[...], conn_ref[cols, :]).astype(BF)
        keep_ref[:, cols] = out[:128]
        send_ref[:, cols] = out[128:]


def token_rows(grad_pre, connector):
    shape = jax.ShapeDtypeStruct((128, 4096), BF)
    return call(rows_kernel, [shape, shape], [], [vmem()] * 2, 14, 0)(grad_pre, connector)


def outer_kernel(at_ref, r0_ref, r1_ref, r2_ref, r3_ref, o0_ref, o1_ref, o2_ref, o3_ref, sum_ref):
    total = r0_ref[...].astype(F32) + r1_ref[...].astype(F32)
    sum_ref[...] = total + r2_ref[...].astype(F32) + r3_ref[...].astype(F32)
    for d, o_ref in enumerate((o0_ref, o1_ref, o2_ref, o3_ref)):
        rows = pl.ds(pl.multiple_of(((at_ref[4] + d) & 3) * 24, 8), 24)
        o_ref[...] = sum_ref[rows, :].astype(BF)


def outer_rows(at, parts):
    return call(
        outer_kernel,
        [jax.ShapeDtypeStruct((24, 896), BF)] * 4,
        [pltpu.VMEM((96, 896), F32)],
        [smem()] + [vmem()] * 4,
        4,
        1,
    )(at, *parts)


def proj_kernel(at_ref, r0_ref, r1_ref, r2_ref, r3_ref, conn_ref, out_ref):
    total = r0_ref[...].astype(F32) + r1_ref[...].astype(F32)
    total = (total + r2_ref[...].astype(F32) + r3_ref[...].astype(F32)).astype(BF)
    for n in range(8):
        chunk = (
            (at_ref[0] ^ (1 - n // 4)) * 4
            + (at_ref[1] ^ (1 - (n % 4) // 2)) * 2
            + (at_ref[2] ^ (1 - n % 2))
        )
        rows = pl.ds(pl.multiple_of(chunk * 512, 512), 512)
        out_ref[n] = nt(total, conn_ref[rows, :]).astype(BF)


def proj_rows(at, parts, connector):
    return call(
        proj_kernel,
        jax.ShapeDtypeStruct((8, 24, 512), BF),
        [],
        [smem()] + [vmem()] * 5,
        14,
        0,
    )(at, *parts, connector)


def connector_kernel(
    at_ref, p0_ref, p1_ref, p2_ref, p3_ref, cot_ref, wc_ref,
    gp_ref, keep_ref, send_ref, s0_ref, s1_ref, s2_ref, s3_ref, pick_ref, pool_ref, poolt_ref,
):
    row = lax.broadcasted_iota(jnp.int32, (64, 128), 0)
    lane = lax.broadcasted_iota(jnp.int32, (64, 128), 1)
    for n, (d, p_ref) in enumerate(((0, p0_ref), (2, p1_ref), (1, p2_ref), (3, p3_ref))):
        tok = slice(n * 64, n * 64 + 64)
        pool_ref[tok, :] = p_ref[:, 0:384]
        code = p_ref[:, 384:512].astype(F32).astype(jnp.int32)
        src = at_ref[5] ^ d
        want = (code >> 1) * 16 + src * 4 + (code & 1) * 2 + (row & 1)
        want = jnp.where(code < 0, -1, want)
        for q in range(4):
            pick_ref[tok, q * 128 : q * 128 + 128] = jnp.where(
                lane + q * 128 == want, 1.0, 0.0
            ).astype(BF)
    for h in range(7):
        cols = slice(h * 128, h * 128 + 128)
        cot = nn(pick_ref[...], cot_ref[:, cols])
        pre = nn(pool_ref[...], wc_ref[:, cols])
        gp_ref[:, cols] = (cot * gelu_parts(pre)[1]).astype(BF)
    tok = nt(gp_ref[...], wc_ref[...])
    keep_ref[...] = tok[:128]
    send_ref[...] = tok[128:]
    poolt_ref[...] = pool_ref[...].astype(F32).T.astype(BF)
    for d, s_ref in enumerate((s0_ref, s1_ref, s2_ref, s3_ref)):
        rows = pl.ds(pl.multiple_of(((at_ref[3] + d) & 3) * 96, 96), 96)
        s_ref[...] = nn(poolt_ref[rows, :], gp_ref[...]).astype(BF)


def connector_part(at, pays, cot, wc):
    shape = jax.ShapeDtypeStruct
    return call(
        connector_kernel,
        [
            shape((256, 896), BF),
            shape((128, 384), F32),
            shape((128, 384), F32),
        ]
        + [shape((96, 896), BF)] * 4,
        [
            pltpu.VMEM((256, 512), BF),
            pltpu.VMEM((256, 384), BF),
            pltpu.VMEM((384, 256), BF),
        ],
        [smem()] + [vmem()] * 6,
        6,
        3,
    )(at, *pays, cot, wc)


def mlp_back_kernel(
    co_ref, near_ref, part_ref, far_ref, normt_ref, slope_ref, hsum_ref, gsum_ref, bsum_ref, wout_ref, scale_ref,
    keep_ref, send_ref, dpre_ref, small_ref, dh_ref,
):
    dtok = (part_ref[0:64, :] + near_ref[0:64, :] + far_ref[...]) * (1.0 / 16.0)
    small_ref[0:1, :] = jnp.sum(dtok * bsum_ref[...], axis=0, keepdims=True)
    dbr = (dtok * scale_ref[...].reshape(1, 384)).astype(BF)
    dh_ref[...] = nt(dbr, wout_ref[...])
    db = jnp.sum(dh_ref[...] * gsum_ref[...], axis=0, keepdims=True)
    for q in range(4):
        small_ref[1 + q : 2 + q, :] = db[:, q * 384 : q * 384 + 384]
    small_ref[5:8, :] = jnp.zeros((3, 384), F32)

    def block(n, carry):
        rows = pl.ds(pl.multiple_of(n * 128, 128), 128)
        toks = pl.ds(pl.multiple_of(n * 8, 8), 8)
        for h in range(4):
            hid = slice(h * 384, h * 384 + 384)
            g = slope_ref[rows, hid].astype(F32).reshape(16, 8, 384)
            d = g * dh_ref[toks, hid][None]
            dpre_ref[h, rows, :] = d.reshape(128, 384).astype(BF)
        return carry

    lax.fori_loop(0, 8, block, 0, unroll=8)
    hsum_t = hsum_ref[...].astype(F32).T.astype(BF)
    normt = jnp.concatenate([normt_ref[n] for n in range(8)], axis=1)
    mine = co_ref[0] == 0
    for h in range(2):
        def put(out_ref):
            for q in range(2):
                rows = slice(q * 384, q * 384 + 384)
                out_ref[rows, :] = nn(normt, dpre_ref[2 * h + q]).astype(out_ref.dtype)
            out_ref[768:1536, :] = nn(hsum_t[h * 768 : h * 768 + 768], dbr).astype(out_ref.dtype)

        here = mine if h == 0 else jnp.logical_not(mine)

        @pl.when(here)
        def _():
            put(keep_ref)

        @pl.when(jnp.logical_not(here))
        def _():
            put(send_ref)


def mlp_back(co, near, part, far, normt, slope, hsum, gsum, bsum, wout, scale):
    shape = jax.ShapeDtypeStruct
    return call(
        mlp_back_kernel,
        [
            shape((1536, 384), BF),
            shape((1536, 384), BF),
            shape((4, 1024, 384), BF),
            shape((8, 384), F32),
        ],
        [pltpu.VMEM((64, 1536), F32)],
        [smem()] + [vmem()] * 10,
        14,
        3,
    )(co, near, part, far, normt, slope, hsum, gsum, bsum, wout, scale)


def front_back_kernel(
    dpre_ref, win_ref, xhat_ref, rstd_ref, gain_ref, xp_ref, out_ref, dc_ref, dk_ref
):
    def block(n, carry):
        t = n // 4
        q = n % 4
        rows = pl.ds(pl.multiple_of(n * 128, 128), 128)
        dn = nt(dpre_ref[0, rows, :], win_ref[:, 0:384])
        for h in range(1, 4):
            dn = dn + nt(dpre_ref[h, rows, :], win_ref[:, h * 384 : h * 384 + 384])
        rstd = rstd_ref[rows, :]
        dx = []
        xh = []
        gains = []
        for lt in range(3):
            lanes = slice(lt * 128, lt * 128 + 128)
            xhat = xhat_ref[lt, rows, :]
            part = dn[:, lanes]
            gains.append(jnp.sum((part * xhat).reshape(16, 8, 128), axis=0))
            dx.append(part * gain_ref[lanes].reshape(1, 128))
            xh.append(xhat)
        m1 = jnp.sum(dx[0] + dx[1] + dx[2], axis=1, keepdims=True) * (1.0 / 384.0)
        m2 = jnp.sum(dx[0] * xh[0] + dx[1] * xh[1] + dx[2] * xh[2], axis=1, keepdims=True) * (
            1.0 / 384.0
        )
        for lt in range(3):
            dc = rstd * (dx[lt] - m1 - xh[lt] * m2)
            for jj in range(4):
                for im in range(4):
                    at = (jj * 4 + im) * 8
                    for s, w in enumerate(shifted(dc[at : at + 8])):
                        dc_ref[s, lt, t, jj, q * 4 + im] = w
        return tuple(c + g for c, g in zip(carry, gains))

    zero = jnp.zeros((8, 128), F32)
    gains = lax.fori_loop(0, 8, block, (zero, zero, zero), unroll=8)
    for lt in range(3):
        lanes = slice(lt * 128, lt * 128 + 128)
        out_ref[49:50, lanes] = jnp.sum(gains[lt], axis=0, keepdims=True)

    dk_ref[...] = jnp.zeros_like(dk_ref)

    def conv(n, carry):
        lt = n // 8
        t = (n // 4) % 2
        jj = n % 4
        x = xp_ref[lt, t, jj].astype(F32)
        x = [x[i * 8 : i * 8 + 8] for i in range(16)]
        for b in range(7):
            q = jj + (7 - b)
            s = q // 4
            jin = q % 4
            acc = [None] * 7
            for i in range(16):
                v = dc_ref[s, lt, t, jin, i]
                for a in range(7):
                    r = i + a - 3
                    if 0 <= r < 16:
                        term = v * x[r]
                        acc[a] = term if acc[a] is None else acc[a] + term
            for a in range(7):
                dk_ref[lt, a * 7 + b] += acc[a]
        return carry

    lax.fori_loop(0, 24, conv, 0)
    for lt in range(3):
        lanes = slice(lt * 128, lt * 128 + 128)
        out_ref[0:49, lanes] = jnp.sum(dk_ref[lt], axis=1)
    out_ref[50:56, :] = jnp.zeros((6, 384), F32)


def front_back(dpre, win, xhat, rstd, gain, xp):
    return call(
        front_back_kernel,
        jax.ShapeDtypeStruct((56, 384), F32),
        [pltpu.VMEM((3, 3, 2, 4, 16, 8, 128), F32), pltpu.VMEM((3, 49, 8, 128), F32)],
        [vmem()] * 6,
        15,
        2,
    )(dpre, win, xhat, rstd, gain, xp)


def three(v):
    return [v[:, q * 128 : q * 128 + 128] for q in range(3)]


def two_parts(v):
    high = v.astype(BF).astype(F32)
    return three(high) + three(v - high)


def pack_kernel(keep_ref, recv_ref, a_ref, b_ref, out_ref):
    pad = jnp.zeros((2, 128), F32)

    def one(n, small):
        rows = slice(n * 24, n * 24 + 24)
        pair = keep_ref[rows, :].astype(F32) + recv_ref[rows, :].astype(F32)
        out_ref[n] = jnp.concatenate(three(pair) + two_parts(small) + [pad], axis=0).astype(BF)

    for n in range(64):
        one(n, a_ref[n : n + 1, :] if n < 8 else b_ref[n - 8 : n - 7, :])


def pack(keep, recv, small_a, small_b):
    return call(
        pack_kernel, jax.ShapeDtypeStruct((64, 80, 128), BF), [], [vmem()] * 4, 6, 2
    )(keep, recv, small_a, small_b)


def settle_kernel(parts_ref, *refs):
    proj_refs, out_ref = refs[:8], refs[8]
    total = parts_ref[0].astype(F32)
    for n in range(1, 64):
        total = total + parts_ref[n].astype(F32)
    total = total * (1.0 / 128.0)
    small = total[72:75] + total[75:78]
    high = small.astype(BF).astype(F32)
    proj = proj_refs[0][...].astype(F32)
    for ref in proj_refs[1:]:
        proj = proj + ref[...].astype(F32)
    proj = proj * (1.0 / 128.0)
    shard = jnp.concatenate(
        [total[:72], high, small - high, total[78:80]]
        + [proj[:, q * 128 : q * 128 + 128] for q in range(4)],
        axis=0,
    ).astype(BF)
    for n in range(64):
        out_ref[n] = shard


def settle(parts, proj):
    return call(
        settle_kernel, jax.ShapeDtypeStruct((64, 176, 128), BF), [], [vmem()] * 9, 6, 2
    )(parts, *proj)


def place_kernel(
    co_ref, mine_ref, other_ref,
    in_ref, out_ref, proj_ref, kernel_ref, gain_ref, bias_ref, scale_ref,
):
    def put(src_ref, half):
        def pair(low, high, at):
            return jnp.concatenate(
                [
                    src_ref[low, at : at + 24, :].astype(F32),
                    src_ref[high, at : at + 24, :].astype(F32),
                ],
                axis=0,
            ).astype(BF)

        for p in range(3):
            for m in range(8):
                rows = slice(m * 48, m * 48 + 48)
                for q in range(2):
                    n = q * 16 + 2 * m
                    col = half * 768 + q * 384 + p * 128
                    in_ref[rows, col : col + 128] = pair(n, n + 1, p * 24)
            for m in range(16):
                at = half * 768 + m * 48
                out_ref[at : at + 48, p * 128 : p * 128 + 128] = pair(
                    32 + 2 * m, 33 + 2 * m, p * 24
                )
        for yl in range(2):
            for yh in range(2):
                for p in range(4):
                    col = (half * 4 + yh * 2 + yl) * 512 + p * 128
                    for m in range(8):
                        n = yl * 32 + 4 * m + yh
                        proj_ref[m * 48 : m * 48 + 48, col : col + 128] = pair(
                            n, n + 2, 80 + p * 24
                        )

    low = co_ref[0] == 0

    @pl.when(low)
    def _():
        put(mine_ref, 0)
        put(other_ref, 1)

    @pl.when(jnp.logical_not(low))
    def _():
        put(other_ref, 0)
        put(mine_ref, 1)

    for n in range(58):
        small = mine_ref[n, 64:80, :].astype(F32) + other_ref[n, 64:80, :].astype(F32)
        small = small[8:11] + small[11:14]
        for p in range(3):
            lanes = slice(p * 128, p * 128 + 128)
            row = small[p : p + 1]
            if n == 0:
                scale_ref[lanes] = row.reshape(128)
            elif n < 5:
                bias_ref[(n - 1) * 384 + p * 128 : (n - 1) * 384 + p * 128 + 128] = row.reshape(128)
            elif n == 57:
                gain_ref[lanes] = row.reshape(128)
            elif n >= 8:
                a, b = (n - 8) // 7, (n - 8) % 7
                kernel_ref[a, b : b + 1, lanes] = row


def place(co, mine, other):
    shape = jax.ShapeDtypeStruct
    return call(
        place_kernel,
        [
            shape((384, 1536), BF),
            shape((1536, 384), BF),
            shape((384, 4096), BF),
            shape((7, 7, 384), F32),
            shape((384,), F32),
            shape((1536,), F32),
            shape((384,), F32),
        ],
        [],
        [smem()] + [vmem()] * 2,
        14,
        5,
    )(co, mine, other)


def swap(v, axes, size, d):
    return lax.ppermute(v, axes, [(i, i ^ d) for i in range(size)])


def turn(parts, axis):
    return [parts[0]] + [
        lax.ppermute(parts[d], axis, [(i, (i + d) % 4) for i in range(4)]) for d in (1, 2, 3)
    ]


def exchange(v, axes):
    return lax.all_to_all(v, axes, split_axis=0, concat_axis=0, tiled=True)


def on_device(
    image_tiles,
    depth_kernel,
    norm_gain,
    weight_in,
    bias_in,
    weight_out,
    layer_scale,
    weight_proj,
    image_counts,
    destination,
    row_offset,
    connector,
    cotangent,
):
    at = ("co", "yh", "yl", "z", "x", BB)
    at = jnp.stack([lax.axis_index(axis) for axis in at]).astype(jnp.int32)
    sent = call(
        arrange_kernel,
        jax.ShapeDtypeStruct((512, 896), BF),
        [],
        [vmem()],
        4,
        2,
    )(cotangent)
    cot = exchange(sent.reshape(32, 16, 896), ENC).reshape(512, 896)
    image_tiles, sent, at = lax.optimization_barrier((image_tiles, sent, at))

    live = jnp.arange(32, dtype=jnp.int32) // 16 < image_counts[0]
    code = jnp.where(live, destination[0] * 2 + row_offset[0], -1).astype(BF)
    code = jnp.broadcast_to(jnp.repeat(code, 2)[:, None], (64, 128))
    pay, normt, xhat, rstd, slope, hsum, gsum, bsum, xp = forward(
        image_tiles,
        depth_kernel,
        norm_gain,
        weight_in,
        bias_in,
        weight_out,
        layer_scale,
        code,
    )
    pays = [pay] + [swap(pay, BB, 4, d) for d in (2, 1, 3)]
    wc = fold(lax.optimization_barrier((weight_proj, pay))[0], connector)
    grad_pre, part, give, *outer = connector_part(at, pays, cot, wc)

    near = swap(give, "co", 2, 1)
    far = swap(part[64:] + near[64:], "yh", 2, 1)
    outer = turn(outer, "z")
    row_part, row_give = token_rows(grad_pre, connector)
    row_near = swap(row_give, "co", 2, 1).astype(F32)
    row_tail = (row_part[64:].astype(F32) + row_near[64:]).astype(BF)
    near, far, row_tail = lax.optimization_barrier((near, far, row_tail))
    row_far = swap(row_tail, "yh", 2, 1)
    keep, send, dpre, small_a = mlp_back(
        at, near, part, far, normt, slope, hsum, gsum, bsum, weight_out, layer_scale
    )
    send, dpre, *outer = lax.optimization_barrier((send, dpre, *outer))
    recv = swap(send, "co", 2, 1)
    outer = turn(outer_rows(at, outer), "x")
    small_b = front_back(dpre, weight_in, xhat, rstd, norm_gain, xp)
    small_b, row_far, outer = lax.optimization_barrier((small_b, row_far, outer))
    packed = pack(keep, recv, small_a, small_b)
    parts = exchange(packed, SAME_CORE)
    packed, outer = lax.optimization_barrier((packed, outer))

    proj = proj_rows(at, outer, connector)
    proj = [proj[7]] + [
        swap(proj[n], COLS, 8, (1 - n % 2) * 4 + (1 - (n % 4) // 2) * 2 + (1 - n // 4))
        for n in range(7)
    ]
    shards = settle(parts, proj)
    whole = exchange(shards, SAME_CORE)

    token_grads = (row_part[:64].astype(F32) + row_near[:64] + row_far.astype(F32)).astype(BF)
    whole, token_grads = lax.optimization_barrier((whole, token_grads))
    grad_in, grad_out, grad_proj, grad_kernel, grad_gain, grad_bias, grad_scale = place(
        at, whole, swap(whole, "co", 2, 1)
    )

    return (
        grad_kernel,
        grad_gain,
        grad_in,
        grad_bias,
        grad_out,
        grad_scale,
        grad_proj,
        token_grads,
    )


def solution(mesh):
    fine = Mesh(mesh.devices.reshape(2, 4, 4, 2, 2), ALL)
    in_specs = (
        P(ALL, None, None, None),
        P(),
        P(),
        P(),
        P(),
        P(),
        P(),
        P(),
        P(ALL),
        P(ALL, None),
        P(ALL, None),
        P(None, BB),
        P(ENC, BB),
    )
    out_specs = (P(), P(), P(), P(), P(), P(), P(), P(ALL, None))
    return jax.shard_map(
        on_device, mesh=fine, in_specs=in_specs, out_specs=out_specs, check_vma=False
    )
```

```python
import jax
import jax.numpy as jnp
import numpy as np
from jax import lax
from jax.experimental import pallas as pl
from jax.experimental.pallas import tpu as pltpu
from jax.sharding import Mesh, PartitionSpec as P

EPS = 1e-06
GELU_A = float(np.sqrt(2.0 / np.pi))
GELU_B = 0.044715
BF = jnp.bfloat16
F32 = jnp.float32
ALL = ("yl", "z", "x", "yh", "co")
ENC = ("yl", "z", "x")
BB = ("yh", "co")
SAME_CORE = ("yl", "z", "x", "yh")
COLS = ("yl", "yh", "co")
MIB = 1024 * 1024


def cost(us):
    return pl.CostEstimate(flops=int(us * 1.1e9) + 1, bytes_accessed=1, transcendentals=0)


def nn(a, b):
    return lax.dot_general(a, b, (((1,), (0,)), ((), ())), preferred_element_type=F32)


def nt(a, b):
    return lax.dot_general(a, b, (((1,), (1,)), ((), ())), preferred_element_type=F32)


def gelu_parts(u):
    u2 = u * u
    t = jnp.tanh(u * (GELU_A + (GELU_A * GELU_B) * u2))
    half = 0.5 * t + 0.5
    value = u * half
    slope = half + value * (1.0 - half) * (2.0 * GELU_A + (6.0 * GELU_A * GELU_B) * u2)
    return value, slope


def vmem():
    return pl.BlockSpec(memory_space=pltpu.VMEM)


def hbm():
    return pl.BlockSpec(memory_space=pltpu.HBM)


def smem():
    return pl.BlockSpec(memory_space=pltpu.SMEM)


def call(kernel, out_shape, scratch, in_specs, limit, us):
    multi = isinstance(out_shape, (list, tuple))
    return pl.pallas_call(
        kernel,
        out_shape=out_shape,
        in_specs=in_specs,
        out_specs=[vmem()] * len(out_shape) if multi else vmem(),
        scratch_shapes=scratch,
        compiler_params=pltpu.CompilerParams(vmem_limit_bytes=limit * MIB),
        cost_estimate=cost(us),
    )


def arrange_kernel(cot_ref, out_ref):
    r = lax.broadcasted_iota(jnp.int32, (512, 512), 0)
    s = lax.broadcasted_iota(jnp.int32, (512, 512), 1)
    want = ((r // 4) % 4) * 128 + (r // 16) * 4 + r % 4
    pick = jnp.where(s == want, 1.0, 0.0).astype(BF)
    out_ref[...] = nn(pick, cot_ref[...]).astype(BF)


def shifted(v):
    row = lax.broadcasted_iota(jnp.int32, (8, 128), 0)
    down = jnp.where(row == 0, 0.0, pltpu.roll(v, 1, 0))
    up = jnp.where(row == 7, 0.0, pltpu.roll(v, 7, 0))
    return down, v, up


def forward_kernel(
    x_hbm, k_ref, gain_ref, win_hbm, bias_ref, wout_hbm, scale_ref, code_ref,
    pay_ref, normt_ref, xhat_ref, rstd_ref, slope_ref, hsum_ref, gsum_ref, bsum_ref, xp_ref,
    xf_ref, xs_ref, kb_ref, conv_ref, norm_ref, hs_ref, x_ref, win_ref, wout_ref, sem,
):
    load_x = [pltpu.make_async_copy(x_hbm.at[t], x_ref.at[t], sem.at[t]) for t in range(2)]
    load_win = pltpu.make_async_copy(win_hbm, win_ref, sem.at[2])
    load_wout = pltpu.make_async_copy(wout_hbm, wout_ref, sem.at[3])
    for load in load_x + [load_win, load_wout]:
        load.start()
    for lt in range(3):
        lanes = slice(lt * 128, lt * 128 + 128)
        for a in range(7):
            kb_ref[lt, a] = k_ref[a, :, lanes]
    for t in range(2):
        load_x[t].wait()
        for lt in range(3):
            xf_ref[lt, t] = x_ref[t, :, :, lt * 128 : lt * 128 + 128].astype(F32)

    def split(n, carry):
        lt = n // 2
        t = n % 2
        for jj in range(4):
            plain = []
            for i in range(16):
                v = xf_ref[lt, t, i, pl.ds(jj, 8, stride=4), :]
                plain.append(v)
                for s, w in enumerate(shifted(v)):
                    xs_ref[s, lt, t, jj, i] = w
            xp_ref[lt, t, jj] = jnp.concatenate(plain, axis=0).astype(BF)
        return carry

    lax.fori_loop(0, 6, split, 0)

    def conv(n, carry):
        lt = n // 8
        t = (n // 4) % 2
        jj = n % 4
        acc = [None] * 16
        for b in range(7):
            q = jj + (b + 1)
            s = q // 4
            jin = q % 4
            w = [
                jnp.broadcast_to(kb_ref[lt, a, pl.ds(b, 1), :], (8, 128)) for a in range(7)
            ]
            for r in range(16):
                v = xs_ref[s, lt, t, jin, r]
                for a in range(7):
                    i = r - a + 3
                    if 0 <= i < 16:
                        term = v * w[a]
                        acc[i] = term if acc[i] is None else acc[i] + term
        for i in range(16):
            conv_ref[lt, t, i // 4, jj, i % 4] = acc[i]
        return carry

    lax.fori_loop(0, 24, conv, 0)

    def block(n, carry):
        t = n // 4
        q = n % 4
        rows = pl.ds(pl.multiple_of(n * 128, 128), 128)
        c = [conv_ref[lt, t, q].reshape(128, 128) for lt in range(3)]
        mean = jnp.sum(c[0] + c[1] + c[2], axis=1, keepdims=True) * (1.0 / 384.0)
        c = [v - mean for v in c]
        var = jnp.sum(c[0] * c[0] + c[1] * c[1] + c[2] * c[2], axis=1, keepdims=True) * (
            1.0 / 384.0
        )
        rstd = lax.rsqrt(var + EPS)
        rstd_ref[rows, :] = jnp.broadcast_to(rstd, (128, 128))
        for lt in range(3):
            lanes = slice(lt * 128, lt * 128 + 128)
            xhat = c[lt] * rstd
            xhat_ref[lt, rows, :] = xhat.astype(BF)
            normed = xhat * gain_ref[lanes].reshape(1, 128)
            norm_ref[n // 2, (n % 2) * 128 : (n % 2) * 128 + 128, lanes] = normed.astype(BF)
            normt_ref[n, lanes, :] = normed.T.astype(BF)
        return carry

    def widen(m, carry):
        for h in range(6):
            hid = slice(h * 256, h * 256 + 256)
            u = nn(norm_ref[m], win_ref[:, hid]) + bias_ref[hid].reshape(1, 256)
            value, slope = gelu_parts(u)
            toks = pl.ds(pl.multiple_of(m * 16, 8), 16)
            rows = pl.ds(pl.multiple_of(m * 256, 256), 256)
            hs_ref[toks, hid] = jnp.sum(value.reshape(2, 16, 8, 256), axis=1).reshape(16, 256)
            gsum_ref[toks, hid] = jnp.sum(slope.reshape(2, 16, 8, 256), axis=1).reshape(16, 256)
            slope_ref[rows, hid] = slope.astype(BF)
        return carry

    load_win.wait()
    for m in range(4):
        block(2 * m, 0)
        block(2 * m + 1, 0)
        widen(m, 0)
    load_wout.wait()

    hs = hs_ref[...]
    hi = hs.astype(BF)
    hsum_ref[...] = hi
    lo = (hs - hi.astype(F32)).astype(BF)
    bsum = nn(hi, wout_ref[...]) + nn(lo, wout_ref[...])
    bsum_ref[...] = bsum
    for lt in range(3):
        lanes = slice(lt * 128, lt * 128 + 128)
        for t in range(2):
            for q in range(4):
                total = xs_ref[1, lt, t, 0, 4 * q]
                for jj in range(4):
                    for im in range(4):
                        if jj + im > 0:
                            total = total + xs_ref[1, lt, t, jj, 4 * q + im]
                tok = slice(t * 32 + q * 8, t * 32 + q * 8 + 8)
                hs_ref[tok, lanes] = total
        pooled = hs_ref[:, lanes] + scale_ref[lanes].reshape(1, 128) * bsum[:, lanes]
        pay_ref[:, lanes] = (pooled * (1.0 / 16.0)).astype(BF)
    pay_ref[:, 384:512] = code_ref[...]


def forward(x, k, gain, win, bias, wout, scale, code):
    shape = jax.ShapeDtypeStruct
    return call(
        forward_kernel,
        [
            shape((64, 512), BF),
            shape((8, 384, 128), BF),
            shape((3, 1024, 128), BF),
            shape((1024, 128), F32),
            shape((1024, 1536), BF),
            shape((64, 1536), BF),
            shape((64, 1536), F32),
            shape((64, 384), F32),
            shape((3, 2, 4, 128, 128), BF),
        ],
        [
            pltpu.VMEM((3, 2, 16, 32, 128), F32),
            pltpu.VMEM((3, 3, 2, 4, 16, 8, 128), F32),
            pltpu.VMEM((3, 7, 7, 128), F32),
            pltpu.VMEM((3, 2, 4, 4, 4, 8, 128), F32),
            pltpu.VMEM((4, 256, 384), BF),
            pltpu.VMEM((64, 1536), F32),
            pltpu.VMEM((2, 16, 32, 384), BF),
            pltpu.VMEM((384, 1536), BF),
            pltpu.VMEM((1536, 384), BF),
            pltpu.SemaphoreType.DMA((4,)),
        ],
        [hbm(), vmem(), vmem(), hbm(), vmem(), hbm(), vmem(), vmem()],
        26,
        14,
    )(x, k, gain, win, bias, wout, scale, code)


def fold_kernel(proj_ref, conn_ref, out_ref):
    for at, size in ((0, 512), (512, 384)):
        out_ref[:, at : at + size] = nn(proj_ref[...], conn_ref[:, at : at + size]).astype(BF)


def fold(weight_proj, connector):
    return call(
        fold_kernel, jax.ShapeDtypeStruct((384, 896), BF), [], [vmem()] * 2, 16, 0
    )(weight_proj, connector)


def rows_kernel(gp_ref, conn_ref, keep_ref, send_ref):
    for n in range(8):
        cols = slice(n * 512, n * 512 + 512)
        out = nt(gp_ref[...], conn_ref[cols, :]).astype(BF)
        keep_ref[:, cols] = out[:128]
        send_ref[:, cols] = out[128:]


def token_rows(grad_pre, connector):
    shape = jax.ShapeDtypeStruct((128, 4096), BF)
    return call(rows_kernel, [shape, shape], [], [vmem()] * 2, 14, 0)(grad_pre, connector)


def outer_kernel(at_ref, r0_ref, r1_ref, r2_ref, r3_ref, o0_ref, o1_ref, o2_ref, o3_ref, sum_ref):
    total = r0_ref[...].astype(F32) + r1_ref[...].astype(F32)
    sum_ref[...] = total + r2_ref[...].astype(F32) + r3_ref[...].astype(F32)
    for d, o_ref in enumerate((o0_ref, o1_ref, o2_ref, o3_ref)):
        rows = pl.ds(pl.multiple_of(((at_ref[4] + d) & 3) * 24, 8), 24)
        o_ref[...] = sum_ref[rows, :].astype(BF)


def outer_rows(at, parts):
    return call(
        outer_kernel,
        [jax.ShapeDtypeStruct((24, 896), BF)] * 4,
        [pltpu.VMEM((96, 896), F32)],
        [smem()] + [vmem()] * 4,
        4,
        1,
    )(at, *parts)


def proj_kernel(at_ref, r0_ref, r1_ref, r2_ref, r3_ref, conn_ref, out_ref):
    total = r0_ref[...].astype(F32) + r1_ref[...].astype(F32)
    total = (total + r2_ref[...].astype(F32) + r3_ref[...].astype(F32)).astype(BF)
    for n in range(8):
        chunk = (
            (at_ref[0] ^ (1 - n // 4)) * 4
            + (at_ref[1] ^ (1 - (n % 4) // 2)) * 2
            + (at_ref[2] ^ (1 - n % 2))
        )
        rows = pl.ds(pl.multiple_of(chunk * 512, 512), 512)
        out_ref[n] = nt(total, conn_ref[rows, :]).astype(BF)


def proj_rows(at, parts, connector):
    return call(
        proj_kernel,
        jax.ShapeDtypeStruct((8, 24, 512), BF),
        [],
        [smem()] + [vmem()] * 5,
        14,
        0,
    )(at, *parts, connector)


def connector_kernel(
    at_ref, p0_ref, p1_ref, p2_ref, p3_ref, cot_ref, wc_ref,
    gp_ref, keep_ref, send_ref, s0_ref, s1_ref, s2_ref, s3_ref, pick_ref, pool_ref, poolt_ref,
):
    row = lax.broadcasted_iota(jnp.int32, (64, 128), 0)
    lane = lax.broadcasted_iota(jnp.int32, (64, 128), 1)
    for n, (d, p_ref) in enumerate(((0, p0_ref), (2, p1_ref), (1, p2_ref), (3, p3_ref))):
        tok = slice(n * 64, n * 64 + 64)
        pool_ref[tok, :] = p_ref[:, 0:384]
        code = p_ref[:, 384:512].astype(F32).astype(jnp.int32)
        src = at_ref[5] ^ d
        want = (code >> 1) * 16 + src * 4 + (code & 1) * 2 + (row & 1)
        want = jnp.where(code < 0, -1, want)
        for q in range(4):
            pick_ref[tok, q * 128 : q * 128 + 128] = jnp.where(
                lane + q * 128 == want, 1.0, 0.0
            ).astype(BF)
    for low, high in ((0, 256), (256, 512), (512, 768), (768, 896)):
        cols = slice(low, high)
        cot = nn(pick_ref[...], cot_ref[:, cols])
        pre = nn(pool_ref[...], wc_ref[:, cols])
        gp_ref[:, cols] = (cot * gelu_parts(pre)[1]).astype(BF)
    tok = nt(gp_ref[...], wc_ref[...])
    keep_ref[...] = tok[:128]
    send_ref[...] = tok[128:]
    poolt_ref[...] = pool_ref[...].astype(F32).T.astype(BF)
    for d, s_ref in enumerate((s0_ref, s1_ref, s2_ref, s3_ref)):
        rows = pl.ds(pl.multiple_of(((at_ref[3] + d) & 3) * 96, 96), 96)
        s_ref[...] = nn(poolt_ref[rows, :], gp_ref[...]).astype(BF)


def connector_part(at, pays, cot, wc):
    shape = jax.ShapeDtypeStruct
    return call(
        connector_kernel,
        [
            shape((256, 896), BF),
            shape((128, 384), F32),
            shape((128, 384), F32),
        ]
        + [shape((96, 896), BF)] * 4,
        [
            pltpu.VMEM((256, 512), BF),
            pltpu.VMEM((256, 384), BF),
            pltpu.VMEM((384, 256), BF),
        ],
        [smem()] + [vmem()] * 6,
        6,
        3,
    )(at, *pays, cot, wc)


def mlp_back_kernel(
    co_ref, near_ref, part_ref, far_ref, normt_ref, slope_ref, hsum_ref, gsum_ref, bsum_ref, wout_ref, scale_ref,
    keep_ref, send_ref, dpre_ref, small_ref, dh_ref,
):
    dtok = (part_ref[0:64, :] + near_ref[0:64, :] + far_ref[...].astype(F32)) * (1.0 / 16.0)
    small_ref[0:1, :] = jnp.sum(dtok * bsum_ref[...], axis=0, keepdims=True)
    dbr = (dtok * scale_ref[...].reshape(1, 384)).astype(BF)
    dh_ref[...] = nt(dbr, wout_ref[...])
    db = jnp.sum(dh_ref[...] * gsum_ref[...], axis=0, keepdims=True)
    for q in range(4):
        small_ref[1 + q : 2 + q, :] = db[:, q * 384 : q * 384 + 384]
    small_ref[5:8, :] = jnp.zeros((3, 384), F32)

    def block(n, carry):
        rows = pl.ds(pl.multiple_of(n * 128, 128), 128)
        toks = pl.ds(pl.multiple_of(n * 8, 8), 8)
        for h in range(4):
            hid = slice(h * 384, h * 384 + 384)
            g = slope_ref[rows, hid].astype(F32).reshape(16, 8, 384)
            d = g * dh_ref[toks, hid][None]
            dpre_ref[h, rows, :] = d.reshape(128, 384).astype(BF)
        return carry

    lax.fori_loop(0, 8, block, 0, unroll=8)
    hsum_t = hsum_ref[...].astype(F32).T.astype(BF)
    normt = jnp.concatenate([normt_ref[n] for n in range(8)], axis=1)
    mine = co_ref[0] == 0
    for h in range(2):
        def put(out_ref):
            for q in range(2):
                rows = slice(q * 384, q * 384 + 384)
                out_ref[rows, :] = nn(normt, dpre_ref[2 * h + q]).astype(out_ref.dtype)
            out_ref[768:1536, :] = nn(hsum_t[h * 768 : h * 768 + 768], dbr).astype(out_ref.dtype)

        here = mine if h == 0 else jnp.logical_not(mine)

        @pl.when(here)
        def _():
            put(keep_ref)

        @pl.when(jnp.logical_not(here))
        def _():
            put(send_ref)


def mlp_back(co, near, part, far, normt, slope, hsum, gsum, bsum, wout, scale):
    shape = jax.ShapeDtypeStruct
    return call(
        mlp_back_kernel,
        [
            shape((1536, 384), BF),
            shape((1536, 384), BF),
            shape((4, 1024, 384), BF),
            shape((8, 384), F32),
        ],
        [pltpu.VMEM((64, 1536), F32)],
        [smem()] + [vmem()] * 10,
        14,
        12,
    )(co, near, part, far, normt, slope, hsum, gsum, bsum, wout, scale)


def front_back_kernel(
    dpre_ref, win_ref, xhat_ref, rstd_ref, gain_ref, xp_ref, out_ref, dc_ref, dk_ref
):
    def block(n, carry):
        t = n // 4
        q = n % 4
        rows = pl.ds(pl.multiple_of(n * 128, 128), 128)
        dn = dns[n // 2][(n % 2) * 128 : (n % 2) * 128 + 128]
        rstd = rstd_ref[rows, :]
        dx = []
        xh = []
        gains = []
        for lt in range(3):
            lanes = slice(lt * 128, lt * 128 + 128)
            xhat = xhat_ref[lt, rows, :].astype(F32)
            part = dn[:, lanes]
            gains.append(jnp.sum((part * xhat).reshape(16, 8, 128), axis=0))
            dx.append(part * gain_ref[lanes].reshape(1, 128))
            xh.append(xhat)
        m1 = jnp.sum(dx[0] + dx[1] + dx[2], axis=1, keepdims=True) * (1.0 / 384.0)
        m2 = jnp.sum(dx[0] * xh[0] + dx[1] * xh[1] + dx[2] * xh[2], axis=1, keepdims=True) * (
            1.0 / 384.0
        )
        for lt in range(3):
            dc = rstd * (dx[lt] - m1 - xh[lt] * m2)
            for jj in range(4):
                for im in range(4):
                    at = (jj * 4 + im) * 8
                    for s, w in enumerate(shifted(dc[at : at + 8])):
                        dc_ref[s, lt, t, jj, q * 4 + im] = w
        return tuple(c + g for c, g in zip(carry, gains))

    zero = jnp.zeros((8, 128), F32)
    gains = (zero, zero, zero)
    dns = []
    for m in range(4):
        part = slice(m * 256, m * 256 + 256)
        dn = nt(dpre_ref[0, part, :], win_ref[:, 0:384])
        for h in range(1, 4):
            dn = dn + nt(dpre_ref[h, part, :], win_ref[:, h * 384 : h * 384 + 384])
        dns.append(dn)
        gains = block(2 * m, gains)
        gains = block(2 * m + 1, gains)
    for lt in range(3):
        lanes = slice(lt * 128, lt * 128 + 128)
        out_ref[49:50, lanes] = jnp.sum(gains[lt], axis=0, keepdims=True)

    dk_ref[...] = jnp.zeros_like(dk_ref)

    def conv(n, carry):
        lt = n // 8
        t = (n // 4) % 2
        jj = n % 4
        x = xp_ref[lt, t, jj].astype(F32)
        x = [x[i * 8 : i * 8 + 8] for i in range(16)]
        for b in range(7):
            q = jj + (7 - b)
            s = q // 4
            jin = q % 4
            acc = [None] * 7
            for i in range(16):
                v = dc_ref[s, lt, t, jin, i]
                for a in range(7):
                    r = i + a - 3
                    if 0 <= r < 16:
                        term = v * x[r]
                        acc[a] = term if acc[a] is None else acc[a] + term
            for a in range(7):
                dk_ref[lt, a * 7 + b] += acc[a]
        return carry

    lax.fori_loop(0, 24, conv, 0)
    for lt in range(3):
        lanes = slice(lt * 128, lt * 128 + 128)
        out_ref[0:49, lanes] = jnp.sum(dk_ref[lt], axis=1)
    out_ref[50:56, :] = jnp.zeros((6, 384), F32)


def front_back(dpre, win, xhat, rstd, gain, xp):
    return call(
        front_back_kernel,
        jax.ShapeDtypeStruct((56, 384), F32),
        [pltpu.VMEM((3, 3, 2, 4, 16, 8, 128), F32), pltpu.VMEM((3, 49, 8, 128), F32)],
        [vmem()] * 6,
        15,
        2,
    )(dpre, win, xhat, rstd, gain, xp)


def three(v):
    return [v[:, q * 128 : q * 128 + 128] for q in range(3)]


def two_parts(v):
    high = v.astype(BF).astype(F32)
    return three(high) + three(v - high)


def pack_kernel(keep_ref, recv_ref, a_ref, b_ref, out_ref):
    pad = jnp.zeros((2, 128), F32)

    def one(n, small):
        rows = slice(n * 24, n * 24 + 24)
        pair = keep_ref[rows, :].astype(F32) + recv_ref[rows, :].astype(F32)
        out_ref[n] = jnp.concatenate(three(pair) + two_parts(small) + [pad], axis=0).astype(BF)

    for n in range(64):
        one(n, a_ref[n : n + 1, :] if n < 8 else b_ref[n - 8 : n - 7, :])


def pack(keep, recv, small_a, small_b):
    return call(
        pack_kernel, jax.ShapeDtypeStruct((64, 80, 128), BF), [], [vmem()] * 4, 6, 2
    )(keep, recv, small_a, small_b)


def settle_kernel(parts_ref, *refs):
    proj_refs, out_ref = refs[:8], refs[8]
    total = parts_ref[0].astype(F32)
    for n in range(1, 64):
        total = total + parts_ref[n].astype(F32)
    total = total * (1.0 / 128.0)
    small = total[72:75] + total[75:78]
    high = small.astype(BF).astype(F32)
    proj = proj_refs[0][...].astype(F32)
    for ref in proj_refs[1:]:
        proj = proj + ref[...].astype(F32)
    proj = proj * (1.0 / 128.0)
    shard = jnp.concatenate(
        [total[:72], high, small - high, total[78:80]]
        + [proj[:, q * 128 : q * 128 + 128] for q in range(4)],
        axis=0,
    ).astype(BF)
    for n in range(64):
        out_ref[n] = shard


def settle(parts, proj):
    return call(
        settle_kernel, jax.ShapeDtypeStruct((64, 176, 128), BF), [], [vmem()] * 9, 6, 2
    )(parts, *proj)


def place_half(src_ref, half, refs, outs, sem):
    in_ref, out_ref, proj_ref = refs

    def pair(low, high, at):
        return jnp.concatenate(
            [
                src_ref[low, at : at + 24, :].astype(F32),
                src_ref[high, at : at + 24, :].astype(F32),
            ],
            axis=0,
        ).astype(BF)

    wide = pl.ds(pl.multiple_of(half * 768, 128), 768)
    tall = pl.ds(pl.multiple_of(half * 768, 128), 768)
    cols = pl.ds(pl.multiple_of(half * 2048, 128), 2048)
    copies = [
        pltpu.make_async_copy(in_ref, outs[0].at[:, wide], sem.at[0]),
        pltpu.make_async_copy(out_ref, outs[1].at[tall, :], sem.at[1]),
        pltpu.make_async_copy(proj_ref, outs[2].at[:, cols], sem.at[2]),
    ]
    for yl in range(2):
        for yh in range(2):
            for p in range(4):
                col = (yh * 2 + yl) * 512 + p * 128
                for m in range(8):
                    n = yl * 32 + 4 * m + yh
                    proj_ref[m * 48 : m * 48 + 48, col : col + 128] = pair(n, n + 2, 80 + p * 24)
    copies[2].start()
    for p in range(3):
        for m in range(16):
            out_ref[m * 48 : m * 48 + 48, p * 128 : p * 128 + 128] = pair(
                32 + 2 * m, 33 + 2 * m, p * 24
            )
    copies[1].start()
    for p in range(3):
        for m in range(8):
            for q in range(2):
                n = q * 16 + 2 * m
                col = q * 384 + p * 128
                in_ref[m * 48 : m * 48 + 48, col : col + 128] = pair(n, n + 1, p * 24)
    copies[0].start()
    return copies


def small_rows(src_ref, n):
    rows = src_ref[n, 64:80, :].astype(F32)
    return rows[8:11] + rows[11:14]


def place_own_kernel(
    co_ref, mine_ref, in_hbm, out_hbm, proj_hbm, small_ref, in_ref, out_ref, proj_ref, sem
):
    copies = place_half(
        mine_ref, co_ref[0], (in_ref, out_ref, proj_ref), (in_hbm, out_hbm, proj_hbm), sem
    )
    for n in range(64):
        small = small_rows(mine_ref, n)
        for p in range(3):
            small_ref[n : n + 1, p * 128 : p * 128 + 128] = small[p : p + 1]
    for copy in copies:
        copy.wait()


def place_other_kernel(
    co_ref, other_ref, small_ref, in_from, out_from, proj_from,
    in_hbm, out_hbm, proj_hbm, kernel_ref, gain_ref, bias_ref, scale_ref,
    in_ref, out_ref, proj_ref, sem,
):
    copies = place_half(
        other_ref, 1 - co_ref[0], (in_ref, out_ref, proj_ref), (in_hbm, out_hbm, proj_hbm), sem
    )
    for n in range(58):
        small = small_rows(other_ref, n)
        for p in range(3):
            lanes = slice(p * 128, p * 128 + 128)
            row = small[p : p + 1] + small_ref[n : n + 1, lanes]
            if n == 0:
                scale_ref[lanes] = row.reshape(128)
            elif n < 5:
                bias_ref[(n - 1) * 384 + p * 128 : (n - 1) * 384 + p * 128 + 128] = row.reshape(128)
            elif n == 57:
                gain_ref[lanes] = row.reshape(128)
            elif n >= 8:
                a, b = (n - 8) // 7, (n - 8) % 7
                kernel_ref[a, b : b + 1, lanes] = row
    for copy in copies:
        copy.wait()


def place(co, mine, other):
    shape = jax.ShapeDtypeStruct
    large = [shape((384, 1536), BF), shape((1536, 384), BF), shape((384, 4096), BF)]
    scratch = [
        pltpu.VMEM((384, 768), BF),
        pltpu.VMEM((768, 384), BF),
        pltpu.VMEM((384, 2048), BF),
        pltpu.SemaphoreType.DMA((3,)),
    ]
    params = pltpu.CompilerParams(vmem_limit_bytes=10 * MIB)
    *held, small = pl.pallas_call(
        place_own_kernel,
        out_shape=large + [shape((64, 384), F32)],
        in_specs=[smem(), vmem()],
        out_specs=[hbm()] * 3 + [vmem()],
        scratch_shapes=scratch,
        compiler_params=params,
        cost_estimate=cost(3),
    )(co, mine)
    return pl.pallas_call(
        place_other_kernel,
        out_shape=large
        + [shape((7, 7, 384), F32), shape((384,), F32), shape((1536,), F32), shape((384,), F32)],
        in_specs=[smem(), vmem(), vmem()] + [hbm()] * 3,
        out_specs=[hbm()] * 3 + [vmem()] * 4,
        scratch_shapes=scratch,
        input_output_aliases={3: 0, 4: 1, 5: 2},
        compiler_params=params,
        cost_estimate=cost(3),
    )(co, other, small, *held)


def swap(v, axes, size, d):
    return lax.ppermute(v, axes, [(i, i ^ d) for i in range(size)])


def turn(parts, axis):
    return [parts[0]] + [
        lax.ppermute(parts[d], axis, [(i, (i + d) % 4) for i in range(4)]) for d in (1, 2, 3)
    ]


def exchange(v, axes):
    return lax.all_to_all(v, axes, split_axis=0, concat_axis=0, tiled=True)


def on_device(
    image_tiles,
    depth_kernel,
    norm_gain,
    weight_in,
    bias_in,
    weight_out,
    layer_scale,
    weight_proj,
    image_counts,
    destination,
    row_offset,
    connector,
    cotangent,
):
    at = ("co", "yh", "yl", "z", "x", BB)
    at = jnp.stack([lax.axis_index(axis) for axis in at]).astype(jnp.int32)
    sent = call(
        arrange_kernel,
        jax.ShapeDtypeStruct((512, 896), BF),
        [],
        [vmem()],
        4,
        2,
    )(cotangent)
    cot = exchange(sent.reshape(32, 16, 896), ENC).reshape(512, 896)
    image_tiles, sent, at = lax.optimization_barrier((image_tiles, sent, at))

    live = jnp.arange(32, dtype=jnp.int32) // 16 < image_counts[0]
    code = jnp.where(live, destination[0] * 2 + row_offset[0], -1).astype(BF)
    code = jnp.broadcast_to(jnp.repeat(code, 2)[:, None], (64, 128))
    pay, normt, xhat, rstd, slope, hsum, gsum, bsum, xp = forward(
        image_tiles,
        depth_kernel,
        norm_gain,
        weight_in,
        bias_in,
        weight_out,
        layer_scale,
        code,
    )
    pays = [pay] + [swap(pay, BB, 4, d) for d in (2, 1, 3)]
    wc = fold(lax.optimization_barrier((weight_proj, pay))[0], connector)
    grad_pre, part, give, *outer = connector_part(at, pays, cot, wc)

    near = swap(give, "co", 2, 1)
    far = swap((part[64:] + near[64:]).astype(BF), "yh", 2, 1)
    outer = turn(outer, "z")
    row_part, row_give = token_rows(grad_pre, connector)
    row_near = swap(row_give, "co", 2, 1).astype(F32)
    row_tail = (row_part[64:].astype(F32) + row_near[64:]).astype(BF)
    near, far, row_tail = lax.optimization_barrier((near, far, row_tail))
    row_far = swap(row_tail, "yh", 2, 1)
    keep, send, dpre, small_a = mlp_back(
        at, near, part, far, normt, slope, hsum, gsum, bsum, weight_out, layer_scale
    )
    send, dpre, *outer = lax.optimization_barrier((send, dpre, *outer))
    recv = swap(send, "co", 2, 1)
    outer = turn(outer_rows(at, outer), "x")
    small_b = front_back(dpre, weight_in, xhat, rstd, norm_gain, xp)
    small_b, row_far, outer = lax.optimization_barrier((small_b, row_far, outer))
    packed = pack(keep, recv, small_a, small_b)
    parts = exchange(packed, SAME_CORE)
    packed, outer = lax.optimization_barrier((packed, outer))

    proj = proj_rows(at, outer, connector)
    proj = [proj[7]] + [
        swap(proj[n], COLS, 8, (1 - n % 2) * 4 + (1 - (n % 4) // 2) * 2 + (1 - n // 4))
        for n in range(7)
    ]
    shards = settle(parts, proj)
    whole = exchange(shards, SAME_CORE)

    token_grads = (row_part[:64].astype(F32) + row_near[:64] + row_far.astype(F32)).astype(BF)
    whole, token_grads = lax.optimization_barrier((whole, token_grads))
    grad_in, grad_out, grad_proj, grad_kernel, grad_gain, grad_bias, grad_scale = place(
        at, whole, swap(whole, "co", 2, 1)
    )

    return (
        grad_kernel,
        grad_gain,
        grad_in,
        grad_bias,
        grad_out,
        grad_scale,
        grad_proj,
        token_grads,
    )


def solution(mesh):
    fine = Mesh(mesh.devices.reshape(2, 4, 4, 2, 2), ALL)
    in_specs = (
        P(ALL, None, None, None),
        P(),
        P(),
        P(),
        P(),
        P(),
        P(),
        P(),
        P(ALL),
        P(ALL, None),
        P(ALL, None),
        P(None, BB),
        P(ENC, BB),
    )
    out_specs = (P(), P(), P(), P(), P(), P(), P(), P(ALL, None))
    return jax.shard_map(
        on_device, mesh=fine, in_specs=in_specs, out_specs=out_specs, check_vma=False
    )
```

```python
import jax
import jax.numpy as jnp
import numpy as np
from jax import lax
from jax.experimental import pallas as pl
from jax.experimental.pallas import tpu as pltpu
from jax.sharding import Mesh, PartitionSpec as P

EPS = 1e-06
GELU_A = float(np.sqrt(2.0 / np.pi))
GELU_B = 0.044715
BF = jnp.bfloat16
F32 = jnp.float32
ALL = ("yl", "z", "x", "yh", "co")
ENC = ("yl", "z", "x")
BB = ("yh", "co")
SAME_CORE = ("yl", "z", "x", "yh")
COLS = ("yl", "yh", "co")
MIB = 1024 * 1024


def cost(us):
    return pl.CostEstimate(flops=int(us * 1.1e9) + 1, bytes_accessed=1, transcendentals=0)


def nn(a, b):
    return lax.dot_general(a, b, (((1,), (0,)), ((), ())), preferred_element_type=F32)


def nt(a, b):
    return lax.dot_general(a, b, (((1,), (1,)), ((), ())), preferred_element_type=F32)


def gelu_parts(u):
    u2 = u * u
    t = jnp.tanh(u * (GELU_A + (GELU_A * GELU_B) * u2))
    half = 0.5 * t + 0.5
    value = u * half
    slope = half + value * (1.0 - half) * (2.0 * GELU_A + (6.0 * GELU_A * GELU_B) * u2)
    return value, slope


def vmem():
    return pl.BlockSpec(memory_space=pltpu.VMEM)


def hbm():
    return pl.BlockSpec(memory_space=pltpu.HBM)


def smem():
    return pl.BlockSpec(memory_space=pltpu.SMEM)


def call(kernel, out_shape, scratch, in_specs, limit, us):
    multi = isinstance(out_shape, (list, tuple))
    return pl.pallas_call(
        kernel,
        out_shape=out_shape,
        in_specs=in_specs,
        out_specs=[vmem()] * len(out_shape) if multi else vmem(),
        scratch_shapes=scratch,
        compiler_params=pltpu.CompilerParams(vmem_limit_bytes=limit * MIB),
        cost_estimate=cost(us),
    )


def arrange_kernel(cot_ref, out_ref):
    r = lax.broadcasted_iota(jnp.int32, (512, 512), 0)
    s = lax.broadcasted_iota(jnp.int32, (512, 512), 1)
    want = ((r // 4) % 4) * 128 + (r // 16) * 4 + r % 4
    pick = jnp.where(s == want, 1.0, 0.0).astype(BF)
    out_ref[...] = nn(pick, cot_ref[...]).astype(BF)


def shifted(v):
    row = lax.broadcasted_iota(jnp.int32, (8, 128), 0)
    down = jnp.where(row == 0, 0.0, pltpu.roll(v, 1, 0))
    up = jnp.where(row == 7, 0.0, pltpu.roll(v, 7, 0))
    return down, v, up


def forward_kernel(
    x_hbm, k_ref, gain_ref, win_hbm, bias_ref, wout_hbm, scale_ref, code_ref,
    pay_ref, normt_ref, xhat_ref, rstd_ref, slope_ref, hsum_ref, gsum_ref, bsum_ref, xp_ref,
    xf_ref, xs_ref, kb_ref, conv_ref, norm_ref, hs_ref, x_ref, win_ref, wout_ref, sem,
):
    load_x = [pltpu.make_async_copy(x_hbm.at[t], x_ref.at[t], sem.at[t]) for t in range(2)]
    load_win = pltpu.make_async_copy(win_hbm, win_ref, sem.at[2])
    load_wout = pltpu.make_async_copy(wout_hbm, wout_ref, sem.at[3])
    for load in load_x + [load_win, load_wout]:
        load.start()
    for lt in range(3):
        lanes = slice(lt * 128, lt * 128 + 128)
        for a in range(7):
            kb_ref[lt, a] = k_ref[a, :, lanes]
    for t in range(2):
        load_x[t].wait()
        for lt in range(3):
            xf_ref[lt, t] = x_ref[t, :, :, lt * 128 : lt * 128 + 128].astype(F32)

    def split(n, carry):
        lt = n // 2
        t = n % 2
        for jj in range(4):
            plain = []
            for i in range(16):
                v = xf_ref[lt, t, i, pl.ds(jj, 8, stride=4), :]
                plain.append(v)
                for s, w in enumerate(shifted(v)):
                    xs_ref[s, lt, t, jj, i] = w
            xp_ref[lt, t, jj] = jnp.concatenate(plain, axis=0).astype(BF)
        return carry

    lax.fori_loop(0, 6, split, 0)

    def conv(n, carry):
        lt = n // 8
        t = (n // 4) % 2
        jj = n % 4
        acc = [None] * 16
        for b in range(7):
            q = jj + (b + 1)
            s = q // 4
            jin = q % 4
            w = [
                jnp.broadcast_to(kb_ref[lt, a, pl.ds(b, 1), :], (8, 128)) for a in range(7)
            ]
            for r in range(16):
                v = xs_ref[s, lt, t, jin, r]
                for a in range(7):
                    i = r - a + 3
                    if 0 <= i < 16:
                        term = v * w[a]
                        acc[i] = term if acc[i] is None else acc[i] + term
        for i in range(16):
            conv_ref[lt, t, i // 4, jj, i % 4] = acc[i]
        return carry

    lax.fori_loop(0, 24, conv, 0)

    def block(n, carry):
        t = n // 4
        q = n % 4
        rows = pl.ds(pl.multiple_of(n * 128, 128), 128)
        c = [conv_ref[lt, t, q].reshape(128, 128) for lt in range(3)]
        mean = jnp.sum(c[0] + c[1] + c[2], axis=1, keepdims=True) * (1.0 / 384.0)
        c = [v - mean for v in c]
        var = jnp.sum(c[0] * c[0] + c[1] * c[1] + c[2] * c[2], axis=1, keepdims=True) * (
            1.0 / 384.0
        )
        rstd = lax.rsqrt(var + EPS)
        rstd_ref[rows, :] = jnp.broadcast_to(rstd, (128, 128))
        for lt in range(3):
            lanes = slice(lt * 128, lt * 128 + 128)
            xhat = c[lt] * rstd
            xhat_ref[lt, rows, :] = xhat.astype(BF)
            normed = xhat * gain_ref[lanes].reshape(1, 128)
            norm_ref[n // 2, (n % 2) * 128 : (n % 2) * 128 + 128, lanes] = normed.astype(BF)
            normt_ref[n, lanes, :] = normed.T.astype(BF)
        return carry

    def widen(m, carry):
        for h in range(6):
            hid = slice(h * 256, h * 256 + 256)
            u = nn(norm_ref[m], win_ref[:, hid]) + bias_ref[hid].reshape(1, 256)
            value, slope = gelu_parts(u)
            toks = pl.ds(pl.multiple_of(m * 16, 8), 16)
            rows = pl.ds(pl.multiple_of(m * 256, 256), 256)
            hs_ref[toks, hid] = jnp.sum(value.reshape(2, 16, 8, 256), axis=1).reshape(16, 256)
            gsum_ref[toks, hid] = jnp.sum(slope.reshape(2, 16, 8, 256), axis=1).reshape(16, 256)
            slope_ref[rows, hid] = slope.astype(BF)
        return carry

    load_win.wait()
    for m in range(4):
        block(2 * m, 0)
        block(2 * m + 1, 0)
        widen(m, 0)
    load_wout.wait()

    hs = hs_ref[...]
    hi = hs.astype(BF)
    hsum_ref[...] = hi
    lo = (hs - hi.astype(F32)).astype(BF)
    bsum = nn(hi, wout_ref[...]) + nn(lo, wout_ref[...])
    bsum_ref[...] = bsum
    for lt in range(3):
        lanes = slice(lt * 128, lt * 128 + 128)
        for t in range(2):
            for q in range(4):
                total = xs_ref[1, lt, t, 0, 4 * q]
                for jj in range(4):
                    for im in range(4):
                        if jj + im > 0:
                            total = total + xs_ref[1, lt, t, jj, 4 * q + im]
                tok = slice(t * 32 + q * 8, t * 32 + q * 8 + 8)
                hs_ref[tok, lanes] = total
        pooled = hs_ref[:, lanes] + scale_ref[lanes].reshape(1, 128) * bsum[:, lanes]
        pay_ref[:, lanes] = (pooled * (1.0 / 16.0)).astype(BF)
    pay_ref[:, 384:512] = code_ref[...]


def forward(x, k, gain, win, bias, wout, scale, code):
    shape = jax.ShapeDtypeStruct
    return call(
        forward_kernel,
        [
            shape((64, 512), BF),
            shape((8, 384, 128), BF),
            shape((3, 1024, 128), BF),
            shape((1024, 128), F32),
            shape((1024, 1536), BF),
            shape((64, 1536), BF),
            shape((64, 1536), F32),
            shape((64, 384), F32),
            shape((3, 2, 4, 128, 128), BF),
        ],
        [
            pltpu.VMEM((3, 2, 16, 32, 128), F32),
            pltpu.VMEM((3, 3, 2, 4, 16, 8, 128), F32),
            pltpu.VMEM((3, 7, 7, 128), F32),
            pltpu.VMEM((3, 2, 4, 4, 4, 8, 128), F32),
            pltpu.VMEM((4, 256, 384), BF),
            pltpu.VMEM((64, 1536), F32),
            pltpu.VMEM((2, 16, 32, 384), BF),
            pltpu.VMEM((384, 1536), BF),
            pltpu.VMEM((1536, 384), BF),
            pltpu.SemaphoreType.DMA((4,)),
        ],
        [hbm(), vmem(), vmem(), hbm(), vmem(), hbm(), vmem(), vmem()],
        26,
        14,
    )(x, k, gain, win, bias, wout, scale, code)


def fold_kernel(proj_ref, conn_ref, out_ref):
    for at, size in ((0, 512), (512, 384)):
        out_ref[:, at : at + size] = nn(proj_ref[...], conn_ref[:, at : at + size]).astype(BF)


def fold(weight_proj, connector):
    return call(
        fold_kernel, jax.ShapeDtypeStruct((384, 896), BF), [], [vmem()] * 2, 16, 0
    )(weight_proj, connector)


def rows_kernel(gp_ref, conn_ref, keep_ref, send_ref):
    for n in range(8):
        cols = slice(n * 512, n * 512 + 512)
        out = nt(gp_ref[...], conn_ref[cols, :]).astype(BF)
        keep_ref[:, cols] = out[:128]
        send_ref[:, cols] = out[128:]


def token_rows(grad_pre, connector):
    shape = jax.ShapeDtypeStruct((128, 4096), BF)
    return call(rows_kernel, [shape, shape], [], [vmem()] * 2, 14, 0)(grad_pre, connector)


def outer_kernel(at_ref, r0_ref, r1_ref, r2_ref, r3_ref, o0_ref, o1_ref, o2_ref, o3_ref, sum_ref):
    total = r0_ref[...].astype(F32) + r1_ref[...].astype(F32)
    sum_ref[...] = total + r2_ref[...].astype(F32) + r3_ref[...].astype(F32)
    for d, o_ref in enumerate((o0_ref, o1_ref, o2_ref, o3_ref)):
        rows = pl.ds(pl.multiple_of(((at_ref[4] + d) & 3) * 24, 8), 24)
        o_ref[...] = sum_ref[rows, :].astype(BF)


def outer_rows(at, parts):
    return call(
        outer_kernel,
        [jax.ShapeDtypeStruct((24, 896), BF)] * 4,
        [pltpu.VMEM((96, 896), F32)],
        [smem()] + [vmem()] * 4,
        4,
        1,
    )(at, *parts)


def proj_kernel(at_ref, r0_ref, r1_ref, r2_ref, r3_ref, conn_ref, out_ref):
    total = r0_ref[...].astype(F32) + r1_ref[...].astype(F32)
    total = (total + r2_ref[...].astype(F32) + r3_ref[...].astype(F32)).astype(BF)
    for n in range(8):
        chunk = (
            (at_ref[0] ^ (1 - n // 4)) * 4
            + (at_ref[1] ^ (1 - (n % 4) // 2)) * 2
            + (at_ref[2] ^ (1 - n % 2))
        )
        rows = pl.ds(pl.multiple_of(chunk * 512, 512), 512)
        out_ref[n] = nt(total, conn_ref[rows, :]).astype(BF)


def proj_rows(at, parts, connector):
    return call(
        proj_kernel,
        jax.ShapeDtypeStruct((8, 24, 512), BF),
        [],
        [smem()] + [vmem()] * 5,
        14,
        0,
    )(at, *parts, connector)


def connector_kernel(
    at_ref, p0_ref, p1_ref, p2_ref, p3_ref, cot_ref, wc_ref,
    gp_ref, keep_ref, send_ref, s0_ref, s1_ref, s2_ref, s3_ref, pick_ref, pool_ref, poolt_ref,
):
    row = lax.broadcasted_iota(jnp.int32, (64, 128), 0)
    lane = lax.broadcasted_iota(jnp.int32, (64, 128), 1)
    for n, (d, p_ref) in enumerate(((0, p0_ref), (2, p1_ref), (1, p2_ref), (3, p3_ref))):
        tok = slice(n * 64, n * 64 + 64)
        pool_ref[tok, :] = p_ref[:, 0:384]
        code = p_ref[:, 384:512].astype(F32).astype(jnp.int32)
        src = at_ref[5] ^ d
        want = (code >> 1) * 16 + src * 4 + (code & 1) * 2 + (row & 1)
        want = jnp.where(code < 0, -1, want)
        for q in range(4):
            pick_ref[tok, q * 128 : q * 128 + 128] = jnp.where(
                lane + q * 128 == want, 1.0, 0.0
            ).astype(BF)
    for low, high in ((0, 256), (256, 512), (512, 768), (768, 896)):
        cols = slice(low, high)
        cot = nn(pick_ref[...], cot_ref[:, cols])
        pre = nn(pool_ref[...], wc_ref[:, cols])
        gp_ref[:, cols] = (cot * gelu_parts(pre)[1]).astype(BF)
    tok = nt(gp_ref[...], wc_ref[...])
    keep_ref[...] = tok[:128]
    send_ref[...] = tok[128:]
    poolt_ref[...] = pool_ref[...].astype(F32).T.astype(BF)
    for d, s_ref in enumerate((s0_ref, s1_ref, s2_ref, s3_ref)):
        rows = pl.ds(pl.multiple_of(((at_ref[3] + d) & 3) * 96, 96), 96)
        s_ref[...] = nn(poolt_ref[rows, :], gp_ref[...]).astype(BF)


def connector_part(at, pays, cot, wc):
    shape = jax.ShapeDtypeStruct
    return call(
        connector_kernel,
        [
            shape((256, 896), BF),
            shape((128, 384), F32),
            shape((128, 384), F32),
        ]
        + [shape((96, 896), BF)] * 4,
        [
            pltpu.VMEM((256, 512), BF),
            pltpu.VMEM((256, 384), BF),
            pltpu.VMEM((384, 256), BF),
        ],
        [smem()] + [vmem()] * 6,
        6,
        3,
    )(at, *pays, cot, wc)


def mlp_back_kernel(
    co_ref, near_ref, part_ref, far_ref, normt_ref, slope_ref, hsum_ref, gsum_ref, bsum_ref, wout_ref, scale_ref,
    keep_ref, send_ref, dpre_ref, small_ref, dh_ref,
):
    dtok = (part_ref[0:64, :] + near_ref[0:64, :] + far_ref[...].astype(F32)) * (1.0 / 16.0)
    small_ref[0:1, :] = jnp.sum(dtok * bsum_ref[...], axis=0, keepdims=True)
    dbr = (dtok * scale_ref[...].reshape(1, 384)).astype(BF)
    dh_ref[...] = nt(dbr, wout_ref[...])
    db = jnp.sum(dh_ref[...] * gsum_ref[...], axis=0, keepdims=True)
    for q in range(4):
        small_ref[1 + q : 2 + q, :] = db[:, q * 384 : q * 384 + 384]
    small_ref[5:8, :] = jnp.zeros((3, 384), F32)

    def block(n, carry):
        rows = pl.ds(pl.multiple_of(n * 128, 128), 128)
        toks = pl.ds(pl.multiple_of(n * 8, 8), 8)
        for h in range(4):
            hid = slice(h * 384, h * 384 + 384)
            g = slope_ref[rows, hid].astype(F32).reshape(16, 8, 384)
            d = g * dh_ref[toks, hid][None]
            dpre_ref[h, rows, :] = d.reshape(128, 384).astype(BF)
        return carry

    lax.fori_loop(0, 8, block, 0, unroll=8)
    hsum_t = hsum_ref[...].astype(F32).T.astype(BF)
    normt = jnp.concatenate([normt_ref[n] for n in range(8)], axis=1)
    mine = co_ref[0] == 0
    for h in range(2):
        def put(out_ref):
            for q in range(2):
                rows = slice(q * 384, q * 384 + 384)
                out_ref[rows, :] = nn(normt, dpre_ref[2 * h + q]).astype(out_ref.dtype)
            out_ref[768:1536, :] = nn(hsum_t[h * 768 : h * 768 + 768], dbr).astype(out_ref.dtype)

        here = mine if h == 0 else jnp.logical_not(mine)

        @pl.when(here)
        def _():
            put(keep_ref)

        @pl.when(jnp.logical_not(here))
        def _():
            put(send_ref)


def mlp_back(co, near, part, far, normt, slope, hsum, gsum, bsum, wout, scale):
    shape = jax.ShapeDtypeStruct
    return call(
        mlp_back_kernel,
        [
            shape((1536, 384), BF),
            shape((1536, 384), BF),
            shape((4, 1024, 384), BF),
            shape((8, 384), F32),
        ],
        [pltpu.VMEM((64, 1536), F32)],
        [smem()] + [vmem()] * 10,
        14,
        12,
    )(co, near, part, far, normt, slope, hsum, gsum, bsum, wout, scale)


def front_back_kernel(
    dpre_ref, win_ref, xhat_ref, rstd_ref, gain_ref, xp_ref, out_ref, dc_ref, dk_ref
):
    def block(n, carry):
        t = n // 4
        q = n % 4
        rows = pl.ds(pl.multiple_of(n * 128, 128), 128)
        dn = dns[n // 2][(n % 2) * 128 : (n % 2) * 128 + 128]
        rstd = rstd_ref[rows, :]
        dx = []
        xh = []
        gains = []
        for lt in range(3):
            lanes = slice(lt * 128, lt * 128 + 128)
            xhat = xhat_ref[lt, rows, :].astype(F32)
            part = dn[:, lanes]
            gains.append(jnp.sum((part * xhat).reshape(16, 8, 128), axis=0))
            dx.append(part * gain_ref[lanes].reshape(1, 128))
            xh.append(xhat)
        m1 = jnp.sum(dx[0] + dx[1] + dx[2], axis=1, keepdims=True) * (1.0 / 384.0)
        m2 = jnp.sum(dx[0] * xh[0] + dx[1] * xh[1] + dx[2] * xh[2], axis=1, keepdims=True) * (
            1.0 / 384.0
        )
        for lt in range(3):
            dc = rstd * (dx[lt] - m1 - xh[lt] * m2)
            for jj in range(4):
                for im in range(4):
                    at = (jj * 4 + im) * 8
                    for s, w in enumerate(shifted(dc[at : at + 8])):
                        dc_ref[s, lt, t, jj, q * 4 + im] = w
        return tuple(c + g for c, g in zip(carry, gains))

    zero = jnp.zeros((8, 128), F32)
    gains = (zero, zero, zero)
    dns = []
    for m in range(4):
        part = slice(m * 256, m * 256 + 256)
        dn = nt(dpre_ref[0, part, :], win_ref[:, 0:384])
        for h in range(1, 4):
            dn = dn + nt(dpre_ref[h, part, :], win_ref[:, h * 384 : h * 384 + 384])
        dns.append(dn)
        gains = block(2 * m, gains)
        gains = block(2 * m + 1, gains)
    for lt in range(3):
        lanes = slice(lt * 128, lt * 128 + 128)
        out_ref[49:50, lanes] = jnp.sum(gains[lt], axis=0, keepdims=True)

    dk_ref[...] = jnp.zeros_like(dk_ref)

    def conv(n, carry):
        lt = n // 8
        t = (n // 4) % 2
        jj = n % 4
        x = xp_ref[lt, t, jj].astype(F32)
        x = [x[i * 8 : i * 8 + 8] for i in range(16)]
        for b in range(7):
            q = jj + (7 - b)
            s = q // 4
            jin = q % 4
            acc = [None] * 7
            for i in range(16):
                v = dc_ref[s, lt, t, jin, i]
                for a in range(7):
                    r = i + a - 3
                    if 0 <= r < 16:
                        term = v * x[r]
                        acc[a] = term if acc[a] is None else acc[a] + term
            for a in range(7):
                dk_ref[lt, a * 7 + b] += acc[a]
        return carry

    lax.fori_loop(0, 24, conv, 0)
    for lt in range(3):
        lanes = slice(lt * 128, lt * 128 + 128)
        out_ref[0:49, lanes] = jnp.sum(dk_ref[lt], axis=1)
    out_ref[50:56, :] = jnp.zeros((6, 384), F32)


def front_back(dpre, win, xhat, rstd, gain, xp):
    return call(
        front_back_kernel,
        jax.ShapeDtypeStruct((56, 384), F32),
        [pltpu.VMEM((3, 3, 2, 4, 16, 8, 128), F32), pltpu.VMEM((3, 49, 8, 128), F32)],
        [vmem()] * 6,
        15,
        2,
    )(dpre, win, xhat, rstd, gain, xp)


def three(v):
    return [v[:, q * 128 : q * 128 + 128] for q in range(3)]


def two_parts(v):
    high = v.astype(BF).astype(F32)
    return three(high) + three(v - high)


def pack_kernel(keep_ref, recv_ref, a_ref, b_ref, out_ref):
    pad = jnp.zeros((2, 128), F32)

    def one(n, small):
        rows = slice(n * 24, n * 24 + 24)
        pair = keep_ref[rows, :].astype(F32) + recv_ref[rows, :].astype(F32)
        out_ref[n] = jnp.concatenate(three(pair) + two_parts(small) + [pad], axis=0).astype(BF)

    for n in range(64):
        one(n, a_ref[n : n + 1, :] if n < 8 else b_ref[n - 8 : n - 7, :])


def pack(keep, recv, small_a, small_b):
    return call(
        pack_kernel, jax.ShapeDtypeStruct((64, 80, 128), BF), [], [vmem()] * 4, 6, 2
    )(keep, recv, small_a, small_b)


def settle_kernel(parts_ref, *refs):
    proj_refs, out_ref = refs[:8], refs[8]
    total = parts_ref[0].astype(F32)
    for n in range(1, 64):
        total = total + parts_ref[n].astype(F32)
    total = total * (1.0 / 128.0)
    small = total[72:75] + total[75:78]
    high = small.astype(BF).astype(F32)
    proj = proj_refs[0][...].astype(F32)
    for ref in proj_refs[1:]:
        proj = proj + ref[...].astype(F32)
    proj = proj * (1.0 / 128.0)
    shard = jnp.concatenate(
        [total[:72], high, small - high, total[78:80]]
        + [proj[:, q * 128 : q * 128 + 128] for q in range(4)],
        axis=0,
    ).astype(BF)
    for n in range(64):
        out_ref[n] = shard


def settle(parts, proj):
    return call(
        settle_kernel, jax.ShapeDtypeStruct((64, 176, 128), BF), [], [vmem()] * 9, 6, 2
    )(parts, *proj)


def place_half(src_ref, half, refs, outs, sem):
    in_ref, out_ref, proj_ref = refs

    def pair(low, high, at):
        return jnp.concatenate(
            [
                src_ref[low, at : at + 24, :].astype(F32),
                src_ref[high, at : at + 24, :].astype(F32),
            ],
            axis=0,
        ).astype(BF)

    wide = pl.ds(pl.multiple_of(half * 768, 128), 768)
    tall = pl.ds(pl.multiple_of(half * 768, 128), 768)
    cols = pl.ds(pl.multiple_of(half * 2048, 128), 2048)
    copies = [
        pltpu.make_async_copy(in_ref, outs[0].at[:, wide], sem.at[0]),
        pltpu.make_async_copy(out_ref, outs[1].at[tall, :], sem.at[1]),
        pltpu.make_async_copy(proj_ref, outs[2].at[:, cols], sem.at[2]),
    ]
    for yl in range(2):
        for yh in range(2):
            for p in range(4):
                col = (yh * 2 + yl) * 512 + p * 128
                for m in range(8):
                    n = yl * 32 + 4 * m + yh
                    proj_ref[m * 48 : m * 48 + 48, col : col + 128] = pair(n, n + 2, 80 + p * 24)
    copies[2].start()
    for p in range(3):
        for m in range(16):
            out_ref[m * 48 : m * 48 + 48, p * 128 : p * 128 + 128] = pair(
                32 + 2 * m, 33 + 2 * m, p * 24
            )
    copies[1].start()
    for p in range(3):
        for m in range(8):
            for q in range(2):
                n = q * 16 + 2 * m
                col = q * 384 + p * 128
                in_ref[m * 48 : m * 48 + 48, col : col + 128] = pair(n, n + 1, p * 24)
    copies[0].start()
    return copies


def small_rows(src_ref, n):
    rows = src_ref[n, 64:80, :].astype(F32)
    return rows[8:11] + rows[11:14]


def place_own_kernel(
    co_ref, mine_ref, in_hbm, out_hbm, proj_hbm, small_ref, in_ref, out_ref, proj_ref, sem
):
    copies = place_half(
        mine_ref, co_ref[0], (in_ref, out_ref, proj_ref), (in_hbm, out_hbm, proj_hbm), sem
    )
    for n in range(64):
        small = small_rows(mine_ref, n)
        for p in range(3):
            small_ref[n : n + 1, p * 128 : p * 128 + 128] = small[p : p + 1]
    for copy in copies:
        copy.wait()


def place_other_kernel(
    co_ref, other_ref, small_ref, in_from, out_from, proj_from,
    in_hbm, out_hbm, proj_hbm, kernel_ref, gain_ref, bias_ref, scale_ref,
    in_ref, out_ref, proj_ref, sem,
):
    copies = place_half(
        other_ref, 1 - co_ref[0], (in_ref, out_ref, proj_ref), (in_hbm, out_hbm, proj_hbm), sem
    )
    for n in range(58):
        small = small_rows(other_ref, n)
        for p in range(3):
            lanes = slice(p * 128, p * 128 + 128)
            row = small[p : p + 1] + small_ref[n : n + 1, lanes]
            if n == 0:
                scale_ref[lanes] = row.reshape(128)
            elif n < 5:
                bias_ref[(n - 1) * 384 + p * 128 : (n - 1) * 384 + p * 128 + 128] = row.reshape(128)
            elif n == 57:
                gain_ref[lanes] = row.reshape(128)
            elif n >= 8:
                a, b = (n - 8) // 7, (n - 8) % 7
                kernel_ref[a, b : b + 1, lanes] = row
    for copy in copies:
        copy.wait()


def place(co, mine, other):
    shape = jax.ShapeDtypeStruct
    large = [shape((384, 1536), BF), shape((1536, 384), BF), shape((384, 4096), BF)]
    scratch = [
        pltpu.VMEM((384, 768), BF),
        pltpu.VMEM((768, 384), BF),
        pltpu.VMEM((384, 2048), BF),
        pltpu.SemaphoreType.DMA((3,)),
    ]
    params = pltpu.CompilerParams(vmem_limit_bytes=10 * MIB)
    *held, small = pl.pallas_call(
        place_own_kernel,
        out_shape=large + [shape((64, 384), F32)],
        in_specs=[smem(), vmem()],
        out_specs=[hbm()] * 3 + [vmem()],
        scratch_shapes=scratch,
        compiler_params=params,
        cost_estimate=cost(3),
    )(co, mine)
    return pl.pallas_call(
        place_other_kernel,
        out_shape=large
        + [shape((7, 7, 384), F32), shape((384,), F32), shape((1536,), F32), shape((384,), F32)],
        in_specs=[smem(), vmem(), vmem()] + [hbm()] * 3,
        out_specs=[hbm()] * 3 + [vmem()] * 4,
        scratch_shapes=scratch,
        input_output_aliases={3: 0, 4: 1, 5: 2},
        compiler_params=params,
        cost_estimate=cost(3),
    )(co, other, small, *held)


def swap(v, axes, size, d):
    return lax.ppermute(v, axes, [(i, i ^ d) for i in range(size)])


def turn(parts, axis):
    return [parts[0]] + [
        lax.ppermute(parts[d], axis, [(i, (i + d) % 4) for i in range(4)]) for d in (1, 2, 3)
    ]


def exchange(v, axes):
    return lax.all_to_all(v, axes, split_axis=0, concat_axis=0, tiled=True)


def on_device(
    image_tiles,
    depth_kernel,
    norm_gain,
    weight_in,
    bias_in,
    weight_out,
    layer_scale,
    weight_proj,
    image_counts,
    destination,
    row_offset,
    connector,
    cotangent,
):
    at = ("co", "yh", "yl", "z", "x", BB)
    at = jnp.stack([lax.axis_index(axis) for axis in at]).astype(jnp.int32)
    sent = call(
        arrange_kernel,
        jax.ShapeDtypeStruct((512, 896), BF),
        [],
        [vmem()],
        4,
        2,
    )(cotangent)
    cot = exchange(sent.reshape(32, 16, 896), ENC).reshape(512, 896)
    image_tiles, sent, at = lax.optimization_barrier((image_tiles, sent, at))

    live = jnp.arange(32, dtype=jnp.int32) // 16 < image_counts[0]
    code = jnp.where(live, destination[0] * 2 + row_offset[0], -1).astype(BF)
    code = jnp.broadcast_to(jnp.repeat(code, 2)[:, None], (64, 128))
    pay, normt, xhat, rstd, slope, hsum, gsum, bsum, xp = forward(
        image_tiles,
        depth_kernel,
        norm_gain,
        weight_in,
        bias_in,
        weight_out,
        layer_scale,
        code,
    )
    pays = [pay] + [swap(pay, BB, 4, d) for d in (2, 1, 3)]
    wc = fold(lax.optimization_barrier((weight_proj, pay))[0], connector)
    grad_pre, part, give, *outer = connector_part(at, pays, cot, wc)

    near = swap(give, "co", 2, 1)
    far = swap((part[64:] + near[64:]).astype(BF), "yh", 2, 1)
    outer = turn(outer, "z")
    row_part, row_give = token_rows(grad_pre, connector)
    near, far, row_part, row_give = lax.optimization_barrier((near, far, row_part, row_give))
    row_near = swap(row_give, "co", 2, 1)
    row_tail = row_part[64:].astype(F32) + row_near[64:].astype(F32)
    row_far = swap(row_tail.astype(BF), "yh", 2, 1)
    keep, send, dpre, small_a = mlp_back(
        at, near, part, far, normt, slope, hsum, gsum, bsum, weight_out, layer_scale
    )
    send, dpre, *outer = lax.optimization_barrier((send, dpre, *outer))
    recv = swap(send, "co", 2, 1)
    outer = turn(outer_rows(at, outer), "x")
    small_b = front_back(dpre, weight_in, xhat, rstd, norm_gain, xp)
    small_b, row_far, outer = lax.optimization_barrier((small_b, row_far, outer))
    packed = pack(keep, recv, small_a, small_b)
    parts = exchange(packed, SAME_CORE)
    packed, outer = lax.optimization_barrier((packed, outer))

    proj = proj_rows(at, outer, connector)
    proj = [proj[7]] + [
        swap(proj[n], COLS, 8, (1 - n % 2) * 4 + (1 - (n % 4) // 2) * 2 + (1 - n // 4))
        for n in range(7)
    ]
    shards = settle(parts, proj)
    whole = exchange(shards, SAME_CORE)

    token_grads = row_part[:64].astype(F32) + row_near[:64].astype(F32) + row_far.astype(F32)
    token_grads = token_grads.astype(BF)
    whole, token_grads = lax.optimization_barrier((whole, token_grads))
    grad_in, grad_out, grad_proj, grad_kernel, grad_gain, grad_bias, grad_scale = place(
        at, whole, swap(whole, "co", 2, 1)
    )

    return (
        grad_kernel,
        grad_gain,
        grad_in,
        grad_bias,
        grad_out,
        grad_scale,
        grad_proj,
        token_grads,
    )


def solution(mesh):
    fine = Mesh(mesh.devices.reshape(2, 4, 4, 2, 2), ALL)
    in_specs = (
        P(ALL, None, None, None),
        P(),
        P(),
        P(),
        P(),
        P(),
        P(),
        P(),
        P(ALL),
        P(ALL, None),
        P(ALL, None),
        P(None, BB),
        P(ENC, BB),
    )
    out_specs = (P(), P(), P(), P(), P(), P(), P(), P(ALL, None))
    return jax.shard_map(
        on_device, mesh=fine, in_specs=in_specs, out_specs=out_specs, check_vma=False
    )
```

```python
import jax
import jax.numpy as jnp
import numpy as np
from jax import lax
from jax.experimental import pallas as pl
from jax.experimental.pallas import tpu as pltpu
from jax.sharding import Mesh, PartitionSpec as P

EPS = 1e-06
GELU_A = float(np.sqrt(2.0 / np.pi))
GELU_B = 0.044715
BF = jnp.bfloat16
F32 = jnp.float32
ALL = ("yl", "z", "x", "yh", "co")
ENC = ("yl", "z", "x")
BB = ("yh", "co")
SAME_CORE = ("yl", "z", "x", "yh")
COLS = ("yl", "yh", "co")
MIB = 1024 * 1024


def cost(us):
    return pl.CostEstimate(flops=int(us * 1.1e9) + 1, bytes_accessed=1, transcendentals=0)


def nn(a, b):
    return lax.dot_general(a, b, (((1,), (0,)), ((), ())), preferred_element_type=F32)


def nt(a, b):
    return lax.dot_general(a, b, (((1,), (1,)), ((), ())), preferred_element_type=F32)


def gelu_parts(u):
    u2 = u * u
    t = jnp.tanh(u * (GELU_A + (GELU_A * GELU_B) * u2))
    half = 0.5 * t + 0.5
    value = u * half
    slope = half + value * (1.0 - half) * (2.0 * GELU_A + (6.0 * GELU_A * GELU_B) * u2)
    return value, slope


def vmem():
    return pl.BlockSpec(memory_space=pltpu.VMEM)


def hbm():
    return pl.BlockSpec(memory_space=pltpu.HBM)


def smem():
    return pl.BlockSpec(memory_space=pltpu.SMEM)


def call(kernel, out_shape, scratch, in_specs, limit, us):
    multi = isinstance(out_shape, (list, tuple))
    return pl.pallas_call(
        kernel,
        out_shape=out_shape,
        in_specs=in_specs,
        out_specs=[vmem()] * len(out_shape) if multi else vmem(),
        scratch_shapes=scratch,
        compiler_params=pltpu.CompilerParams(vmem_limit_bytes=limit * MIB),
        cost_estimate=cost(us),
    )


def arrange_kernel(cot_ref, out_ref):
    r = lax.broadcasted_iota(jnp.int32, (512, 512), 0)
    s = lax.broadcasted_iota(jnp.int32, (512, 512), 1)
    want = ((r // 4) % 4) * 128 + (r // 16) * 4 + r % 4
    pick = jnp.where(s == want, 1.0, 0.0).astype(BF)
    out_ref[...] = nn(pick, cot_ref[...]).astype(BF)


def shifted(v):
    row = lax.broadcasted_iota(jnp.int32, (8, 128), 0)
    down = jnp.where(row == 0, 0.0, pltpu.roll(v, 1, 0))
    up = jnp.where(row == 7, 0.0, pltpu.roll(v, 7, 0))
    return down, v, up


def forward_kernel(
    x_hbm, k_ref, gain_ref, win_hbm, bias_ref, wout_hbm, scale_ref, code_ref,
    pay_ref, normt_ref, xhat_ref, rstd_ref, slope_ref, hsum_ref, gsum_ref, bsum_ref, xp_ref,
    xf_ref, xs_ref, kb_ref, conv_ref, norm_ref, hs_ref, x_ref, win_ref, wout_ref, sem,
):
    load_x = [pltpu.make_async_copy(x_hbm.at[t], x_ref.at[t], sem.at[t]) for t in range(2)]
    load_win = pltpu.make_async_copy(win_hbm, win_ref, sem.at[2])
    load_wout = pltpu.make_async_copy(wout_hbm, wout_ref, sem.at[3])
    for load in load_x + [load_win, load_wout]:
        load.start()
    for lt in range(3):
        lanes = slice(lt * 128, lt * 128 + 128)
        for a in range(7):
            kb_ref[lt, a] = k_ref[a, :, lanes]
    for t in range(2):
        load_x[t].wait()
        for lt in range(3):
            xf_ref[lt, t] = x_ref[t, :, :, lt * 128 : lt * 128 + 128].astype(F32)

    def split(n, carry):
        lt = n // 2
        t = n % 2
        for jj in range(4):
            plain = []
            for i in range(16):
                v = xf_ref[lt, t, i, pl.ds(jj, 8, stride=4), :]
                plain.append(v)
                for s, w in enumerate(shifted(v)):
                    xs_ref[s, lt, t, jj, i] = w
            xp_ref[lt, t, jj] = jnp.concatenate(plain, axis=0).astype(BF)
        return carry

    lax.fori_loop(0, 6, split, 0)

    def conv(n, carry):
        lt = n // 8
        t = (n // 4) % 2
        jj = n % 4
        acc = [None] * 16
        for b in range(7):
            q = jj + (b + 1)
            s = q // 4
            jin = q % 4
            w = [
                jnp.broadcast_to(kb_ref[lt, a, pl.ds(b, 1), :], (8, 128)) for a in range(7)
            ]
            for r in range(16):
                v = xs_ref[s, lt, t, jin, r]
                for a in range(7):
                    i = r - a + 3
                    if 0 <= i < 16:
                        term = v * w[a]
                        acc[i] = term if acc[i] is None else acc[i] + term
        for i in range(16):
            conv_ref[lt, t, i // 4, jj, i % 4] = acc[i]
        return carry

    lax.fori_loop(0, 24, conv, 0)

    def block(n, carry):
        t = n // 4
        q = n % 4
        rows = pl.ds(pl.multiple_of(n * 128, 128), 128)
        c = [conv_ref[lt, t, q].reshape(128, 128) for lt in range(3)]
        mean = jnp.sum(c[0] + c[1] + c[2], axis=1, keepdims=True) * (1.0 / 384.0)
        c = [v - mean for v in c]
        var = jnp.sum(c[0] * c[0] + c[1] * c[1] + c[2] * c[2], axis=1, keepdims=True) * (
            1.0 / 384.0
        )
        rstd = lax.rsqrt(var + EPS)
        rstd_ref[rows, :] = jnp.broadcast_to(rstd, (128, 128))
        for lt in range(3):
            lanes = slice(lt * 128, lt * 128 + 128)
            xhat = c[lt] * rstd
            xhat_ref[lt, rows, :] = xhat.astype(BF)
            normed = xhat * gain_ref[lanes].reshape(1, 128)
            norm_ref[n // 2, (n % 2) * 128 : (n % 2) * 128 + 128, lanes] = normed.astype(BF)
            normt_ref[n, lanes, :] = normed.T.astype(BF)
        return carry

    def widen(m, carry):
        for h in range(6):
            hid = slice(h * 256, h * 256 + 256)
            u = nn(norm_ref[m], win_ref[:, hid]) + bias_ref[hid].reshape(1, 256)
            value, slope = gelu_parts(u)
            toks = pl.ds(pl.multiple_of(m * 16, 8), 16)
            rows = pl.ds(pl.multiple_of(m * 256, 256), 256)
            hs_ref[toks, hid] = jnp.sum(value.reshape(2, 16, 8, 256), axis=1).reshape(16, 256)
            gsum_ref[toks, hid] = jnp.sum(slope.reshape(2, 16, 8, 256), axis=1).reshape(16, 256)
            slope_ref[rows, hid] = slope.astype(BF)
        return carry

    load_win.wait()
    for m in range(4):
        block(2 * m, 0)
        block(2 * m + 1, 0)
        widen(m, 0)
    load_wout.wait()

    hs = hs_ref[...]
    hi = hs.astype(BF)
    hsum_ref[...] = hi
    lo = (hs - hi.astype(F32)).astype(BF)
    bsum = nn(hi, wout_ref[...]) + nn(lo, wout_ref[...])
    bsum_ref[...] = bsum
    for lt in range(3):
        lanes = slice(lt * 128, lt * 128 + 128)
        for t in range(2):
            for q in range(4):
                total = xs_ref[1, lt, t, 0, 4 * q]
                for jj in range(4):
                    for im in range(4):
                        if jj + im > 0:
                            total = total + xs_ref[1, lt, t, jj, 4 * q + im]
                tok = slice(t * 32 + q * 8, t * 32 + q * 8 + 8)
                hs_ref[tok, lanes] = total
        pooled = hs_ref[:, lanes] + scale_ref[lanes].reshape(1, 128) * bsum[:, lanes]
        pay_ref[:, lanes] = (pooled * (1.0 / 16.0)).astype(BF)
    pay_ref[:, 384:512] = code_ref[...]


def forward(x, k, gain, win, bias, wout, scale, code):
    shape = jax.ShapeDtypeStruct
    return call(
        forward_kernel,
        [
            shape((64, 512), BF),
            shape((8, 384, 128), BF),
            shape((3, 1024, 128), BF),
            shape((1024, 128), F32),
            shape((1024, 1536), BF),
            shape((64, 1536), BF),
            shape((64, 1536), F32),
            shape((64, 384), F32),
            shape((3, 2, 4, 128, 128), BF),
        ],
        [
            pltpu.VMEM((3, 2, 16, 32, 128), F32),
            pltpu.VMEM((3, 3, 2, 4, 16, 8, 128), F32),
            pltpu.VMEM((3, 7, 7, 128), F32),
            pltpu.VMEM((3, 2, 4, 4, 4, 8, 128), F32),
            pltpu.VMEM((4, 256, 384), BF),
            pltpu.VMEM((64, 1536), F32),
            pltpu.VMEM((2, 16, 32, 384), BF),
            pltpu.VMEM((384, 1536), BF),
            pltpu.VMEM((1536, 384), BF),
            pltpu.SemaphoreType.DMA((4,)),
        ],
        [hbm(), vmem(), vmem(), hbm(), vmem(), hbm(), vmem(), vmem()],
        26,
        14,
    )(x, k, gain, win, bias, wout, scale, code)


def fold_kernel(proj_ref, conn_ref, out_ref):
    for at, size in ((0, 512), (512, 384)):
        out_ref[:, at : at + size] = nn(proj_ref[...], conn_ref[:, at : at + size]).astype(BF)


def fold(weight_proj, connector):
    return call(
        fold_kernel, jax.ShapeDtypeStruct((384, 896), BF), [], [vmem()] * 2, 16, 0
    )(weight_proj, connector)


def rows_kernel(gp_ref, conn_ref, keep_ref, send_ref):
    for n in range(8):
        cols = slice(n * 512, n * 512 + 512)
        out = nt(gp_ref[...], conn_ref[cols, :]).astype(BF)
        keep_ref[:, cols] = out[:128]
        send_ref[:, cols] = out[128:]


def token_rows(grad_pre, connector):
    shape = jax.ShapeDtypeStruct((128, 4096), BF)
    return call(rows_kernel, [shape, shape], [], [vmem()] * 2, 14, 0)(grad_pre, connector)


def outer_kernel(at_ref, r0_ref, r1_ref, r2_ref, r3_ref, o0_ref, o1_ref, o2_ref, o3_ref, sum_ref):
    total = r0_ref[...].astype(F32) + r1_ref[...].astype(F32)
    sum_ref[...] = total + r2_ref[...].astype(F32) + r3_ref[...].astype(F32)
    for d, o_ref in enumerate((o0_ref, o1_ref, o2_ref, o3_ref)):
        rows = pl.ds(pl.multiple_of(((at_ref[4] + d) & 3) * 24, 8), 24)
        o_ref[...] = sum_ref[rows, :].astype(BF)


def outer_rows(at, parts):
    return call(
        outer_kernel,
        [jax.ShapeDtypeStruct((24, 896), BF)] * 4,
        [pltpu.VMEM((96, 896), F32)],
        [smem()] + [vmem()] * 4,
        4,
        1,
    )(at, *parts)


def proj_kernel(at_ref, r0_ref, r1_ref, r2_ref, r3_ref, conn_ref, out_ref):
    total = r0_ref[...].astype(F32) + r1_ref[...].astype(F32)
    total = (total + r2_ref[...].astype(F32) + r3_ref[...].astype(F32)).astype(BF)
    for n in range(8):
        chunk = (
            (at_ref[0] ^ (1 - n // 4)) * 4
            + (at_ref[1] ^ (1 - (n % 4) // 2)) * 2
            + (at_ref[2] ^ (1 - n % 2))
        )
        rows = pl.ds(pl.multiple_of(chunk * 512, 512), 512)
        out_ref[n] = nt(total, conn_ref[rows, :]).astype(BF)


def proj_rows(at, parts, connector):
    return call(
        proj_kernel,
        jax.ShapeDtypeStruct((8, 24, 512), BF),
        [],
        [smem()] + [vmem()] * 5,
        14,
        0,
    )(at, *parts, connector)


def connector_kernel(
    at_ref, p0_ref, p1_ref, p2_ref, p3_ref, cot_ref, wc_ref,
    gp_ref, keep_ref, send_ref, s0_ref, s1_ref, s2_ref, s3_ref, pick_ref, pool_ref, poolt_ref,
):
    row = lax.broadcasted_iota(jnp.int32, (64, 128), 0)
    lane = lax.broadcasted_iota(jnp.int32, (64, 128), 1)
    for n, (d, p_ref) in enumerate(((0, p0_ref), (2, p1_ref), (1, p2_ref), (3, p3_ref))):
        tok = slice(n * 64, n * 64 + 64)
        pool_ref[tok, :] = p_ref[:, 0:384]
        code = p_ref[:, 384:512].astype(F32).astype(jnp.int32)
        src = at_ref[5] ^ d
        want = (code >> 1) * 16 + src * 4 + (code & 1) * 2 + (row & 1)
        want = jnp.where(code < 0, -1, want)
        for q in range(4):
            pick_ref[tok, q * 128 : q * 128 + 128] = jnp.where(
                lane + q * 128 == want, 1.0, 0.0
            ).astype(BF)
    for low, high in ((0, 256), (256, 512), (512, 768), (768, 896)):
        cols = slice(low, high)
        cot = nn(pick_ref[...], cot_ref[:, cols])
        pre = nn(pool_ref[...], wc_ref[:, cols])
        gp_ref[:, cols] = (cot * gelu_parts(pre)[1]).astype(BF)
    tok = nt(gp_ref[...], wc_ref[...])
    keep_ref[...] = tok[:128]
    send_ref[...] = tok[128:].astype(BF)
    poolt_ref[...] = pool_ref[...].astype(F32).T.astype(BF)
    for d, s_ref in enumerate((s0_ref, s1_ref, s2_ref, s3_ref)):
        rows = pl.ds(pl.multiple_of(((at_ref[3] + d) & 3) * 96, 96), 96)
        s_ref[...] = nn(poolt_ref[rows, :], gp_ref[...]).astype(BF)


def connector_part(at, pays, cot, wc):
    shape = jax.ShapeDtypeStruct
    return call(
        connector_kernel,
        [
            shape((256, 896), BF),
            shape((128, 384), F32),
            shape((128, 384), BF),
        ]
        + [shape((96, 896), BF)] * 4,
        [
            pltpu.VMEM((256, 512), BF),
            pltpu.VMEM((256, 384), BF),
            pltpu.VMEM((384, 256), BF),
        ],
        [smem()] + [vmem()] * 6,
        6,
        3,
    )(at, *pays, cot, wc)


def mlp_back_kernel(
    co_ref, near_ref, part_ref, far_ref, normt_ref, slope_ref, hsum_ref, gsum_ref, bsum_ref, wout_ref, scale_ref,
    keep_ref, send_ref, dpre_ref, small_ref, dh_ref,
):
    dtok = (part_ref[0:64, :] + near_ref[0:64, :].astype(F32) + far_ref[...].astype(F32)) * (1.0 / 16.0)
    small_ref[0:1, :] = jnp.sum(dtok * bsum_ref[...], axis=0, keepdims=True)
    dbr = (dtok * scale_ref[...].reshape(1, 384)).astype(BF)
    dh_ref[...] = nt(dbr, wout_ref[...])
    db = jnp.sum(dh_ref[...] * gsum_ref[...], axis=0, keepdims=True)
    for q in range(4):
        small_ref[1 + q : 2 + q, :] = db[:, q * 384 : q * 384 + 384]
    small_ref[5:8, :] = jnp.zeros((3, 384), F32)

    def block(n, carry):
        rows = pl.ds(pl.multiple_of(n * 128, 128), 128)
        toks = pl.ds(pl.multiple_of(n * 8, 8), 8)
        for h in range(4):
            hid = slice(h * 384, h * 384 + 384)
            g = slope_ref[rows, hid].astype(F32).reshape(16, 8, 384)
            d = g * dh_ref[toks, hid][None]
            dpre_ref[h, rows, :] = d.reshape(128, 384).astype(BF)
        return carry

    lax.fori_loop(0, 8, block, 0, unroll=8)
    hsum_t = hsum_ref[...].astype(F32).T.astype(BF)
    normt = jnp.concatenate([normt_ref[n] for n in range(8)], axis=1)
    mine = co_ref[0] == 0
    for h in range(2):
        def put(out_ref):
            for q in range(2):
                rows = slice(q * 384, q * 384 + 384)
                out_ref[rows, :] = nn(normt, dpre_ref[2 * h + q]).astype(out_ref.dtype)
            out_ref[768:1536, :] = nn(hsum_t[h * 768 : h * 768 + 768], dbr).astype(out_ref.dtype)

        here = mine if h == 0 else jnp.logical_not(mine)

        @pl.when(here)
        def _():
            put(keep_ref)

        @pl.when(jnp.logical_not(here))
        def _():
            put(send_ref)


def mlp_back(co, near, part, far, normt, slope, hsum, gsum, bsum, wout, scale):
    shape = jax.ShapeDtypeStruct
    return call(
        mlp_back_kernel,
        [
            shape((1536, 384), BF),
            shape((1536, 384), BF),
            shape((4, 1024, 384), BF),
            shape((8, 384), F32),
        ],
        [pltpu.VMEM((64, 1536), F32)],
        [smem()] + [vmem()] * 10,
        14,
        12,
    )(co, near, part, far, normt, slope, hsum, gsum, bsum, wout, scale)


def front_back_kernel(
    dpre_ref, win_ref, xhat_ref, rstd_ref, gain_ref, xp_ref, out_ref, dc_ref, dk_ref
):
    def block(n, carry):
        t = n // 4
        q = n % 4
        rows = pl.ds(pl.multiple_of(n * 128, 128), 128)
        dn = dns[n // 2][(n % 2) * 128 : (n % 2) * 128 + 128]
        rstd = rstd_ref[rows, :]
        dx = []
        xh = []
        gains = []
        for lt in range(3):
            lanes = slice(lt * 128, lt * 128 + 128)
            xhat = xhat_ref[lt, rows, :].astype(F32)
            part = dn[:, lanes]
            gains.append(jnp.sum((part * xhat).reshape(16, 8, 128), axis=0))
            dx.append(part * gain_ref[lanes].reshape(1, 128))
            xh.append(xhat)
        m1 = jnp.sum(dx[0] + dx[1] + dx[2], axis=1, keepdims=True) * (1.0 / 384.0)
        m2 = jnp.sum(dx[0] * xh[0] + dx[1] * xh[1] + dx[2] * xh[2], axis=1, keepdims=True) * (
            1.0 / 384.0
        )
        for lt in range(3):
            dc = rstd * (dx[lt] - m1 - xh[lt] * m2)
            for jj in range(4):
                for im in range(4):
                    at = (jj * 4 + im) * 8
                    for s, w in enumerate(shifted(dc[at : at + 8])):
                        dc_ref[s, lt, t, jj, q * 4 + im] = w
        return tuple(c + g for c, g in zip(carry, gains))

    zero = jnp.zeros((8, 128), F32)
    gains = (zero, zero, zero)
    dns = []
    for m in range(4):
        part = slice(m * 256, m * 256 + 256)
        dn = nt(dpre_ref[0, part, :], win_ref[:, 0:384])
        for h in range(1, 4):
            dn = dn + nt(dpre_ref[h, part, :], win_ref[:, h * 384 : h * 384 + 384])
        dns.append(dn)
        gains = block(2 * m, gains)
        gains = block(2 * m + 1, gains)
    for lt in range(3):
        lanes = slice(lt * 128, lt * 128 + 128)
        out_ref[49:50, lanes] = jnp.sum(gains[lt], axis=0, keepdims=True)

    dk_ref[...] = jnp.zeros_like(dk_ref)

    def conv(n, carry):
        lt = n // 8
        t = (n // 4) % 2
        jj = n % 4
        x = xp_ref[lt, t, jj].astype(F32)
        x = [x[i * 8 : i * 8 + 8] for i in range(16)]
        for b in range(7):
            q = jj + (7 - b)
            s = q // 4
            jin = q % 4
            acc = [None] * 7
            for i in range(16):
                v = dc_ref[s, lt, t, jin, i]
                for a in range(7):
                    r = i + a - 3
                    if 0 <= r < 16:
                        term = v * x[r]
                        acc[a] = term if acc[a] is None else acc[a] + term
            for a in range(7):
                dk_ref[lt, a * 7 + b] += acc[a]
        return carry

    lax.fori_loop(0, 24, conv, 0)
    for lt in range(3):
        lanes = slice(lt * 128, lt * 128 + 128)
        out_ref[0:49, lanes] = jnp.sum(dk_ref[lt], axis=1)
    out_ref[50:56, :] = jnp.zeros((6, 384), F32)


def front_back(dpre, win, xhat, rstd, gain, xp):
    return call(
        front_back_kernel,
        jax.ShapeDtypeStruct((56, 384), F32),
        [pltpu.VMEM((3, 3, 2, 4, 16, 8, 128), F32), pltpu.VMEM((3, 49, 8, 128), F32)],
        [vmem()] * 6,
        15,
        2,
    )(dpre, win, xhat, rstd, gain, xp)


def three(v):
    return [v[:, q * 128 : q * 128 + 128] for q in range(3)]


def two_parts(v):
    high = v.astype(BF).astype(F32)
    return three(high) + three(v - high)


def pack_kernel(keep_ref, recv_ref, a_ref, b_ref, out_ref):
    pad = jnp.zeros((2, 128), F32)

    def one(n, small):
        rows = slice(n * 24, n * 24 + 24)
        pair = keep_ref[rows, :].astype(F32) + recv_ref[rows, :].astype(F32)
        out_ref[n] = jnp.concatenate(three(pair) + two_parts(small) + [pad], axis=0).astype(BF)

    for n in range(64):
        one(n, a_ref[n : n + 1, :] if n < 8 else b_ref[n - 8 : n - 7, :])


def pack(keep, recv, small_a, small_b):
    return call(
        pack_kernel, jax.ShapeDtypeStruct((64, 80, 128), BF), [], [vmem()] * 4, 6, 2
    )(keep, recv, small_a, small_b)


def settle_kernel(parts_ref, *refs):
    proj_refs, out_ref = refs[:8], refs[8]
    total = parts_ref[0].astype(F32)
    for n in range(1, 64):
        total = total + parts_ref[n].astype(F32)
    total = total * (1.0 / 128.0)
    small = total[72:75] + total[75:78]
    high = small.astype(BF).astype(F32)
    proj = proj_refs[0][...].astype(F32)
    for ref in proj_refs[1:]:
        proj = proj + ref[...].astype(F32)
    proj = proj * (1.0 / 128.0)
    shard = jnp.concatenate(
        [total[:72], high, small - high, total[78:80]]
        + [proj[:, q * 128 : q * 128 + 128] for q in range(4)],
        axis=0,
    ).astype(BF)
    for n in range(64):
        out_ref[n] = shard


def settle(parts, proj):
    return call(
        settle_kernel, jax.ShapeDtypeStruct((64, 176, 128), BF), [], [vmem()] * 9, 6, 2
    )(parts, *proj)


def place_half(src_ref, half, refs, outs, sem):
    in_ref, out_ref, proj_ref = refs

    def pair(low, high, at):
        return jnp.concatenate(
            [
                src_ref[low, at : at + 24, :].astype(F32),
                src_ref[high, at : at + 24, :].astype(F32),
            ],
            axis=0,
        ).astype(BF)

    wide = pl.ds(pl.multiple_of(half * 768, 128), 768)
    tall = pl.ds(pl.multiple_of(half * 768, 128), 768)
    cols = pl.ds(pl.multiple_of(half * 2048, 128), 2048)
    copies = [
        pltpu.make_async_copy(in_ref, outs[0].at[:, wide], sem.at[0]),
        pltpu.make_async_copy(out_ref, outs[1].at[tall, :], sem.at[1]),
        pltpu.make_async_copy(proj_ref, outs[2].at[:, cols], sem.at[2]),
    ]
    for yl in range(2):
        for yh in range(2):
            for p in range(4):
                col = (yh * 2 + yl) * 512 + p * 128
                for m in range(8):
                    n = yl * 32 + 4 * m + yh
                    proj_ref[m * 48 : m * 48 + 48, col : col + 128] = pair(n, n + 2, 80 + p * 24)
    copies[2].start()
    for p in range(3):
        for m in range(16):
            out_ref[m * 48 : m * 48 + 48, p * 128 : p * 128 + 128] = pair(
                32 + 2 * m, 33 + 2 * m, p * 24
            )
    copies[1].start()
    for p in range(3):
        for m in range(8):
            for q in range(2):
                n = q * 16 + 2 * m
                col = q * 384 + p * 128
                in_ref[m * 48 : m * 48 + 48, col : col + 128] = pair(n, n + 1, p * 24)
    copies[0].start()
    return copies


def small_rows(src_ref, n):
    rows = src_ref[n, 64:80, :].astype(F32)
    return rows[8:11] + rows[11:14]


def place_own_kernel(
    co_ref, mine_ref, in_hbm, out_hbm, proj_hbm, small_ref, in_ref, out_ref, proj_ref, sem
):
    copies = place_half(
        mine_ref, co_ref[0], (in_ref, out_ref, proj_ref), (in_hbm, out_hbm, proj_hbm), sem
    )
    for n in range(64):
        small = small_rows(mine_ref, n)
        for p in range(3):
            small_ref[n : n + 1, p * 128 : p * 128 + 128] = small[p : p + 1]
    for copy in copies:
        copy.wait()


def place_other_kernel(
    co_ref, other_ref, small_ref, in_from, out_from, proj_from,
    in_hbm, out_hbm, proj_hbm, kernel_ref, gain_ref, bias_ref, scale_ref,
    in_ref, out_ref, proj_ref, sem,
):
    copies = place_half(
        other_ref, 1 - co_ref[0], (in_ref, out_ref, proj_ref), (in_hbm, out_hbm, proj_hbm), sem
    )
    for n in range(58):
        small = small_rows(other_ref, n)
        for p in range(3):
            lanes = slice(p * 128, p * 128 + 128)
            row = small[p : p + 1] + small_ref[n : n + 1, lanes]
            if n == 0:
                scale_ref[lanes] = row.reshape(128)
            elif n < 5:
                bias_ref[(n - 1) * 384 + p * 128 : (n - 1) * 384 + p * 128 + 128] = row.reshape(128)
            elif n == 57:
                gain_ref[lanes] = row.reshape(128)
            elif n >= 8:
                a, b = (n - 8) // 7, (n - 8) % 7
                kernel_ref[a, b : b + 1, lanes] = row
    for copy in copies:
        copy.wait()


def place(co, mine, other):
    shape = jax.ShapeDtypeStruct
    large = [shape((384, 1536), BF), shape((1536, 384), BF), shape((384, 4096), BF)]
    scratch = [
        pltpu.VMEM((384, 768), BF),
        pltpu.VMEM((768, 384), BF),
        pltpu.VMEM((384, 2048), BF),
        pltpu.SemaphoreType.DMA((3,)),
    ]
    params = pltpu.CompilerParams(vmem_limit_bytes=10 * MIB)
    *held, small = pl.pallas_call(
        place_own_kernel,
        out_shape=large + [shape((64, 384), F32)],
        in_specs=[smem(), vmem()],
        out_specs=[hbm()] * 3 + [vmem()],
        scratch_shapes=scratch,
        compiler_params=params,
        cost_estimate=cost(3),
    )(co, mine)
    return pl.pallas_call(
        place_other_kernel,
        out_shape=large
        + [shape((7, 7, 384), F32), shape((384,), F32), shape((1536,), F32), shape((384,), F32)],
        in_specs=[smem(), vmem(), vmem()] + [hbm()] * 3,
        out_specs=[hbm()] * 3 + [vmem()] * 4,
        scratch_shapes=scratch,
        input_output_aliases={3: 0, 4: 1, 5: 2},
        compiler_params=params,
        cost_estimate=cost(3),
    )(co, other, small, *held)


def swap(v, axes, size, d):
    return lax.ppermute(v, axes, [(i, i ^ d) for i in range(size)])


def turn(parts, axis):
    return [parts[0]] + [
        lax.ppermute(parts[d], axis, [(i, (i + d) % 4) for i in range(4)]) for d in (1, 2, 3)
    ]


def exchange(v, axes):
    return lax.all_to_all(v, axes, split_axis=0, concat_axis=0, tiled=True)


def on_device(
    image_tiles,
    depth_kernel,
    norm_gain,
    weight_in,
    bias_in,
    weight_out,
    layer_scale,
    weight_proj,
    image_counts,
    destination,
    row_offset,
    connector,
    cotangent,
):
    at = ("co", "yh", "yl", "z", "x", BB)
    at = jnp.stack([lax.axis_index(axis) for axis in at]).astype(jnp.int32)
    sent = call(
        arrange_kernel,
        jax.ShapeDtypeStruct((512, 896), BF),
        [],
        [vmem()],
        4,
        2,
    )(cotangent)
    cot = exchange(sent.reshape(32, 16, 896), ENC).reshape(512, 896)
    image_tiles, sent, at = lax.optimization_barrier((image_tiles, sent, at))

    live = jnp.arange(32, dtype=jnp.int32) // 16 < image_counts[0]
    code = jnp.where(live, destination[0] * 2 + row_offset[0], -1).astype(BF)
    code = jnp.broadcast_to(jnp.repeat(code, 2)[:, None], (64, 128))
    pay, normt, xhat, rstd, slope, hsum, gsum, bsum, xp = forward(
        image_tiles,
        depth_kernel,
        norm_gain,
        weight_in,
        bias_in,
        weight_out,
        layer_scale,
        code,
    )
    pays = [pay] + [swap(pay, BB, 4, d) for d in (2, 1, 3)]
    wc = fold(lax.optimization_barrier((weight_proj, pay))[0], connector)
    grad_pre, part, give, *outer = connector_part(at, pays, cot, wc)

    near = swap(give, "co", 2, 1)
    far = swap((part[64:] + near[64:].astype(F32)).astype(BF), "yh", 2, 1)
    outer = turn(outer, "z")
    row_part, row_give = token_rows(grad_pre, connector)
    near, far, row_part, row_give = lax.optimization_barrier((near, far, row_part, row_give))
    row_near = swap(row_give, "co", 2, 1)
    row_tail = row_part[64:].astype(F32) + row_near[64:].astype(F32)
    row_far = swap(row_tail.astype(BF), "yh", 2, 1)
    keep, send, dpre, small_a = mlp_back(
        at, near, part, far, normt, slope, hsum, gsum, bsum, weight_out, layer_scale
    )
    send, dpre, *outer = lax.optimization_barrier((send, dpre, *outer))
    recv = swap(send, "co", 2, 1)
    outer = turn(outer_rows(at, outer), "x")
    small_b = front_back(dpre, weight_in, xhat, rstd, norm_gain, xp)
    small_b, row_far, outer = lax.optimization_barrier((small_b, row_far, outer))
    packed = pack(keep, recv, small_a, small_b)
    parts = exchange(packed, SAME_CORE)
    packed, outer = lax.optimization_barrier((packed, outer))

    proj = proj_rows(at, outer, connector)
    proj = [proj[7]] + [
        swap(proj[n], COLS, 8, (1 - n % 2) * 4 + (1 - (n % 4) // 2) * 2 + (1 - n // 4))
        for n in range(7)
    ]
    shards = settle(parts, proj)
    whole = exchange(shards, SAME_CORE)

    token_grads = row_part[:64].astype(F32) + row_near[:64].astype(F32) + row_far.astype(F32)
    token_grads = token_grads.astype(BF)
    whole, token_grads = lax.optimization_barrier((whole, token_grads))
    grad_in, grad_out, grad_proj, grad_kernel, grad_gain, grad_bias, grad_scale = place(
        at, whole, swap(whole, "co", 2, 1)
    )

    return (
        grad_kernel,
        grad_gain,
        grad_in,
        grad_bias,
        grad_out,
        grad_scale,
        grad_proj,
        token_grads,
    )


def solution(mesh):
    fine = Mesh(mesh.devices.reshape(2, 4, 4, 2, 2), ALL)
    in_specs = (
        P(ALL, None, None, None),
        P(),
        P(),
        P(),
        P(),
        P(),
        P(),
        P(),
        P(ALL),
        P(ALL, None),
        P(ALL, None),
        P(None, BB),
        P(ENC, BB),
    )
    out_specs = (P(), P(), P(), P(), P(), P(), P(), P(ALL, None))
    return jax.shard_map(
        on_device, mesh=fine, in_specs=in_specs, out_specs=out_specs, check_vma=False
    )
```
